32 devices in a mesh: fsdp: 2 (over x), blk: 4 (over y, core), uly: 4 (over z).
Axes of the slice: x: 2, y: 2, z: 4, core: 2. Of those that a mesh axis runs over, the one named last changes fastest.
Arguments:
- tokens: bfloat16 [4096, 768], P(('fsdp', 'blk', 'uly')), may hold values from -6 to 6
- query_weight: bfloat16 [768, 768], P(('fsdp', 'blk'), 'uly'), may hold values from -0.4375 to 0.4375
- key_weight: bfloat16 [768, 768], P(('fsdp', 'blk'), 'uly'), may hold values from -0.21875 to 0.21875
- value_weight: bfloat16 [768, 768], P(('fsdp', 'blk'), 'uly'), may hold values from -0.21875 to 0.21875
- output_weight: bfloat16 [768, 768], P('uly', ('fsdp', 'blk')), may hold values from -0.875 to 0.875
- up_weight: bfloat16 [768, 3072], P(('fsdp', 'blk'), 'uly'), may hold values from -0.21875 to 0.21875
- down_weight: bfloat16 [3072, 768], P('uly', ('fsdp', 'blk')), may hold values from -0.15625 to 0.15625
- query_bias: bfloat16 [768], P(('fsdp', 'blk')), may hold values from -3 to 3
- value_bias: bfloat16 [768], P(('fsdp', 'blk')), may hold values from -3 to 3
- output_bias: bfloat16 [768], P(('fsdp', 'blk')), may hold values from -3 to 3
- up_bias: bfloat16 [3072], P(('fsdp', 'blk')), may hold values from -3 to 3
- down_bias: bfloat16 [768], P(('fsdp', 'blk')), may hold values from -3 to 3
- first_gain: bfloat16 [768], P(('fsdp', 'blk')), may hold values from 0.25 to 1.75
- first_shift: bfloat16 [768], P(('fsdp', 'blk')), may hold values from -3 to 3
- second_gain: bfloat16 [768], P(('fsdp', 'blk')), may hold values from 0.25 to 1.75
- second_shift: bfloat16 [768], P(('fsdp', 'blk')), may hold values from -3 to 3
- cotangent: bfloat16 [4096, 768], P(('fsdp', 'blk', 'uly')), may hold values from -6 to 6
Outputs:
- result: bfloat16 [4096, 768], P(('fsdp', 'blk', 'uly'))
- input_grad: bfloat16 [4096, 768], P(('fsdp', 'blk', 'uly'))
- query_weight_grad: float32 [768, 768], P(('fsdp', 'blk'), 'uly')
- key_weight_grad: float32 [768, 768], P(('fsdp', 'blk'), 'uly')
- value_weight_grad: float32 [768, 768], P(('fsdp', 'blk'), 'uly')
- output_weight_grad: float32 [768, 768], P('uly', ('fsdp', 'blk'))
- up_weight_grad: float32 [768, 3072], P(('fsdp', 'blk'), 'uly')
- down_weight_grad: float32 [3072, 768], P('uly', ('fsdp', 'blk'))
- query_bias_grad: float32 [768], P(('fsdp', 'blk', 'uly'))
- value_bias_grad: float32 [768], P(('fsdp', 'blk', 'uly'))
- output_bias_grad: float32 [768], P(('fsdp', 'blk', 'uly'))
- up_bias_grad: float32 [3072], P(('fsdp', 'blk', 'uly'))
- down_bias_grad: float32 [768], P(('fsdp', 'blk', 'uly'))
- first_gain_grad: float32 [768], P(('fsdp', 'blk', 'uly'))
- first_shift_grad: float32 [768], P(('fsdp', 'blk', 'uly'))
- second_gain_grad: float32 [768], P(('fsdp', 'blk', 'uly'))
- second_shift_grad: float32 [768], P(('fsdp', 'blk', 'uly'))
The draws below stay inside these ranges and needn't reach their ends.
All inputs are finite; a program needn't handle non-finite values.
Results may differ from the reference program's by a relative error of at most 0.023.
Values may be sent and summed in bfloat16 or wider, within the bound.
No kernel may reach another device: no remote copies, remote signals or barrier semaphores. Data moves between devices by JAX's collectives and lax.ppermute only.
A program may use at most 128 MiB of HBM per device.

```python
import jax
import jax.numpy as jnp
from jax import lax

D = 768
HEADS = 12
HEAD_DIM = 64
FF = 3072
LENGTH = 2048
SEQS = 2
TOKENS = 4096


def level_of(stream_key, shape, cuts, smallest, high):
    def one(dim, shards_of):
        heights = jax.random.uniform(jax.random.fold_in(jax.random.fold_in(stream_key, 6), dim), (shards_of,), jnp.float32, smallest / len(cuts), high / len(cuts))
        return jnp.repeat(jnp.exp(heights), shape[dim] // shards_of).reshape((-1,) + (1,) * (len(shape) - dim - 1))

    level = one(*cuts[0])
    for cut in cuts[1:]:
        level = level * one(*cut)
    return level


def gaussian(key, extent, width, bound, shards=(), kind=jnp.bfloat16):
    array = jax.random.normal(key, extent, jnp.float32) * width
    if len(shards) > 0:
        array = level_of(key, extent, shards, -0.22, 0.18) * array
    return jnp.clip(array, min=-bound, max=bound).astype(kind)


def setup_inputs(seed: int = 0) -> dict:
    arg_keys = jax.random.split(jax.random.key(seed), 18)
    return {
        "tokens": gaussian(arg_keys[0], (TOKENS, D), 1.0, 6.0, ((0, 32),)),
        "query_weight": gaussian(arg_keys[1], (D, D), (D // 4) ** -0.5, 0.4375, ((0, 8), (1, 4))),
        "key_weight": gaussian(arg_keys[2], (D, D), D ** -0.5, 0.21875, ((0, 8), (1, 4))),
        "value_weight": gaussian(arg_keys[3], (D, D), D ** -0.5, 0.21875, ((0, 8), (1, 4))),
        "output_weight": gaussian(arg_keys[4], (D, D), (D // 16) ** -0.5, 0.875, ((0, 4), (1, 8))),
        "up_weight": gaussian(arg_keys[5], (D, FF), D ** -0.5, 0.21875, ((0, 8), (1, 4))),
        "down_weight": gaussian(arg_keys[6], (FF, D), (FF // 2) ** -0.5, 0.15625, ((0, 4), (1, 8))),
        "query_bias": gaussian(arg_keys[7], (D,), 0.5, 3.0, ((0, 8),)),
        "value_bias": gaussian(arg_keys[8], (D,), 0.5, 3.0, ((0, 8),)),
        "output_bias": gaussian(arg_keys[9], (D,), 0.5, 3.0, ((0, 8),)),
        "up_bias": gaussian(arg_keys[10], (FF,), 0.5, 3.0, ((0, 8),)),
        "down_bias": gaussian(arg_keys[11], (D,), 0.5, 3.0, ((0, 8),)),
        "first_gain": jnp.clip(1.0 + 0.15 * jax.random.normal(arg_keys[12], (D,), jnp.float32), 0.25, 1.75).astype(jnp.bfloat16),
        "first_shift": gaussian(arg_keys[13], (D,), 0.4, 3.0, ((0, 8),)),
        "second_gain": jnp.clip(1.0 + 0.15 * jax.random.normal(arg_keys[14], (D,), jnp.float32), 0.25, 1.75).astype(jnp.bfloat16),
        "second_shift": gaussian(arg_keys[15], (D,), 0.4, 3.0, ((0, 8),)),
        "cotangent": gaussian(arg_keys[16], (TOKENS, D), 1.0, 6.0, ((0, 32),)),
    }


@jax.custom_vjp
def low(v):
    return lax.optimization_barrier(v.astype(jnp.bfloat16)).astype(jnp.float32)

@jax.custom_vjp
def low_back(v):
    return v

def low_keep(v):
    return (low(v), None)

def low_pass(kept, grad):
    return (grad,)

def back_keep(v):
    return (v, None)

def back_low(kept, grad):
    return (low(grad),)
low.defvjp(low_keep, low_pass)
low_back.defvjp(back_keep, back_low)

def matmul_plain(left_side, right_side):
    return jnp.dot(left_side, right_side, precision=lax.Precision.HIGHEST)

def layer_norm(inputs, gain_vec, shift_vec):
    centre = inputs - lax.optimization_barrier(jnp.mean(inputs, axis=-1, keepdims=True))
    spread = lax.optimization_barrier(jnp.mean(centre * centre, axis=-1, keepdims=True))
    return centre * lax.rsqrt(spread + 1e-05) * gain_vec + shift_vec

def attend(query_all, key_all, value_all):
    length = query_all.shape[0]
    block_rows = min(512, length)
    block_count = length // block_rows
    positions = jnp.arange(length, dtype=jnp.int32)

    def one_block(block_start):
        query_block = lax.dynamic_slice_in_dim(query_all, block_start, block_rows, 0)
        scores = jnp.einsum('qhd,khd->hqk', query_block, key_all, precision=lax.Precision.HIGHEST) * HEAD_DIM ** (-0.5)
        scores = low_back(scores)
        row_index = block_start + jnp.arange(block_rows, dtype=jnp.int32)
        allowed = positions[None, :] <= row_index[:, None]
        scores = jnp.where(allowed[None], scores, -1000000000.0)
        row_max = lax.optimization_barrier(jnp.max(scores, axis=-1, keepdims=True))
        weights_exp = jnp.exp(scores - row_max)
        probabilities = low(weights_exp / lax.optimization_barrier(jnp.sum(weights_exp, axis=-1, keepdims=True)))
        return jnp.einsum('hqk,khd->qhd', probabilities, value_all, precision=lax.Precision.HIGHEST)
    starts = jnp.arange(block_count, dtype=jnp.int32) * block_rows
    outputs = lax.map(jax.checkpoint(one_block), starts)
    return outputs.reshape(length, HEADS * HEAD_DIM)

def block_forward(params, inputs):
    query_weight, key_weight, value_weight, output_weight, up_weight, down_weight, query_bias, value_bias, output_bias, up_bias, down_bias, first_gain, first_shift, second_gain, second_shift = params
    length = inputs.shape[0]
    normed = low(layer_norm(inputs, first_gain, first_shift))
    queries = low_back(low(matmul_plain(normed, query_weight) + query_bias))
    keys_all = low_back(low(matmul_plain(normed, key_weight)))
    values = low_back(low(matmul_plain(normed, value_weight) + value_bias))
    mixed_heads = attend(queries.reshape(length, HEADS, HEAD_DIM), keys_all.reshape(length, HEADS, HEAD_DIM), values.reshape(length, HEADS, HEAD_DIM))
    mixed_heads = low_back(low(mixed_heads))
    branch = low_back(matmul_plain(mixed_heads, output_weight) + output_bias)
    middle = inputs + branch
    second = low(layer_norm(middle, second_gain, second_shift))
    hidden = low_back(matmul_plain(second, up_weight) + up_bias)
    active = low(jax.nn.gelu(hidden, approximate=True))
    outside = low_back(matmul_plain(active, down_weight) + down_bias)
    return middle + outside

def reference(tokens, query_weight, key_weight, value_weight, output_weight, up_weight, down_weight, query_bias, value_bias, output_bias, up_bias, down_bias, first_gain, first_shift, second_gain, second_shift, cotangent):
    params = tuple((item.astype(jnp.float32) for item in (query_weight, key_weight, value_weight, output_weight, up_weight, down_weight, query_bias, value_bias, output_bias, up_bias, down_bias, first_gain, first_shift, second_gain, second_shift)))
    inputs = tokens.astype(jnp.float32).reshape(SEQS, LENGTH, D)
    seeds = cotangent.astype(jnp.float32).reshape(SEQS, LENGTH, D)
    zero_grads = jax.tree.map(jnp.zeros_like, params)

    def per_sequence(totals, seq_pair):
        outputs, pullback = jax.vjp(block_forward, params, seq_pair[0])
        param_grads, input_grads = pullback(seq_pair[1])
        totals = jax.tree.map(lambda total, extra: total + extra, totals, param_grads)
        return (totals, (outputs, input_grads))
    totals, (outputs, input_grads) = lax.scan(per_sequence, zero_grads, (inputs, seeds))
    return (outputs.reshape(TOKENS, D).astype(jnp.bfloat16), input_grads.reshape(TOKENS, D).astype(jnp.bfloat16), totals[0], totals[1], totals[2], totals[3], totals[4], totals[5], totals[6], totals[7], totals[8], totals[9], totals[10], totals[11], totals[12], totals[13], totals[14])
```

```python
import jax
import jax.numpy as jnp
from jax import lax
from jax.experimental import pallas as pl
from jax.experimental.pallas import tpu as pltpu
from jax.sharding import PartitionSpec as P

HEAD_DIM = 64
CUBE = ("fsdp", "blk")
VEC_ROWS = 16
VMEM_LIMIT = 56 * 1024 * 1024

KEY_GROUP, KEY_HALF = (0, 0, 1), (0, 1, 0)
VALUE_GROUP, VALUE_HALF = (2, 2, 1), (0, 1, 1)


def dot_plain(left, right):
    return jnp.dot(left, right, preferred_element_type=jnp.float32)


def dot_rows(left, right):
    return lax.dot_general(
        left, right, (((0,), (0,)), ((), ())), preferred_element_type=jnp.float32
    )


def dot_cols(left, right):
    return lax.dot_general(
        left, right, (((1,), (1,)), ((), ())), preferred_element_type=jnp.float32
    )


def passed_along(array, by):
    peers = lax.axis_size("uly")
    return lax.ppermute(array, "uly", [(i, (i + by) % peers) for i in range(peers)])


def slots_of(array):
    return [array] + [passed_along(array, by) for by in range(1, lax.axis_size("uly"))]


def slots_summed(parts):
    total = parts[0]
    for by in range(1, len(parts)):
        total = total + passed_along(parts[by].astype(jnp.bfloat16), -by).astype(jnp.float32)
    return total


def blk_swapped(array, flip):
    peers = lax.axis_size("blk")
    return lax.ppermute(array, "blk", [(i, i ^ flip) for i in range(peers)])


def cube_swapped(array, even, odd):
    peers = lax.axis_size(CUBE)
    pairs = [(i, i ^ (odd if i & 1 else even)) for i in range(peers)]
    return lax.ppermute(array, CUBE, pairs)


def cube_index():
    return lax.axis_index("fsdp") * lax.axis_size("blk") + lax.axis_index("blk")


def place_kernel(cuts, index_ref, own, first, second, other, *outs):
    me = index_ref[0]
    odd = me & 1
    near, far = jnp.where(odd == 1, 2, 4), jnp.where(odd == 1, 4, 2)
    pieces = [
        (own, 0),
        (first, near),
        (second.at[0], far),
        (second.at[1], 6),
        (other.at[0], 1),
        (other.at[1], far ^ 1),
        (other.at[2], near ^ 1),
        (other.at[3], 7),
    ]
    for piece, flip in pieces:
        for out, (row, rows, column, columns) in zip(outs, cuts):
            out[me ^ flip] = piece[row : row + rows, column : column + columns]


def cube_gathered(array, cuts):
    if lax.axis_size("fsdp") != 2 or lax.axis_size("blk") != 4:
        whole = lax.all_gather(array, CUBE, axis=0, tiled=False)
        return [whole[:, r : r + rows, c : c + cols] for r, rows, c, cols in cuts]
    first = cube_swapped(array, 4, 2)
    second = cube_swapped(jnp.stack([array, first]), 2, 4)
    other = cube_swapped(jnp.concatenate([array[None], first[None], second]), 1, 1)
    index = cube_index().astype(jnp.int32).reshape(1)
    outs = [((8, rows, columns), array.dtype) for _, rows, _, columns in cuts]
    return on_core(
        lambda *refs: place_kernel(cuts, *refs), index, (array, first, second, other), outs
    )


def cube_summed(blocks):
    if lax.axis_size("fsdp") != 2 or lax.axis_size("blk") != 4:
        return lax.psum_scatter(blocks, CUBE, scatter_dimension=0, tiled=False)
    me = cube_index()
    odd = me & 1
    near, far = jnp.where(odd == 1, 2, 4), jnp.where(odd == 1, 4, 2)

    def block(flip):
        return lax.dynamic_index_in_dim(blocks, me ^ flip, 0, False)

    order = (0, far, near, 6)
    sent = jnp.stack([block(flip ^ 1) for flip in (0, near, far, 6)]).astype(jnp.bfloat16)
    got = cube_swapped(sent, 1, 1).astype(jnp.float32)
    held = [block(flip) + got[at] for at, flip in enumerate(order)]
    sent = jnp.stack(held[2:]).astype(jnp.bfloat16)
    got = cube_swapped(sent, 4, 2).astype(jnp.float32)
    held = [held[0] + got[0], held[1] + got[1]]
    got = cube_swapped(held[1].astype(jnp.bfloat16), 2, 4).astype(jnp.float32)
    return held[0] + got


def half_padded(part, half):
    zero = jnp.zeros_like(part)
    return jnp.concatenate([part, zero] if half == 0 else [zero, part], axis=0)


def heads_across(array, halves):
    turned = array.T
    return [
        half_padded(turned[h * HEAD_DIM : (h + 1) * HEAD_DIM], halves[h])
        for h in range(len(halves))
    ]


def group_of(ref, group):
    return ref[:, group * 128 : (group + 1) * 128]


def slot_places(index, uly, slot_rows):
    return ((uly - index // slot_rows) & 3) * slot_rows + index % slot_rows


def causal(rows, uly):
    keys = lax.broadcasted_iota(jnp.int32, (rows, rows), 0)
    queries = lax.broadcasted_iota(jnp.int32, (rows, rows), 1)
    slot_rows = rows // 4
    return slot_places(keys, uly, slot_rows) <= slot_places(queries, uly, slot_rows)


def forward_block(query_t, kv_ref, top, total, mixed, allowed):
    turned = kv_ref[...].T
    for h in range(3):
        scores = dot_plain(group_of(kv_ref, KEY_GROUP[h]), query_t[h])
        if allowed is not None:
            scores = jnp.where(allowed, scores, -1e30)
        block_top = jnp.max(scores, axis=0, keepdims=True)
        low = VALUE_GROUP[h] * 128 + VALUE_HALF[h] * HEAD_DIM
        value_t = turned[low : low + HEAD_DIM]
        own = pl.ds(h * HEAD_DIM, HEAD_DIM)
        if allowed is not None:
            weights = jnp.exp(scores - block_top)
            top[h : h + 1] = block_top
            total[h : h + 1] = jnp.sum(weights, axis=0, keepdims=True)
            mixed[own] = dot_plain(value_t, weights.astype(jnp.bfloat16))
        else:
            old_top = top[h : h + 1]
            new_top = jnp.maximum(old_top, block_top)
            fade = jnp.exp(old_top - new_top)
            weights = jnp.exp(scores - new_top)
            top[h : h + 1] = new_top
            total[h : h + 1] = total[h : h + 1] * fade + jnp.sum(weights, axis=0, keepdims=True)
            mixed[own] = mixed[own] * fade + dot_plain(value_t, weights.astype(jnp.bfloat16))


def forward_near_kernel(place, query, kv_own, kv_core, top, total, mixed):
    blk, uly = place[0], place[1]
    query_t = heads_across(query[...], KEY_HALF)
    top[...] = jnp.zeros_like(top)
    total[...] = jnp.ones_like(total)
    forward_block(query_t, kv_own, top, total, mixed, causal(query.shape[0], uly))

    @pl.when((blk & 1) == 1)
    def _():
        forward_block(query_t, kv_core, top, total, mixed, None)


def forward_far_kernel(
    place, query, kv_y, kv_both, top_in, total_in, mixed_in, out, mixed, lse, top, total
):
    blk = place[0]
    top[...] = top_in[...]
    total[...] = total_in[...]
    mixed[...] = mixed_in[...]

    @pl.when((blk & 2) == 2)
    def _():
        query_t = heads_across(query[...], KEY_HALF)
        forward_block(query_t, kv_y, top, total, mixed, None)
        forward_block(query_t, kv_both, top, total, mixed, None)

    for h in range(3):
        own = pl.ds(h * HEAD_DIM, HEAD_DIM)
        mixed[own] = mixed[own] / total[h : h + 1]
    lse[...] = top[...] + jnp.log(total[...])
    out[...] = mixed[...].T.astype(jnp.bfloat16)


def backward_block(sides, kv_ref, dkv_ref, query_grad_t, allowed):
    query_t, grad_t, query_m, grad_m, delta, lse = sides
    turned = kv_ref[...].T
    columns = [None, None, None]

    def add(group, term):
        columns[group] = term if columns[group] is None else columns[group] + term

    for h in range(3):
        scores = dot_plain(group_of(kv_ref, KEY_GROUP[h]), query_t[h])
        probs = jnp.exp(scores - lse[h : h + 1])
        if allowed is not None:
            probs = jnp.where(allowed, probs, 0.0)
        prob_grad = dot_plain(group_of(kv_ref, VALUE_GROUP[h]), grad_t[h])
        score_grad = (probs * (prob_grad - delta[h])).astype(jnp.bfloat16)
        add(VALUE_GROUP[h], dot_plain(probs.astype(jnp.bfloat16), grad_m[h]))
        add(KEY_GROUP[h], dot_plain(score_grad, query_m[h]))
        low = KEY_GROUP[h] * 128 + KEY_HALF[h] * HEAD_DIM
        own = pl.ds(h * HEAD_DIM, HEAD_DIM)
        query_grad_t[own] += dot_plain(turned[low : low + HEAD_DIM], score_grad)
    for group in range(3):
        dkv_ref[:, group * 128 : (group + 1) * 128] = columns[group].astype(dkv_ref.dtype)


def backward_sides(query, grad, mixed, lse):
    query_t = heads_across(query[...], KEY_HALF)
    grad_all = grad[...].T
    grad_t = [
        half_padded(grad_all[h * HEAD_DIM : (h + 1) * HEAD_DIM], VALUE_HALF[h]) for h in range(3)
    ]
    product = grad_all.astype(jnp.float32) * mixed[...]
    delta = [
        jnp.sum(product[h * HEAD_DIM : (h + 1) * HEAD_DIM], axis=0, keepdims=True)
        for h in range(3)
    ]
    query_m = [item.T for item in query_t]
    grad_m = [item.T for item in grad_t]
    return query_t, grad_t, query_m, grad_m, delta, lse[...]


def backward_far_kernel(place, query, grad, mixed, lse, kv_y, kv_both, dkv_y, dkv_both, query_grad_t):
    blk = place[0]
    query_grad_t[...] = jnp.zeros_like(query_grad_t)

    @pl.when((blk & 2) == 2)
    def _():
        sides = backward_sides(query, grad, mixed, lse)
        backward_block(sides, kv_y, dkv_y, query_grad_t, None)
        backward_block(sides, kv_both, dkv_both, query_grad_t, None)

    @pl.when((blk & 2) == 0)
    def _():
        dkv_y[...] = jnp.zeros_like(dkv_y)
        dkv_both[...] = jnp.zeros_like(dkv_both)


def backward_near_kernel(
    place, query, grad, mixed, lse, kv_own, kv_core, grad_t_in, dkv_own, dkv_core, query_grad, total
):
    blk, uly = place[0], place[1]
    total[...] = grad_t_in[...]
    sides = backward_sides(query, grad, mixed, lse)

    @pl.when((blk & 1) == 1)
    def _():
        backward_block(sides, kv_core, dkv_core, total, None)

    @pl.when((blk & 1) == 0)
    def _():
        dkv_core[...] = jnp.zeros_like(dkv_core)

    backward_block(sides, kv_own, dkv_own, total, causal(query.shape[0], uly))
    query_grad[...] = (total[...] * HEAD_DIM**-0.5).T.astype(jnp.bfloat16)


def on_core(kernel, place, operands, outs, scratch=()):
    vmem = pl.BlockSpec(memory_space=pltpu.VMEM)
    return pl.pallas_call(
        kernel,
        out_shape=[jax.ShapeDtypeStruct(shape, dtype) for shape, dtype in outs],
        in_specs=[pl.BlockSpec(memory_space=pltpu.SMEM)] + [vmem] * len(operands),
        out_specs=[vmem] * len(outs),
        scratch_shapes=[pltpu.VMEM(shape, dtype) for shape, dtype in scratch],
        compiler_params=pltpu.CompilerParams(vmem_limit_bytes=VMEM_LIMIT),
    )(place, *operands)


def normalized(rows):
    centre = rows - jnp.mean(rows, axis=-1, keepdims=True)
    rstd = lax.rsqrt(jnp.mean(centre * centre, axis=-1, keepdims=True) + 1e-05)
    return centre * rstd, rstd


def norm_back(grad, xhat, rstd):
    return rstd * (
        grad
        - jnp.mean(grad, axis=-1, keepdims=True)
        - xhat * jnp.mean(grad * xhat, axis=-1, keepdims=True)
    )


def gelu_tanh(inputs):
    return jax.nn.gelu(inputs, approximate=True)


def shards(
    tokens,
    query_weight,
    key_weight,
    value_weight,
    output_weight,
    up_weight,
    down_weight,
    query_bias,
    value_bias,
    output_bias,
    up_bias,
    down_bias,
    first_gain,
    first_shift,
    second_gain,
    second_shift,
    cotangent,
):
    bf16, f32 = jnp.bfloat16, jnp.float32
    uly, blk = lax.axis_index("uly"), lax.axis_index("blk")
    groups = lax.axis_size("uly")
    owners = lax.axis_size(CUBE)
    part = tokens.shape[0]
    rows = groups * part
    depth, width = query_weight.shape
    units = up_weight.shape[1]
    model = depth * owners
    place = jnp.stack([blk, uly]).astype(jnp.int32)

    qkv_own = jnp.concatenate(
        [key_weight, value_weight[:, 128:], value_weight[:, :128], query_weight], axis=1
    )
    vectors = [
        query_bias,
        value_bias,
        output_bias,
        down_bias,
        first_gain,
        first_shift,
        second_gain,
        second_shift,
    ]
    up_rows = up_bias.shape[0] // depth
    named = len(vectors) + up_rows
    wide = 3 * width
    vector_rows = jnp.concatenate(
        [vector.reshape(1, depth) for vector in vectors] + [up_bias.reshape(up_rows, depth)]
    )
    vector_rows = jnp.pad(vector_rows, ((0, VEC_ROWS - named), (0, wide - depth)))
    qkv_whole, vector_whole = cube_gathered(
        jnp.concatenate([qkv_own, vector_rows], axis=0),
        [(0, depth, 0, wide), (depth, VEC_ROWS, 0, wide)],
    )
    qkv_whole = qkv_whole.reshape(model, wide)
    vector_whole = vector_whole[:, :named, :depth].astype(f32)
    up_bias_whole = vector_whole[:, len(vectors) :].reshape(-1)
    named = vector_whole.transpose(1, 0, 2).reshape(named, model)
    query_bias_own = lax.dynamic_slice_in_dim(named[0], uly * width, width)
    value_bias_own = lax.dynamic_slice_in_dim(named[1], uly * width, width)
    up_bias_own = lax.dynamic_slice_in_dim(up_bias_whole, uly * units, units)
    output_bias_all, down_bias_all = named[2], named[3]
    gain1, shift1, gain2, shift2 = named[4], named[5], named[6], named[7]

    token_slots = slots_of(tokens)
    inputs = jnp.concatenate(token_slots, axis=0).astype(f32)
    cotangent_all = jnp.concatenate(slots_of(cotangent), axis=0)
    output_slots = slots_of(output_weight.T)
    rest_own = jnp.concatenate(output_slots + [up_weight, down_weight.T], axis=1)
    inner = groups * width
    output_t, up_whole, down_t = cube_gathered(
        rest_own,
        [(0, depth, 0, inner), (0, depth, inner, units), (0, depth, inner + units, units)],
    )
    output_t = output_t.reshape(model, inner)
    up_whole = up_whole.reshape(model, units)
    down_t = down_t.reshape(model, units)

    xhat1, rstd1 = normalized(inputs)
    xhat1_low = xhat1.astype(bf16)
    normed = (xhat1 * gain1 + shift1).astype(bf16)
    qkv_bias = jnp.concatenate(
        [
            jnp.zeros((width,), f32),
            value_bias_own[128:],
            value_bias_own[:128],
            query_bias_own,
        ]
    )
    qkv = (dot_plain(normed, qkv_whole) + qkv_bias).astype(bf16)
    kv_own = qkv[:, : 2 * width]
    query = qkv[:, 2 * width :] * jnp.asarray(HEAD_DIM**-0.5, bf16)
    kv_core = blk_swapped(kv_own, 1)
    kv_y = blk_swapped(kv_own, 2)
    kv_both = blk_swapped(kv_y, 1)
    stats = ((8, rows), f32)
    turned = ((width, rows), f32)
    top, total, mixed_t = on_core(
        forward_near_kernel, place, (query, kv_own, kv_core), (stats, stats, turned)
    )
    mixed, mixed_t, lse = on_core(
        forward_far_kernel,
        place,
        (query, kv_y, kv_both, top, total, mixed_t),
        (((rows, width), bf16), turned, stats),
        (stats, stats),
    )

    mixed_slots = [mixed] + [
        jnp.roll(passed_along(mixed, by), by * part, axis=0) for by in range(1, groups)
    ]
    branch = dot_cols(jnp.concatenate(mixed_slots, axis=1), output_t)
    middle = inputs + (branch + output_bias_all)
    xhat2, rstd2 = normalized(middle)
    xhat2_low = xhat2.astype(bf16)
    second = (xhat2 * gain2 + shift2).astype(bf16)
    hidden = dot_plain(second, up_whole) + up_bias_own
    active_wide, gelu_pull = jax.vjp(gelu_tanh, hidden)
    active = active_wide.astype(bf16)
    hidden_back = gelu_pull(dot_plain(cotangent_all, down_t))[0].astype(bf16)
    second_parts = dot_cols(hidden_back, up_whole).reshape(groups, part, model)
    second_back = slots_summed([second_parts[s] for s in range(groups)])
    outside_parts = dot_cols(active, down_t).reshape(groups, part, model)

    seed = cotangent.astype(f32)
    middle_back = seed + norm_back(second_back * gain2, xhat2[:part], rstd2[:part])
    branch_back = middle_back.astype(bf16)
    mixed_back = dot_plain(branch_back, output_t).astype(bf16)
    grad_slots = [mixed_back[:, :width]] + [
        passed_along(mixed_back[:, by * width : (by + 1) * width], -by)
        for by in range(groups - 1, 0, -1)
    ]
    mixed_grad = jnp.concatenate(grad_slots, axis=0)
    sides = (query, mixed_grad, mixed_t, lse)
    pair = ((rows, 2 * width), bf16)
    dkv_y, dkv_both, query_grad_t = on_core(
        backward_far_kernel, place, sides + (kv_y, kv_both), (pair, pair, turned)
    )
    dkv_far = dkv_y.astype(f32) + blk_swapped(dkv_both, 1).astype(f32)
    dkv_from_y = blk_swapped(dkv_far.astype(bf16), 2)
    dkv_own, dkv_core, query_grad = on_core(
        backward_near_kernel,
        place,
        sides + (kv_own, kv_core, query_grad_t),
        (pair, pair, ((rows, width), bf16)),
        (turned,),
    )
    dkv = (
        dkv_own.astype(f32) + blk_swapped(dkv_core, 1).astype(f32) + dkv_from_y.astype(f32)
    ).astype(bf16)
    dqkv = jnp.concatenate([dkv, query_grad], axis=1)

    outside = slots_summed([outside_parts[s] for s in range(groups)])
    result = (middle[:part] + (outside + down_bias_all)).astype(bf16)

    up_grad = dot_rows(xhat2_low, hidden_back)
    down_grad_t = dot_rows(cotangent_all, active)
    wide_total = cube_summed(
        jnp.concatenate([up_grad, down_grad_t], axis=1).reshape(owners, depth, 2 * units)
    )
    hidden_sum = jnp.sum(hidden_back.astype(f32), axis=0)
    seed_sum = jnp.sum(cotangent_all.astype(f32), axis=0)

    branch_all = jnp.concatenate(slots_of(branch_back), axis=0)
    output_grad_t = dot_rows(branch_all, mixed)
    branch_sum = jnp.sum(branch_all.astype(f32), axis=0)
    qkv_grad = dot_rows(xhat1_low, dqkv)
    qkv_sum = jnp.sum(dqkv.astype(f32), axis=0)
    columns = wide + width
    sums = jnp.zeros((owners, VEC_ROWS, columns), f32)
    sums = sums.at[:, 0, :wide].set(qkv_sum[None])
    sums = sums.at[:, 1, :units].set(hidden_sum[None])
    sums = sums.at[:, 2, :depth].set(branch_sum.reshape(owners, depth))
    sums = sums.at[:, 3, :depth].set(seed_sum.reshape(owners, depth))
    blocks = jnp.concatenate(
        [jnp.concatenate([qkv_grad, output_grad_t], axis=1).reshape(owners, depth, columns), sums],
        axis=1,
    )
    near_total = cube_summed(blocks)

    normed_parts = dot_cols(dqkv, qkv_whole).reshape(groups, part, model)
    normed_back = slots_summed([normed_parts[s] for s in range(groups)])
    input_grad = (
        middle_back + norm_back(normed_back * gain1, xhat1[:part], rstd1[:part])
    ).astype(bf16)

    qkv_total = near_total[:depth, :wide]
    output_total = near_total[:depth, wide:].T
    qkv_sums, hidden_sums = near_total[depth, :wide], near_total[depth + 1, :units]
    branch_sums, seed_sums = near_total[depth + 2, :depth], near_total[depth + 3, :depth]
    up_total, down_total = wide_total[:, :units], wide_total[:, units:].T
    own_gain1, own_shift1 = first_gain.astype(f32), first_shift.astype(f32)
    own_gain2, own_shift2 = second_gain.astype(f32), second_shift.astype(f32)
    qkv_weight_grad = own_gain1[:, None] * qkv_total + own_shift1[:, None] * qkv_sums[None]
    up_weight_grad = own_gain2[:, None] * up_total + own_shift2[:, None] * hidden_sums[None]
    qkv_wide, up_wide = qkv_own.astype(f32), up_weight.astype(f32)
    terms = jnp.concatenate(
        [
            jnp.sum(qkv_wide * qkv_total, axis=1),
            jnp.sum(qkv_wide * qkv_sums[None], axis=1),
            jnp.sum(up_wide * up_total, axis=1),
            jnp.sum(up_wide * hidden_sums[None], axis=1),
            qkv_sums[2 * width :],
            qkv_sums[width + 64 : 2 * width],
            qkv_sums[width : width + 64],
            hidden_sums,
        ]
    )
    all_terms = jnp.stack(slots_of(terms))
    share = depth // groups
    added = jnp.sum(all_terms[:, : 4 * depth], axis=0).reshape(4, depth)
    added = lax.dynamic_slice_in_dim(added, uly * share, share, axis=1)
    rank = cube_index() * groups + uly

    def owned(start, length, count):
        at = rank * count
        source = (uly - at // length) % groups
        return lax.dynamic_slice(all_terms, (source, start + at % length), (1, count))[0]

    query_bias_grad = owned(4 * depth, width, share)
    value_bias_grad = owned(4 * depth + width, width, share)
    up_bias_grad = owned(4 * depth + 2 * width, units, up_bias.shape[0] // groups)
    output_bias_grad = lax.dynamic_slice_in_dim(branch_sums, uly * share, share)
    down_bias_grad = lax.dynamic_slice_in_dim(seed_sums, uly * share, share)
    value_weight_grad = jnp.concatenate(
        [qkv_weight_grad[:, width + 64 : 2 * width], qkv_weight_grad[:, width : width + 64]], axis=1
    )
    return (
        result,
        input_grad,
        qkv_weight_grad[:, 2 * width :],
        qkv_weight_grad[:, :width],
        value_weight_grad,
        output_total,
        up_weight_grad,
        down_total,
        query_bias_grad,
        value_bias_grad,
        output_bias_grad,
        up_bias_grad,
        down_bias_grad,
        added[0],
        added[1],
        added[2],
        added[3],
    )


def solution(mesh):
    rows = P(("fsdp", "blk", "uly"), None)
    tall, flat = P(("fsdp", "blk"), "uly"), P("uly", ("fsdp", "blk"))
    vector, vector_out = P(("fsdp", "blk")), P(("fsdp", "blk", "uly"))
    return jax.shard_map(
        shards,
        mesh=mesh,
        in_specs=(rows, tall, tall, tall, flat, tall, flat) + (vector,) * 9 + (rows,),
        out_specs=(rows, rows, tall, tall, tall, flat, tall, flat) + (vector_out,) * 9,
        check_vma=False,
    )
```

```python
import jax
import jax.numpy as jnp
from jax import lax
from jax.experimental import pallas as pl
from jax.experimental.pallas import tpu as pltpu
from jax.sharding import PartitionSpec as P

HEAD_DIM = 64
CUBE = ("fsdp", "blk")
VEC_ROWS = 16
VMEM_LIMIT = 56 * 1024 * 1024
KERNEL_COST = 30_000_000_000
BRIEF_COST = 1
NEAR_COST = 3_000_000_000

KEY_GROUP, KEY_HALF = (0, 0, 1), (0, 1, 0)
VALUE_GROUP, VALUE_HALF = (2, 2, 1), (0, 1, 1)


def dot_plain(left, right):
    return jnp.dot(left, right, preferred_element_type=jnp.float32)


def dot_rows(left, right):
    return lax.dot_general(
        left, right, (((0,), (0,)), ((), ())), preferred_element_type=jnp.float32
    )


def dot_cols(left, right):
    return lax.dot_general(
        left, right, (((1,), (1,)), ((), ())), preferred_element_type=jnp.float32
    )


def passed_along(array, by):
    peers = lax.axis_size("uly")
    return lax.ppermute(array, "uly", [(i, (i + by) % peers) for i in range(peers)])


def slots_of(array):
    return [array] + [passed_along(array, by) for by in range(1, lax.axis_size("uly"))]


def blk_swapped(array, flip):
    peers = lax.axis_size("blk")
    return lax.ppermute(array, "blk", [(i, i ^ flip) for i in range(peers)])


def cube_swapped(array, even, odd):
    peers = lax.axis_size(CUBE)
    pairs = [(i, i ^ (odd if i & 1 else even)) for i in range(peers)]
    return lax.ppermute(array, CUBE, pairs)


def cube_index():
    return lax.axis_index("fsdp") * lax.axis_size("blk") + lax.axis_index("blk")


def place_kernel(cuts, index_ref, own, first, second, other, *outs):
    me = index_ref[0]
    odd = me & 1
    near, far = jnp.where(odd == 1, 2, 4), jnp.where(odd == 1, 4, 2)
    pieces = [
        (own, 0),
        (first, near),
        (second.at[0], far),
        (second.at[1], 6),
        (other.at[0], 1),
        (other.at[1], far ^ 1),
        (other.at[2], near ^ 1),
        (other.at[3], 7),
    ]
    for piece, flip in pieces:
        for out, (row, rows, column, columns) in zip(outs, cuts):
            out[me ^ flip] = piece[row : row + rows, column : column + columns]


def paired():
    return lax.axis_size("fsdp") == 2 and lax.axis_size("blk") == 4


def after(array, *others):
    return lax.optimization_barrier((array,) + others)[0]


def cube_placed(cuts, pieces):
    index = cube_index().astype(jnp.int32).reshape(1)
    outs = [((8, rows, columns), pieces[0].dtype) for _, rows, _, columns in cuts]
    return on_core(lambda *refs: place_kernel(cuts, *refs), index, pieces, outs)


def cube_flips(me):
    odd = me & 1
    return jnp.where(odd == 1, 2, 4), jnp.where(odd == 1, 4, 2)


def grads_kernel(pairs, spread, index, *refs):
    ins, (sent, kept), (whole, extra) = refs[:-4], refs[-4:-2], refs[-2:]
    at = 0
    lefts = []
    for count, last, pad, column, columns in pairs:
        left, right = stacked_slots(ins[at : at + count], last), ins[at + count][...]
        at += count + 1
        if pad:
            right = jnp.concatenate([jnp.zeros((pad, right.shape[1]), right.dtype), right], axis=0).T
        term = dot_plain(left.T, right)
        if pad:
            whole[:, column : column + columns] += term
        else:
            whole[:, column : column + columns] = term
        lefts.append((left, right))
    rows = kept.shape[1]
    depth = whole.shape[0] // 8
    if spread:
        hidden_sum, seed_sum = ins[at][...], ins[at + 1][...]
        qkv_sum = jnp.sum(lefts[0][1].astype(jnp.float32), axis=0, keepdims=True)
        branch_sum = jnp.sum(lefts[1][0].astype(jnp.float32), axis=0, keepdims=True)
        wide = whole.shape[1]
        stacked = jnp.concatenate(
            [qkv_sum, hidden_sum, branch_sum, seed_sum, jnp.zeros((4, wide), jnp.float32)], axis=0
        )
        line = lax.broadcasted_iota(jnp.int32, stacked.shape, 0)
        for block in range(8):
            turned = stacked if block == 0 else pltpu.roll(stacked, wide - depth * block, 1)
            extra[block, 0:8] = jnp.where(line < 2, stacked, turned)
            extra[block, 8:16] = jnp.zeros((8, wide), jnp.float32)
    me = index[0]
    near, far = cube_flips(me)
    for slot, flip in enumerate((0, near, far, 6)):
        block = me ^ flip ^ 1
        sent[slot, 0:depth] = whole[pl.ds(pl.multiple_of(block * depth, 8), depth)].astype(sent.dtype)
        if spread:
            sent[slot, depth:rows] = extra[block].astype(sent.dtype)
    for slot, flip in enumerate((0, far, near, 6)):
        block = me ^ flip
        kept[slot, 0:depth] = whole[pl.ds(pl.multiple_of(block * depth, 8), depth)]
        if spread:
            kept[slot, depth:rows] = extra[block]


def grads_sent(pairs, columns, depth, sums):
    plan = [
        (len(left), last, pad, column, right.shape[0] + pad if pad else right.shape[1])
        for left, last, right, pad, column in pairs
    ]
    operands = [item for left, _, right, _, _ in pairs for item in [*left, right]]
    rows = depth + (VEC_ROWS if sums else 0)
    index = cube_index().astype(jnp.int32).reshape(1)
    return on_core(
        lambda *refs: grads_kernel(plan, bool(sums), *refs),
        index,
        operands + list(sums),
        [((4, rows, columns), jnp.bfloat16), ((4, rows, columns), jnp.float32)],
        [((8 * depth, columns), jnp.float32), ((8, VEC_ROWS, columns), jnp.float32)],
    )


def grads_scattered(pairs, columns, owners, sums):
    model = pairs[0][0][0].shape[1]
    depth = model // owners
    whole = jnp.zeros((model, columns), jnp.float32)

    pairs = [(stacked_slots(left, last), *rest) for left, last, *rest in pairs]
    for left, right, pad, column in pairs:
        if pad:
            column += pad
            right = right.T
        term = dot_rows(left, right)
        whole = whole.at[:, column : column + term.shape[1]].add(term)
    blocks = whole.reshape(owners, depth, columns)
    if sums:
        hidden_sum, seed_sum = sums
        branch_sum = jnp.sum(pairs[1][0].astype(jnp.float32), axis=0)
        extra = jnp.zeros((owners, VEC_ROWS, columns), jnp.float32)
        extra = extra.at[:, 0].set(jnp.sum(pairs[0][1].astype(jnp.float32), axis=0)[None])
        extra = extra.at[:, 1].set(hidden_sum)
        extra = extra.at[:, 2, :depth].set(branch_sum.reshape(owners, depth))
        extra = extra.at[:, 3, :depth].set(seed_sum.reshape(owners, depth))
        blocks = jnp.concatenate([blocks, extra], axis=1)
    return lax.psum_scatter(blocks, CUBE, scatter_dimension=0, tiled=False)


def half_padded(part, half):
    zero = jnp.zeros_like(part)
    return jnp.concatenate([part, zero] if half == 0 else [zero, part], axis=0)


def heads_across(array, halves):
    turned = array.T
    return [
        half_padded(turned[h * HEAD_DIM : (h + 1) * HEAD_DIM], halves[h])
        for h in range(len(halves))
    ]


def group_of(ref, group):
    return ref[:, group * 128 : (group + 1) * 128]


def slot_places(index, uly, slot_rows):
    return ((uly - index // slot_rows) & 3) * slot_rows + index % slot_rows


def causal(rows, uly):
    keys = lax.broadcasted_iota(jnp.int32, (rows, rows), 0)
    queries = lax.broadcasted_iota(jnp.int32, (rows, rows), 1)
    slot_rows = rows // 4
    return slot_places(keys, uly, slot_rows) <= slot_places(queries, uly, slot_rows)


def forward_block(query_t, kv_ref, top, total, mixed, allowed):
    turned = kv_ref[...].T
    for h in range(3):
        scores = dot_plain(group_of(kv_ref, KEY_GROUP[h]), query_t[h])
        if allowed is not None:
            scores = jnp.where(allowed, scores, -1e30)
        block_top = jnp.max(scores, axis=0, keepdims=True)
        low = VALUE_GROUP[h] * 128 + VALUE_HALF[h] * HEAD_DIM
        value_t = turned[low : low + HEAD_DIM]
        own = pl.ds(h * HEAD_DIM, HEAD_DIM)
        if allowed is not None:
            weights = jnp.exp(scores - block_top)
            top[h : h + 1] = block_top
            total[h : h + 1] = jnp.sum(weights, axis=0, keepdims=True)
            mixed[own] = dot_plain(value_t, weights.astype(jnp.bfloat16))
        else:
            old_top = top[h : h + 1]
            new_top = jnp.maximum(old_top, block_top)
            fade = jnp.exp(old_top - new_top)
            weights = jnp.exp(scores - new_top)
            top[h : h + 1] = new_top
            total[h : h + 1] = total[h : h + 1] * fade + jnp.sum(weights, axis=0, keepdims=True)
            mixed[own] = mixed[own] * fade + dot_plain(value_t, weights.astype(jnp.bfloat16))


def forward_near_kernel(place, query, kv_own, kv_core, top, total, mixed):
    blk, uly = place[0], place[1]
    query_t = heads_across(query[...], KEY_HALF)
    top[...] = jnp.zeros_like(top)
    total[...] = jnp.ones_like(total)
    forward_block(query_t, kv_own, top, total, mixed, causal(query.shape[0], uly))

    @pl.when((blk & 1) == 1)
    def _():
        forward_block(query_t, kv_core, top, total, mixed, None)


def forward_far_kernel(
    place, query, kv_y, kv_both, top_in, total_in, mixed_in, out, mixed, lse, top, total
):
    blk = place[0]
    top[...] = top_in[...]
    total[...] = total_in[...]
    mixed[...] = mixed_in[...]

    @pl.when((blk & 2) == 2)
    def _():
        query_t = heads_across(query[...], KEY_HALF)
        forward_block(query_t, kv_y, top, total, mixed, None)
        forward_block(query_t, kv_both, top, total, mixed, None)

    for h in range(3):
        own = pl.ds(h * HEAD_DIM, HEAD_DIM)
        mixed[own] = mixed[own] / total[h : h + 1]
    lse[...] = top[...] + jnp.log(total[...])
    out[...] = mixed[...].astype(jnp.bfloat16)


def backward_block(sides, kv_ref, dkv_ref, query_grad_t, allowed):
    query_t, grad_t, query_m, grad_m, delta, lse = sides
    turned = kv_ref[...].T
    columns = [None, None, None]

    def add(group, term):
        columns[group] = term if columns[group] is None else columns[group] + term

    for h in range(3):
        scores = dot_plain(group_of(kv_ref, KEY_GROUP[h]), query_t[h])
        probs = jnp.exp(scores - lse[h : h + 1])
        if allowed is not None:
            probs = jnp.where(allowed, probs, 0.0)
        prob_grad = dot_plain(group_of(kv_ref, VALUE_GROUP[h]), grad_t[h])
        score_grad = (probs * (prob_grad - delta[h])).astype(jnp.bfloat16)
        add(VALUE_GROUP[h], dot_plain(probs.astype(jnp.bfloat16), grad_m[h]))
        add(KEY_GROUP[h], dot_plain(score_grad, query_m[h]))
        low = KEY_GROUP[h] * 128 + KEY_HALF[h] * HEAD_DIM
        own = pl.ds(h * HEAD_DIM, HEAD_DIM)
        query_grad_t[own] += dot_plain(turned[low : low + HEAD_DIM], score_grad)
    for group in range(3):
        dkv_ref[:, group * 128 : (group + 1) * 128] = columns[group].astype(dkv_ref.dtype)


def backward_sides(query, grads, mixed, lse):
    query_t = heads_across(query[...], KEY_HALF)
    grad_all = jnp.concatenate([ref[...] for ref in grads], axis=1)
    grad_t = [
        half_padded(grad_all[h * HEAD_DIM : (h + 1) * HEAD_DIM], VALUE_HALF[h]) for h in range(3)
    ]
    product = grad_all.astype(jnp.float32) * mixed[...]
    delta = [
        jnp.sum(product[h * HEAD_DIM : (h + 1) * HEAD_DIM], axis=0, keepdims=True)
        for h in range(3)
    ]
    query_m = [item.T for item in query_t]
    grad_m = [item.T for item in grad_t]
    return query_t, grad_t, query_m, grad_m, delta, lse[...]


def backward_both_kernel(place, query, g0, g1, g2, g3, mixed, lse, kv_both, dkv_both, query_grad_t):
    query_grad_t[...] = jnp.zeros_like(query_grad_t)

    @pl.when((place[0] & 2) == 2)
    def _():
        sides = backward_sides(query, (g0, g1, g2, g3), mixed, lse)
        backward_block(sides, kv_both, dkv_both, query_grad_t, None)

    @pl.when((place[0] & 2) == 0)
    def _():
        dkv_both[...] = jnp.zeros_like(dkv_both)


def backward_y_kernel(
    place, query, g0, g1, g2, g3, mixed, lse, kv_y, dkv_core, grad_t_in, dkv_y, total, part
):
    total[...] = grad_t_in[...]

    @pl.when((place[0] & 2) == 2)
    def _():
        sides = backward_sides(query, (g0, g1, g2, g3), mixed, lse)
        backward_block(sides, kv_y, part, total, None)
        dkv_y[...] = (part[...] + dkv_core[...].astype(jnp.float32)).astype(dkv_y.dtype)

    @pl.when((place[0] & 2) == 0)
    def _():
        dkv_y[...] = jnp.zeros_like(dkv_y)


def backward_near_kernel(
    place,
    query,
    g0,
    g1,
    g2,
    g3,
    mixed,
    lse,
    kv_own,
    kv_core,
    grad_t_in,
    dkv_own,
    dkv_core,
    query_grad,
    total,
):
    blk, uly = place[0], place[1]
    total[...] = grad_t_in[...]
    sides = backward_sides(query, (g0, g1, g2, g3), mixed, lse)

    @pl.when((blk & 1) == 1)
    def _():
        backward_block(sides, kv_core, dkv_core, total, None)

    @pl.when((blk & 1) == 0)
    def _():
        dkv_core[...] = jnp.zeros_like(dkv_core)

    backward_block(sides, kv_own, dkv_own, total, causal(query.shape[0], uly))
    query_grad[...] = (total[...] * HEAD_DIM**-0.5).T.astype(jnp.bfloat16)


def on_core(kernel, place, operands, outs, scratch=(), cost=KERNEL_COST):
    vmem = pl.BlockSpec(memory_space=pltpu.VMEM)
    return pl.pallas_call(
        kernel,
        out_shape=[jax.ShapeDtypeStruct(shape, dtype) for shape, dtype in outs],
        in_specs=[pl.BlockSpec(memory_space=pltpu.SMEM)] + [vmem] * len(operands),
        out_specs=[vmem] * len(outs),
        scratch_shapes=[pltpu.VMEM(shape, dtype) for shape, dtype in scratch],
        compiler_params=pltpu.CompilerParams(vmem_limit_bytes=VMEM_LIMIT),
        cost_estimate=pl.CostEstimate(flops=cost, transcendentals=0, bytes_accessed=0),
    )(place, *operands)


def normalized(rows):
    centre = rows - jnp.mean(rows, axis=-1, keepdims=True)
    rstd = lax.rsqrt(jnp.mean(centre * centre, axis=-1, keepdims=True) + 1e-05)
    return centre * rstd, rstd


def norm_back(grad, xhat, rstd):
    return rstd * (
        grad
        - jnp.mean(grad, axis=-1, keepdims=True)
        - xhat * jnp.mean(grad * xhat, axis=-1, keepdims=True)
    )


def stacked_slots(refs, last=False):
    rows = refs[0].shape[0]
    return jnp.concatenate(
        [ref[ref.shape[0] - rows :] if last else ref[:rows] for ref in refs], axis=0
    )


def project_kernel(place, t0, t1, t2, t3, weight, named, bias, query, kv, xhat_low):
    rows = stacked_slots((t0, t1, t2, t3)).astype(jnp.float32)
    xhat, _ = normalized(rows)
    xhat_low[...] = xhat.astype(jnp.bfloat16)
    normed = (xhat * named[0:1] + named[1:2]).astype(jnp.bfloat16)
    qkv = dot_plain(normed, weight[...]) + bias[...]
    wide = kv.shape[1]
    kv[...] = qkv[:, :wide].astype(jnp.bfloat16)
    query[...] = qkv[:, wide:].astype(jnp.bfloat16) * jnp.asarray(HEAD_DIM**-0.5, jnp.bfloat16)


GELU_A, GELU_B = 0.7978845608028654, 0.044715


def middle_kernel(
    place,
    m0,
    m1,
    m2,
    m3,
    t0,
    t1,
    t2,
    t3,
    c0,
    c1,
    c2,
    c3,
    output_t,
    up,
    down_t,
    named,
    up_bias,
    middle_own,
    xhat_low,
    active_low,
    hidden_back_low,
    part_own,
    *parts,
):
    slot = t0.shape[0]
    mixed_t = jnp.concatenate(
        [m0[...]]
        + [
            jnp.concatenate([ref[:, (4 - by) * slot :], ref[:, : (4 - by) * slot]], axis=1)
            for by, ref in ((1, m1), (2, m2), (3, m3))
        ],
        axis=0,
    )
    branch = dot_plain(output_t[...], mixed_t).T
    middle = stacked_slots((t0, t1, t2, t3)).astype(jnp.float32) + (branch + named[0:1])
    middle_own[...] = middle[:slot]
    xhat, _ = normalized(middle)
    xhat_low[...] = xhat.astype(jnp.bfloat16)
    second = (xhat * named[1:2] + named[2:3]).astype(jnp.bfloat16)
    hidden = dot_plain(second, up[...]) + up_bias[...]
    active_grad = dot_plain(stacked_slots((c0, c1, c2, c3)), down_t[...])
    square = hidden * hidden
    bent = jnp.tanh(GELU_A * hidden * (1.0 + GELU_B * square))
    active_low[...] = (0.5 * hidden * (1.0 + bent)).astype(jnp.bfloat16)
    slope = 0.5 * (1.0 + bent) + (0.5 * GELU_A) * hidden * (1.0 - bent * bent) * (
        1.0 + (3.0 * GELU_B) * square
    )
    hidden_back = (active_grad * slope).astype(jnp.bfloat16)
    hidden_back_low[...] = hidden_back
    second_back = dot_cols(hidden_back, up[...])
    part_own[...] = second_back[:slot]
    for by in range(1, 4):
        parts[by - 1][...] = second_back[by * slot : (by + 1) * slot].astype(jnp.bfloat16)


def outside_kernel(
    place, active, down_t, hidden_back, c0, c1, c2, c3, hidden_sum, seed_sum, part_own, *parts
):
    slot = part_own.shape[0]
    outside = dot_cols(active[...], down_t[...])
    part_own[...] = outside[:slot]
    for by in range(1, 4):
        parts[by - 1][...] = outside[by * slot : (by + 1) * slot].astype(jnp.bfloat16)
    hidden_sum[...] = jnp.sum(hidden_back[...].astype(jnp.float32), axis=0, keepdims=True)
    seed = stacked_slots((c0, c1, c2, c3)).astype(jnp.float32)
    seed_sum[...] = jnp.sum(seed, axis=0, keepdims=True)


def branch_kernel(
    place,
    part_own,
    r1,
    r2,
    r3,
    middle,
    seed,
    gain,
    output_t,
    o1,
    o2,
    o3,
    middle_back,
    branch_back,
    s1,
    s2,
    s3,
    *mixed_back_t,
):
    second_back = part_own[...]
    for ref in (r1, r2, r3):
        second_back = second_back + ref[...].astype(jnp.float32)
    xhat, rstd = normalized(middle[...])
    grad = seed[...].astype(jnp.float32) + norm_back(second_back * gain[...], xhat, rstd)
    middle_back[...] = grad
    low = grad.astype(jnp.bfloat16)
    branch_back[...] = low
    slot = low.shape[0]
    for ref, outside in ((s1, o1), (s2, o2), (s3, o3)):
        ref[:slot] = outside[...]
        ref[slot:] = low
    turned = dot_plain(low, output_t[...]).T.astype(jnp.bfloat16)
    width = mixed_back_t[0].shape[0]
    for by in range(4):
        mixed_back_t[by][...] = turned[by * width : (by + 1) * width]


def gather_back_kernel(place, own, core, far, query, weight, dqkv, part_own, *parts):
    wide = own.shape[1]
    width = query.shape[1]
    total = own[...].astype(jnp.float32) + core[...].astype(jnp.float32)
    kv_grad = (total + far[...].astype(jnp.float32)).astype(jnp.bfloat16)
    dqkv[:, :wide] = kv_grad
    dqkv[:, wide : wide + width] = query[...]
    dqkv[:, wide + width :] = jnp.zeros((query.shape[0], width), jnp.bfloat16)
    normed_back = dot_cols(dqkv[:, : wide + width], weight[...])
    slot = part_own.shape[0]
    part_own[...] = normed_back[:slot]
    for by in range(1, 4):
        parts[by - 1][...] = normed_back[by * slot : (by + 1) * slot].astype(jnp.bfloat16)


def slots_returned(parts):
    return [passed_along(parts[by - 1], -by) for by in range(1, 4)]


def shards(
    tokens,
    query_weight,
    key_weight,
    value_weight,
    output_weight,
    up_weight,
    down_weight,
    query_bias,
    value_bias,
    output_bias,
    up_bias,
    down_bias,
    first_gain,
    first_shift,
    second_gain,
    second_shift,
    cotangent,
):
    bf16, f32 = jnp.bfloat16, jnp.float32
    uly, blk = lax.axis_index("uly"), lax.axis_index("blk")
    groups = lax.axis_size("uly")
    owners = lax.axis_size(CUBE)
    part = tokens.shape[0]
    rows = groups * part
    depth, width = query_weight.shape
    units = up_weight.shape[1]
    model = depth * owners
    place = jnp.stack([blk, uly]).astype(jnp.int32)

    qkv_own = jnp.concatenate(
        [key_weight, value_weight[:, 128:], value_weight[:, :128], query_weight], axis=1
    )
    vectors = [
        query_bias,
        value_bias,
        output_bias,
        down_bias,
        first_gain,
        first_shift,
        second_gain,
        second_shift,
    ]
    up_rows = up_bias.shape[0] // depth
    named = len(vectors) + up_rows
    wide = 3 * width
    vector_rows = jnp.concatenate(
        [vector.reshape(1, depth) for vector in vectors] + [up_bias.reshape(up_rows, depth)]
    )
    vector_rows = jnp.pad(vector_rows, ((0, VEC_ROWS - named), (0, wide - depth)))
    chunk = depth // groups
    output_own = output_weight.T
    output_rows = jnp.concatenate(
        [output_own[at * chunk : (at + 1) * chunk] for at in range(groups)], axis=1
    )
    spare = -(part + chunk) % 16
    token_sent = jnp.concatenate([tokens, jnp.pad(output_rows, ((0, spare), (0, 0)))], axis=0)
    token_slots = [tokens, passed_along(token_sent, 1), None, None]
    qkv_sent = jnp.concatenate([qkv_own, vector_rows], axis=0)
    qkv_cuts = [(0, depth, 0, wide), (depth, VEC_ROWS, 0, wide)]
    if paired():
        qkv_sent = after(qkv_sent, token_slots[1])
        token_later = after(token_sent, token_slots[1])
        token_slots[3] = passed_along(token_later, 3)
        token_slots[2] = passed_along(token_later, 2)
        qkv_first = after(cube_swapped(qkv_sent, 4, 2), token_slots[3])
        qkv_second = cube_swapped(jnp.stack([qkv_sent, qkv_first]), 2, 4)
        qkv_second = after(qkv_second, token_slots[2])
        qkv_other = cube_swapped(
            jnp.concatenate([qkv_sent[None], qkv_first[None], qkv_second]), 1, 1
        )
        qkv_whole, vector_whole = cube_placed(
            qkv_cuts, (qkv_sent, qkv_first, qkv_second, qkv_other)
        )
    else:
        token_slots = [tokens] + slots_of(token_sent)[1:]
        whole = lax.all_gather(qkv_sent, CUBE, axis=0, tiled=False)
        qkv_whole, vector_whole = whole[:, :depth], whole[:, depth:]
    qkv_whole = qkv_whole.reshape(model, wide)
    vector_whole = vector_whole[:, :named, :depth].astype(f32)
    up_bias_whole = vector_whole[:, len(vectors) :].reshape(-1)
    named = vector_whole.transpose(1, 0, 2).reshape(named, model)
    query_bias_own = lax.dynamic_slice_in_dim(named[0], uly * width, width)
    value_bias_own = lax.dynamic_slice_in_dim(named[1], uly * width, width)
    up_bias_own = lax.dynamic_slice_in_dim(up_bias_whole, uly * units, units)
    output_bias_all, down_bias_all = named[2], named[3]
    gain1, gain2, shift2 = named[4], named[6], named[7]

    qkv_bias = jnp.concatenate(
        [jnp.zeros((width,), f32), value_bias_own[128:], value_bias_own[:128], query_bias_own]
    )

    units_grad = 2 * units
    inner = groups * width
    rest_cuts = [
        (0, depth, 0, inner),
        (0, depth, inner, units),
        (0, depth, inner + units, units),
    ]
    cotangent_later = after(cotangent, *token_slots[1:])
    cotangent_slots = [cotangent] + [passed_along(cotangent_later, by) for by in range(1, groups)]
    output_slots = [output_own] + [
        jnp.concatenate(
            [item[part : part + chunk, at * width : (at + 1) * width] for at in range(groups)], axis=0
        )
        for item in token_slots[1:]
    ]
    rest_own = jnp.concatenate(output_slots + [up_weight, down_weight.T], axis=1)
    if paired():
        rest_own = after(rest_own, qkv_second)
        rest_first = cube_swapped(rest_own, 4, 2)

    query, kv_own, xhat1_low = on_core(
        project_kernel,
        place,
        token_slots + [after(qkv_whole, cotangent_slots[1]), named[4:6], qkv_bias[None]],
        [((rows, width), bf16), ((rows, 2 * width), bf16), ((rows, model), bf16)],
    )
    kv_y = blk_swapped(kv_own, 2)
    kv_core = blk_swapped(kv_own, 1)
    stats = ((8, rows), f32)
    turned = ((width, rows), f32)
    top, total, mixed_t = on_core(
        forward_near_kernel, place, (query, kv_own, kv_core), (stats, stats, turned)
    )
    kv_both = after(blk_swapped(after(kv_y, top), 1), *cotangent_slots[2:])
    if paired():
        rest_second = cube_swapped(after(jnp.stack([rest_own, rest_first]), kv_own), 2, 4)
        rest_second = after(rest_second, kv_both)
        rest_held = jnp.concatenate([rest_own[None], rest_first[None], rest_second])
        rest_other = cube_swapped(rest_held, 1, 1)
        kv_both = after(kv_both, rest_held)
    mixed_low, mixed_t, lse = on_core(
        forward_far_kernel,
        place,
        (query, kv_y, kv_both, top, total, mixed_t),
        (((width, rows), bf16), turned, stats),
        (stats, stats),
    )
    mixed_slots = slots_of(mixed_low)
    if paired():
        rest_other = after(rest_other, mixed_low)
        output_t, up_whole, down_t = cube_placed(
            rest_cuts, (rest_own, rest_first, rest_second, rest_other)
        )
    else:
        whole = lax.all_gather(rest_own, CUBE, axis=0, tiled=False)
        output_t, up_whole, down_t = [whole[:, :, c : c + n] for _, _, c, n in rest_cuts]
    output_t = output_t.reshape(model, inner)
    up_whole = up_whole.reshape(model, units)
    down_t = down_t.reshape(model, units)

    slab = ((part, model), f32)
    slabs = [((part, model), bf16)] * (groups - 1)
    wide_low = ((rows, model), bf16)
    units_low = ((rows, units), bf16)
    middle, xhat2_low, active, hidden_back, second_own, *second_parts = on_core(
        middle_kernel,
        place,
        mixed_slots
        + token_slots
        + cotangent_slots
        + [output_t, up_whole, down_t, jnp.stack([output_bias_all, gain2, shift2]), up_bias_own[None]],
        [slab, wide_low, units_low, units_low, slab] + slabs,
    )
    second_returned = slots_returned(second_parts)
    wide_pairs = [
        ([xhat2_low], False, hidden_back, 0, 0),
        (cotangent_slots, False, active, 0, units),
    ]
    if paired():
        wide_sent, wide_kept = grads_sent(wide_pairs, units_grad, depth, ())
        second_own = after(second_own, wide_sent)
    hidden_sum, seed_sum, outside_own, *outside_parts = on_core(
        outside_kernel,
        place,
        [active, down_t, hidden_back] + cotangent_slots,
        [((1, units), f32), ((1, model), f32), slab] + slabs,
    )
    second_own = after(second_own, outside_own)

    middle_back, branch_back, s1, s2, s3, *mixed_back_t = on_core(
        branch_kernel,
        place,
        [second_own] + second_returned + [middle, cotangent, gain2[None], output_t] + outside_parts,
        [slab, ((part, model), bf16)]
        + [((2 * part, model), bf16)] * 3
        + [((width, part), bf16)] * groups,
    )
    grad_slots = [mixed_back_t[0]] + [
        passed_along(mixed_back_t[by], -by) for by in range(groups - 1, 0, -1)
    ]
    if paired():
        wide_got = cube_swapped(after(wide_sent, mixed_back_t[0]), 1, 1)
    sides = [query] + grad_slots + [mixed_t, lse]
    pair = ((rows, 2 * width), bf16)
    dkv_both, query_grad_t = on_core(
        backward_both_kernel, place, sides + [kv_both], (pair, turned), cost=BRIEF_COST
    )
    shared = slots_returned([after(item, *grad_slots[1:]) for item in (s1, s2, s3)])
    branch_slots = [branch_back] + shared[::-1]
    if paired():
        wide_held = wide_kept + after(wide_got, dkv_both).astype(f32)
        wide_sent = wide_held[2:].astype(bf16)
        wide_got = cube_swapped(wide_sent, 4, 2)
    dkv_y, query_grad_t = on_core(
        backward_y_kernel,
        place,
        sides + [kv_y, blk_swapped(dkv_both, 1), query_grad_t],
        (pair, turned),
        [((rows, 2 * width), f32)],
        cost=BRIEF_COST,
    )
    dkv_from_y = blk_swapped(dkv_y, 2)
    if paired():
        wide_got = after(wide_got, dkv_y).astype(f32)
        wide_held = wide_held[:2] + wide_got
        wide_sent = wide_held[1].astype(bf16)
    dkv_own, dkv_core, query_grad = on_core(
        backward_near_kernel,
        place,
        sides + [kv_own, kv_core, query_grad_t],
        (pair, pair, ((rows, width), bf16)),
        (turned,),
        cost=NEAR_COST,
    )
    dkv_core = blk_swapped(dkv_core, 1)
    dqkv, normed_own, *normed_parts = on_core(
        gather_back_kernel,
        place,
        [dkv_own, dkv_core, dkv_from_y, query_grad, qkv_whole],
        [((rows, wide + width), bf16), slab] + slabs,
        cost=BRIEF_COST,
    )
    normed_returned = slots_returned(normed_parts)

    columns = wide + width
    near_pairs = [
        ([xhat1_low], False, dqkv, 0, 0),
        (branch_slots, True, mixed_low, wide - 512, 512),
    ]
    sums = (hidden_sum, seed_sum)
    if paired():
        near_sent, near_kept = grads_sent(near_pairs, columns, depth, sums)
        near_got = cube_swapped(near_sent, 1, 1).astype(f32)
        near_held = near_kept + near_got
        near_next = near_held[2:].astype(bf16)
        near_got = cube_swapped(near_next, 4, 2).astype(f32)
        near_held = near_held[:2] + near_got
        near_last = near_held[1].astype(bf16)
        near_got = cube_swapped(near_last, 2, 4).astype(f32)
        near_total = near_held[0] + near_got
        wide_got = cube_swapped(after(wide_sent, near_sent), 2, 4).astype(f32)
        wide_total = wide_held[0] + wide_got
    else:
        near_total = grads_scattered(near_pairs, columns, owners, sums)
        wide_total = grads_scattered(wide_pairs, units_grad, owners, ())
        near_last = near_total

    normed_back = normed_own
    for item in normed_returned:
        normed_back = normed_back + after(item, near_last).astype(f32)
    outside = outside_own
    for item in shared:
        outside = outside + after(item, near_last)[:part].astype(f32)
    xhat1, rstd1 = normalized(tokens.astype(f32))
    input_grad = (middle_back + norm_back(normed_back * gain1, xhat1, rstd1)).astype(bf16)
    result = (middle + (outside + down_bias_all)).astype(bf16)

    qkv_total = near_total[:depth, :wide]
    output_total = near_total[:depth, wide:].T
    qkv_sums, hidden_sums = near_total[depth, :wide], near_total[depth + 1, :units]
    branch_sums, seed_sums = near_total[depth + 2, :depth], near_total[depth + 3, :depth]
    up_total, down_total = wide_total[:, :units], wide_total[:, units:].T
    own_gain1, own_shift1 = first_gain.astype(f32), first_shift.astype(f32)
    own_gain2, own_shift2 = second_gain.astype(f32), second_shift.astype(f32)
    qkv_weight_grad = own_gain1[:, None] * qkv_total + own_shift1[:, None] * qkv_sums[None]
    up_weight_grad = own_gain2[:, None] * up_total + own_shift2[:, None] * hidden_sums[None]
    qkv_wide, up_wide = qkv_own.astype(f32), up_weight.astype(f32)
    terms = jnp.concatenate(
        [
            jnp.sum(qkv_wide * qkv_total, axis=1),
            jnp.sum(qkv_wide * qkv_sums[None], axis=1),
            jnp.sum(up_wide * up_total, axis=1),
            jnp.sum(up_wide * hidden_sums[None], axis=1),
            qkv_sums[2 * width :],
            qkv_sums[width + 64 : 2 * width],
            qkv_sums[width : width + 64],
            hidden_sums,
        ]
    )
    all_terms = jnp.stack(slots_of(terms))
    share = depth // groups
    added = jnp.sum(all_terms[:, : 4 * depth], axis=0).reshape(4, depth)
    added = lax.dynamic_slice_in_dim(added, uly * share, share, axis=1)
    rank = cube_index() * groups + uly

    def owned(start, length, count):
        at = rank * count
        source = (uly - at // length) % groups
        return lax.dynamic_slice(all_terms, (source, start + at % length), (1, count))[0]

    query_bias_grad = owned(4 * depth, width, share)
    value_bias_grad = owned(4 * depth + width, width, share)
    up_bias_grad = owned(4 * depth + 2 * width, units, up_bias.shape[0] // groups)
    output_bias_grad = lax.dynamic_slice_in_dim(branch_sums, uly * share, share)
    down_bias_grad = lax.dynamic_slice_in_dim(seed_sums, uly * share, share)
    value_weight_grad = jnp.concatenate(
        [qkv_weight_grad[:, width + 64 : 2 * width], qkv_weight_grad[:, width : width + 64]], axis=1
    )
    return (
        result,
        input_grad,
        qkv_weight_grad[:, 2 * width :],
        qkv_weight_grad[:, :width],
        value_weight_grad,
        output_total,
        up_weight_grad,
        down_total,
        query_bias_grad,
        value_bias_grad,
        output_bias_grad,
        up_bias_grad,
        down_bias_grad,
        added[0],
        added[1],
        added[2],
        added[3],
    )


def solution(mesh):
    rows = P(("fsdp", "blk", "uly"), None)
    tall, flat = P(("fsdp", "blk"), "uly"), P("uly", ("fsdp", "blk"))
    vector, vector_out = P(("fsdp", "blk")), P(("fsdp", "blk", "uly"))
    return jax.shard_map(
        shards,
        mesh=mesh,
        in_specs=(rows, tall, tall, tall, flat, tall, flat) + (vector,) * 9 + (rows,),
        out_specs=(rows, rows, tall, tall, tall, flat, tall, flat) + (vector_out,) * 9,
        check_vma=False,
    )
```

```python
import jax
import jax.numpy as jnp
from jax import lax
from jax.experimental import pallas as pl
from jax.experimental.pallas import tpu as pltpu
from jax.sharding import PartitionSpec as P

HEAD_DIM = 64
CUBE = ("fsdp", "blk")
VEC_ROWS = 16
VMEM_LIMIT = 56 * 1024 * 1024
KERNEL_COST = 30_000_000_000

KEY_GROUP, KEY_HALF = (0, 0, 1), (0, 1, 0)
VALUE_GROUP, VALUE_HALF = (2, 2, 1), (0, 1, 1)


def dot_plain(left, right):
    return jnp.dot(left, right, preferred_element_type=jnp.float32)


def dot_rows(left, right):
    return lax.dot_general(
        left, right, (((0,), (0,)), ((), ())), preferred_element_type=jnp.float32
    )


def dot_cols(left, right):
    return lax.dot_general(
        left, right, (((1,), (1,)), ((), ())), preferred_element_type=jnp.float32
    )


def passed_along(array, by):
    peers = lax.axis_size("uly")
    return lax.ppermute(array, "uly", [(i, (i + by) % peers) for i in range(peers)])


def slots_of(array):
    return [array] + [passed_along(array, by) for by in range(1, lax.axis_size("uly"))]


def blk_swapped(array, flip):
    peers = lax.axis_size("blk")
    return lax.ppermute(array, "blk", [(i, i ^ flip) for i in range(peers)])


def cube_swapped(array, even, odd):
    peers = lax.axis_size(CUBE)
    pairs = [(i, i ^ (odd if i & 1 else even)) for i in range(peers)]
    return lax.ppermute(array, CUBE, pairs)


def cube_index():
    return lax.axis_index("fsdp") * lax.axis_size("blk") + lax.axis_index("blk")


def place_kernel(cuts, index_ref, own, first, second, other, *outs):
    me = index_ref[0]
    odd = me & 1
    near, far = jnp.where(odd == 1, 2, 4), jnp.where(odd == 1, 4, 2)
    pieces = [
        (own, 0),
        (first, near),
        (second.at[0], far),
        (second.at[1], 6),
        (other.at[0], 1),
        (other.at[1], far ^ 1),
        (other.at[2], near ^ 1),
        (other.at[3], 7),
    ]
    for piece, flip in pieces:
        for out, (row, rows, column, columns) in zip(outs, cuts):
            out[me ^ flip] = piece[row : row + rows, column : column + columns]


def paired():
    return lax.axis_size("fsdp") == 2 and lax.axis_size("blk") == 4


def after(array, *others):
    return lax.optimization_barrier((array,) + others)[0]


def cube_placed(cuts, pieces):
    index = cube_index().astype(jnp.int32).reshape(1)
    outs = [((8, rows, columns), pieces[0].dtype) for _, rows, _, columns in cuts]
    return on_core(lambda *refs: place_kernel(cuts, *refs), index, pieces, outs)


def cube_flips(me):
    odd = me & 1
    return jnp.where(odd == 1, 2, 4), jnp.where(odd == 1, 4, 2)


def grads_kernel(pairs, spread, index, *refs):
    ins, (sent, kept), (whole, extra) = refs[:-4], refs[-4:-2], refs[-2:]
    at = 0
    for count, flipped, column, columns in pairs:
        left, right = stacked_slots(ins[at : at + count]), ins[at + count][...]
        at += count + 1
        whole[:, column : column + columns] = dot_plain(left.T, right.T if flipped else right)
    rows = kept.shape[1]
    model, wide = whole.shape
    depth = model // 8
    if spread:
        hidden_sum, seed_sum, branch = ins[at], ins[at + 1], ins[at + 2]
        half = hidden_sum.shape[1] // 2
        right_sum = jnp.sum(right.astype(jnp.float32), axis=0, keepdims=True)
        branch_sum = jnp.sum(branch[...].astype(jnp.float32), axis=0, keepdims=True)
        whole_rows = jnp.concatenate([right_sum, jnp.zeros((7, wide), jnp.float32)], axis=0)
        part_rows = jnp.concatenate(
            [branch_sum, seed_sum[...], jnp.zeros((6, model), jnp.float32)], axis=0
        )
        for block in range(8):
            turned = part_rows if block == 0 else pltpu.roll(part_rows, model - depth * block, 1)
            extra[block, 0:8] = whole_rows
            extra[block, 1:2, 0:half] = hidden_sum[:, :half]
            extra[block, 2:3, 0:half] = hidden_sum[:, half:]
            extra[block, 8:16] = turned[:, :wide]
    me = index[0]
    near, far = cube_flips(me)
    for slot, flip in enumerate((0, near, far, 6)):
        block = me ^ flip ^ 1
        sent[slot, 0:depth] = whole[pl.ds(pl.multiple_of(block * depth, 8), depth)].astype(sent.dtype)
        if spread:
            sent[slot, depth:rows] = extra[block].astype(sent.dtype)
    for slot, flip in enumerate((0, far, near, 6)):
        block = me ^ flip
        kept[slot, 0:depth] = whole[pl.ds(pl.multiple_of(block * depth, 8), depth)]
        if spread:
            kept[slot, depth:rows] = extra[block]


def grads_sent(pairs, columns, depth):
    plan = [
        (len(left), flipped, column, right.shape[0 if flipped else 1])
        for left, flipped, right, column in pairs
    ]
    operands = [item for left, _, right, _ in pairs for item in [*left, right]]
    index = cube_index().astype(jnp.int32).reshape(1)
    return on_core(
        lambda *refs: grads_kernel(plan, False, *refs),
        index,
        operands,
        [((4, depth, columns), jnp.bfloat16), ((4, depth, columns), jnp.float32)],
        [((8 * depth, columns), jnp.float32), ((8, VEC_ROWS, columns), jnp.float32)],
    )


def grads_scattered(pairs, columns, owners, sums):
    blocks = []
    for left, flipped, right, _ in pairs:
        right = right.T if flipped else right
        blocks.append(dot_rows(stacked_slots(left), right))
    model = blocks[0].shape[0]
    depth = model // owners
    blocks = jnp.concatenate(blocks, axis=1).reshape(owners, depth, columns)
    if sums:
        hidden_sum, seed_sum, branch = sums
        half = hidden_sum.shape[1] // 2
        branch_sum = jnp.sum(branch.astype(jnp.float32), axis=0)
        extra = jnp.zeros((owners, VEC_ROWS, columns), jnp.float32)
        extra = extra.at[:, 0].set(jnp.sum(pairs[0][2].astype(jnp.float32), axis=0)[None])
        extra = extra.at[:, 1, :half].set(hidden_sum[:, :half])
        extra = extra.at[:, 2, :half].set(hidden_sum[:, half:])
        extra = extra.at[:, 8, :depth].set(branch_sum.reshape(owners, depth))
        extra = extra.at[:, 9, :depth].set(seed_sum.reshape(owners, depth))
        blocks = jnp.concatenate([blocks, extra], axis=1)
    return lax.psum_scatter(blocks, CUBE, scatter_dimension=0, tiled=False)


def half_padded(part, half):
    zero = jnp.zeros_like(part)
    return jnp.concatenate([part, zero] if half == 0 else [zero, part], axis=0)


def heads_across(array, halves):
    turned = array.T
    return [
        half_padded(turned[h * HEAD_DIM : (h + 1) * HEAD_DIM], halves[h])
        for h in range(len(halves))
    ]


def group_of(ref, group):
    return ref[:, group * 128 : (group + 1) * 128]


def slot_places(index, uly, slot_rows):
    return ((uly - index // slot_rows) & 3) * slot_rows + index % slot_rows


def causal(rows, uly):
    keys = lax.broadcasted_iota(jnp.int32, (rows, rows), 0)
    queries = lax.broadcasted_iota(jnp.int32, (rows, rows), 1)
    slot_rows = rows // 4
    return slot_places(keys, uly, slot_rows) <= slot_places(queries, uly, slot_rows)


def forward_block(query_t, kv_ref, top, total, mixed, allowed):
    turned = kv_ref[...].T
    for h in range(3):
        scores = dot_plain(group_of(kv_ref, KEY_GROUP[h]), query_t[h])
        if allowed is not None:
            scores = jnp.where(allowed, scores, -1e30)
        block_top = jnp.max(scores, axis=0, keepdims=True)
        low = VALUE_GROUP[h] * 128 + VALUE_HALF[h] * HEAD_DIM
        value_t = turned[low : low + HEAD_DIM]
        own = pl.ds(h * HEAD_DIM, HEAD_DIM)
        if allowed is not None:
            weights = jnp.exp(scores - block_top)
            top[h : h + 1] = block_top
            total[h : h + 1] = jnp.sum(weights, axis=0, keepdims=True)
            mixed[own] = dot_plain(value_t, weights.astype(jnp.bfloat16))
        else:
            old_top = top[h : h + 1]
            new_top = jnp.maximum(old_top, block_top)
            fade = jnp.exp(old_top - new_top)
            weights = jnp.exp(scores - new_top)
            top[h : h + 1] = new_top
            total[h : h + 1] = total[h : h + 1] * fade + jnp.sum(weights, axis=0, keepdims=True)
            mixed[own] = mixed[own] * fade + dot_plain(value_t, weights.astype(jnp.bfloat16))


def forward_near_kernel(place, query, kv_own, kv_core, top, total, mixed):
    blk, uly = place[0], place[1]
    query_t = heads_across(query[...], KEY_HALF)
    top[...] = jnp.zeros_like(top)
    total[...] = jnp.ones_like(total)
    forward_block(query_t, kv_own, top, total, mixed, causal(query.shape[0], uly))

    @pl.when((blk & 1) == 1)
    def _():
        forward_block(query_t, kv_core, top, total, mixed, None)


def forward_far_kernel(
    place, query, kv_y, kv_both, top_in, total_in, mixed_in, out, mixed, lse, top, total
):
    blk = place[0]
    top[...] = top_in[...]
    total[...] = total_in[...]
    mixed[...] = mixed_in[...]

    @pl.when((blk & 2) == 2)
    def _():
        query_t = heads_across(query[...], KEY_HALF)
        forward_block(query_t, kv_y, top, total, mixed, None)
        forward_block(query_t, kv_both, top, total, mixed, None)

    for h in range(3):
        own = pl.ds(h * HEAD_DIM, HEAD_DIM)
        mixed[own] = mixed[own] / total[h : h + 1]
    lse[...] = top[...] + jnp.log(total[...])
    out[...] = mixed[...].astype(jnp.bfloat16)


def backward_block(sides, kv_ref, dkv_ref, query_grad_t, allowed):
    query_t, grad_t, query_m, grad_m, delta, lse = sides
    turned = kv_ref[...].T
    columns = [None, None, None]

    def add(group, term):
        columns[group] = term if columns[group] is None else columns[group] + term

    for h in range(3):
        scores = dot_plain(group_of(kv_ref, KEY_GROUP[h]), query_t[h])
        probs = jnp.exp(scores - lse[h : h + 1])
        if allowed is not None:
            probs = jnp.where(allowed, probs, 0.0)
        prob_grad = dot_plain(group_of(kv_ref, VALUE_GROUP[h]), grad_t[h])
        score_grad = (probs * (prob_grad - delta[h])).astype(jnp.bfloat16)
        add(VALUE_GROUP[h], dot_plain(probs.astype(jnp.bfloat16), grad_m[h]))
        add(KEY_GROUP[h], dot_plain(score_grad, query_m[h]))
        low = KEY_GROUP[h] * 128 + KEY_HALF[h] * HEAD_DIM
        own = pl.ds(h * HEAD_DIM, HEAD_DIM)
        query_grad_t[own] += dot_plain(turned[low : low + HEAD_DIM], score_grad)
    for group in range(3):
        dkv_ref[:, group * 128 : (group + 1) * 128] = columns[group].astype(dkv_ref.dtype)


def backward_sides(query, grads, mixed, lse):
    query_t = heads_across(query[...], KEY_HALF)
    grad_all = jnp.concatenate([ref[...] for ref in grads], axis=1)
    grad_t = [
        half_padded(grad_all[h * HEAD_DIM : (h + 1) * HEAD_DIM], VALUE_HALF[h]) for h in range(3)
    ]
    product = grad_all.astype(jnp.float32) * mixed[...]
    delta = [
        jnp.sum(product[h * HEAD_DIM : (h + 1) * HEAD_DIM], axis=0, keepdims=True)
        for h in range(3)
    ]
    query_m = [item.T for item in query_t]
    grad_m = [item.T for item in grad_t]
    return query_t, grad_t, query_m, grad_m, delta, lse[...]


def backward_both_kernel(place, query, g0, g1, g2, g3, mixed, lse, kv_both, dkv_both, query_grad_t):
    query_grad_t[...] = jnp.zeros_like(query_grad_t)

    @pl.when((place[0] & 2) == 2)
    def _():
        sides = backward_sides(query, (g0, g1, g2, g3), mixed, lse)
        backward_block(sides, kv_both, dkv_both, query_grad_t, None)

    @pl.when((place[0] & 2) == 0)
    def _():
        dkv_both[...] = jnp.zeros_like(dkv_both)


def backward_y_kernel(
    place, query, g0, g1, g2, g3, mixed, lse, kv_y, dkv_core, grad_t_in, dkv_y, total, part
):
    total[...] = grad_t_in[...]

    @pl.when((place[0] & 2) == 2)
    def _():
        sides = backward_sides(query, (g0, g1, g2, g3), mixed, lse)
        backward_block(sides, kv_y, part, total, None)
        dkv_y[...] = (part[...] + dkv_core[...].astype(jnp.float32)).astype(dkv_y.dtype)

    @pl.when((place[0] & 2) == 0)
    def _():
        dkv_y[...] = jnp.zeros_like(dkv_y)


def backward_near_kernel(
    place,
    query,
    g0,
    g1,
    g2,
    g3,
    mixed,
    lse,
    kv_own,
    kv_core,
    grad_t_in,
    dkv_own,
    dkv_core,
    query_grad,
    total,
):
    blk, uly = place[0], place[1]
    total[...] = grad_t_in[...]
    sides = backward_sides(query, (g0, g1, g2, g3), mixed, lse)

    @pl.when((blk & 1) == 1)
    def _():
        backward_block(sides, kv_core, dkv_core, total, None)

    @pl.when((blk & 1) == 0)
    def _():
        dkv_core[...] = jnp.zeros_like(dkv_core)

    backward_block(sides, kv_own, dkv_own, total, causal(query.shape[0], uly))
    query_grad[...] = (total[...] * HEAD_DIM**-0.5).T.astype(jnp.bfloat16)


def on_core(kernel, place, operands, outs, scratch=()):
    vmem = pl.BlockSpec(memory_space=pltpu.VMEM)
    return pl.pallas_call(
        kernel,
        out_shape=[jax.ShapeDtypeStruct(shape, dtype) for shape, dtype in outs],
        in_specs=[pl.BlockSpec(memory_space=pltpu.SMEM)] + [vmem] * len(operands),
        out_specs=[vmem] * len(outs),
        scratch_shapes=[pltpu.VMEM(shape, dtype) for shape, dtype in scratch],
        compiler_params=pltpu.CompilerParams(vmem_limit_bytes=VMEM_LIMIT),
        cost_estimate=pl.CostEstimate(flops=KERNEL_COST, transcendentals=0, bytes_accessed=0),
    )(place, *operands)


def normalized(rows):
    centre = rows - jnp.mean(rows, axis=-1, keepdims=True)
    rstd = lax.rsqrt(jnp.mean(centre * centre, axis=-1, keepdims=True) + 1e-05)
    return centre * rstd, rstd


def norm_back(grad, xhat, rstd):
    return rstd * (
        grad
        - jnp.mean(grad, axis=-1, keepdims=True)
        - xhat * jnp.mean(grad * xhat, axis=-1, keepdims=True)
    )


def stacked_slots(refs):
    rows = refs[0].shape[0]
    return jnp.concatenate([ref[:rows] for ref in refs], axis=0)


def project_kernel(place, t0, t1, t2, t3, weight, named, bias, query, kv, xhat_low):
    rows = stacked_slots((t0, t1, t2, t3)).astype(jnp.float32)
    xhat, _ = normalized(rows)
    xhat_low[...] = xhat.astype(jnp.bfloat16)
    normed = (xhat * named[0:1] + named[1:2]).astype(jnp.bfloat16)
    qkv = dot_plain(normed, weight[...]) + bias[...]
    wide = kv.shape[1]
    kv[...] = qkv[:, :wide].astype(jnp.bfloat16)
    query[...] = qkv[:, wide:].astype(jnp.bfloat16) * jnp.asarray(HEAD_DIM**-0.5, jnp.bfloat16)


GELU_A, GELU_B = 0.7978845608028654, 0.044715


def middle_kernel(
    place,
    m0,
    m1,
    m2,
    m3,
    t0,
    t1,
    t2,
    t3,
    c0,
    c1,
    c2,
    c3,
    output_t,
    up,
    down_t,
    named,
    up_bias,
    middle_own,
    xhat_low,
    mixed_own,
    active_low,
    hidden_back_low,
    part_own,
    *parts,
):
    slot = t0.shape[0]
    mixed_t = jnp.concatenate(
        [m0[...]]
        + [
            jnp.concatenate([ref[:, (4 - by) * slot :], ref[:, : (4 - by) * slot]], axis=1)
            for by, ref in ((1, m1), (2, m2), (3, m3))
        ],
        axis=0,
    )
    mixed_own[...] = mixed_t[:, :slot]
    branch = dot_plain(output_t[...], mixed_t).T
    middle = stacked_slots((t0, t1, t2, t3)).astype(jnp.float32) + (branch + named[0:1])
    middle_own[...] = middle[:slot]
    xhat, _ = normalized(middle)
    xhat_low[...] = xhat.astype(jnp.bfloat16)
    second = (xhat * named[1:2] + named[2:3]).astype(jnp.bfloat16)
    hidden = dot_plain(second, up[...]) + up_bias[...]
    active_grad = dot_plain(stacked_slots((c0, c1, c2, c3)), down_t[...])
    square = hidden * hidden
    bent = jnp.tanh(GELU_A * hidden * (1.0 + GELU_B * square))
    active_low[...] = (0.5 * hidden * (1.0 + bent)).astype(jnp.bfloat16)
    slope = 0.5 * (1.0 + bent) + (0.5 * GELU_A) * hidden * (1.0 - bent * bent) * (
        1.0 + (3.0 * GELU_B) * square
    )
    hidden_back = (active_grad * slope).astype(jnp.bfloat16)
    hidden_back_low[...] = hidden_back
    second_back = dot_cols(hidden_back, up[...])
    part_own[...] = second_back[:slot]
    for by in range(1, 4):
        parts[by - 1][...] = second_back[by * slot : (by + 1) * slot].astype(jnp.bfloat16)


def outside_kernel(
    place, active, down_t, hidden_back, c0, c1, c2, c3, hidden_sum, seed_sum, part_own, *parts
):
    slot = part_own.shape[0]
    outside = dot_cols(active[...], down_t[...])
    part_own[...] = outside[:slot]
    for by in range(1, 4):
        parts[by - 1][...] = outside[by * slot : (by + 1) * slot].astype(jnp.bfloat16)
    hidden_sum[...] = jnp.sum(hidden_back[...].astype(jnp.float32), axis=0, keepdims=True)
    seed = stacked_slots((c0, c1, c2, c3)).astype(jnp.float32)
    seed_sum[...] = jnp.sum(seed, axis=0, keepdims=True)


def branch_kernel(
    place,
    part_own,
    r1,
    r2,
    r3,
    middle,
    seed,
    gain,
    output_t,
    middle_back,
    branch_back,
    *mixed_back_t,
):
    second_back = part_own[...]
    for ref in (r1, r2, r3):
        second_back = second_back + ref[...].astype(jnp.float32)
    xhat, rstd = normalized(middle[...])
    grad = seed[...].astype(jnp.float32) + norm_back(second_back * gain[...], xhat, rstd)
    middle_back[...] = grad
    low = grad.astype(jnp.bfloat16)
    branch_back[...] = low
    turned = dot_plain(low, output_t[...]).T.astype(jnp.bfloat16)
    width = mixed_back_t[0].shape[0]
    for by in range(4):
        mixed_back_t[by][...] = turned[by * width : (by + 1) * width]


def gather_back_kernel(place, own, core, far, query, weight, o1, o2, o3, dqkv, part_own, *parts):
    wide = own.shape[1]
    width = query.shape[1]
    total = own[...].astype(jnp.float32) + core[...].astype(jnp.float32)
    kv_grad = (total + far[...].astype(jnp.float32)).astype(jnp.bfloat16)
    dqkv[:, :wide] = kv_grad
    dqkv[:, wide : wide + width] = query[...]
    spare = dqkv.shape[1] - wide - width
    dqkv[:, wide + width :] = jnp.zeros((query.shape[0], spare), jnp.bfloat16)
    normed_back = dot_cols(dqkv[:, : wide + width], weight[...])
    slot = part_own.shape[0]
    part_own[...] = normed_back[:slot]
    for by, outside in ((1, o1), (2, o2), (3, o3)):
        parts[by - 1][:slot] = normed_back[by * slot : (by + 1) * slot].astype(jnp.bfloat16)
        parts[by - 1][slot:] = outside[...]


def last_kernel(index, *refs):
    ins, (xhat, hidden_sum, seed_sum, branch) = refs[:8], refs[8:12]
    part_own, p1, p2, p3, sent, kept, dqkv, whole, extra = refs[12:]
    gather_back_kernel(index, *ins, dqkv, part_own, p1, p2, p3)
    plan = [(1, False, 0, dqkv.shape[1])]
    grads_kernel(
        plan, True, index, xhat, dqkv, hidden_sum, seed_sum, branch, sent, kept, whole, extra
    )


def slots_returned(parts):
    return [passed_along(parts[by - 1], -by) for by in range(1, 4)]


def shards(
    tokens,
    query_weight,
    key_weight,
    value_weight,
    output_weight,
    up_weight,
    down_weight,
    query_bias,
    value_bias,
    output_bias,
    up_bias,
    down_bias,
    first_gain,
    first_shift,
    second_gain,
    second_shift,
    cotangent,
):
    bf16, f32 = jnp.bfloat16, jnp.float32
    uly, blk = lax.axis_index("uly"), lax.axis_index("blk")
    groups = lax.axis_size("uly")
    owners = lax.axis_size(CUBE)
    part = tokens.shape[0]
    rows = groups * part
    depth, width = query_weight.shape
    units = up_weight.shape[1]
    model = depth * owners
    place = jnp.stack([blk, uly]).astype(jnp.int32)

    qkv_own = jnp.concatenate(
        [key_weight, value_weight[:, 128:], value_weight[:, :128], query_weight], axis=1
    )
    vectors = [
        query_bias,
        value_bias,
        output_bias,
        down_bias,
        first_gain,
        first_shift,
        second_gain,
        second_shift,
    ]
    up_rows = up_bias.shape[0] // depth
    named = len(vectors) + up_rows
    wide = 3 * width
    vector_rows = jnp.concatenate(
        [vector.reshape(1, depth) for vector in vectors] + [up_bias.reshape(up_rows, depth)]
    )
    vector_rows = jnp.pad(vector_rows, ((0, VEC_ROWS - named), (0, wide - depth)))
    chunk = depth // groups
    output_own = output_weight.T
    output_rows = jnp.concatenate(
        [output_own[at * chunk : (at + 1) * chunk] for at in range(groups)], axis=1
    )
    spare = -(part + chunk) % 16
    token_sent = jnp.concatenate([tokens, jnp.pad(output_rows, ((0, spare), (0, 0)))], axis=0)
    token_slots = [tokens, passed_along(token_sent, 1), None, None]
    qkv_sent = jnp.concatenate([qkv_own, vector_rows], axis=0)
    qkv_cuts = [(0, depth, 0, wide), (depth, VEC_ROWS, 0, wide)]
    if paired():
        qkv_sent = after(qkv_sent, token_slots[1])
        token_later = after(token_sent, token_slots[1])
        token_slots[3] = passed_along(token_later, 3)
        token_slots[2] = passed_along(token_later, 2)
        qkv_first = after(cube_swapped(qkv_sent, 4, 2), token_slots[3])
        qkv_second = cube_swapped(jnp.stack([qkv_sent, qkv_first]), 2, 4)
        qkv_second = after(qkv_second, token_slots[2])
        qkv_other = cube_swapped(
            jnp.concatenate([qkv_sent[None], qkv_first[None], qkv_second]), 1, 1
        )
        qkv_whole, vector_whole = cube_placed(
            qkv_cuts, (qkv_sent, qkv_first, qkv_second, qkv_other)
        )
    else:
        token_slots = [tokens] + slots_of(token_sent)[1:]
        whole = lax.all_gather(qkv_sent, CUBE, axis=0, tiled=False)
        qkv_whole, vector_whole = whole[:, :depth], whole[:, depth:]
    qkv_whole = qkv_whole.reshape(model, wide)
    vector_whole = vector_whole[:, :named, :depth].astype(f32)
    up_bias_whole = vector_whole[:, len(vectors) :].reshape(-1)
    named = vector_whole.transpose(1, 0, 2).reshape(named, model)
    query_bias_own = lax.dynamic_slice_in_dim(named[0], uly * width, width)
    value_bias_own = lax.dynamic_slice_in_dim(named[1], uly * width, width)
    up_bias_own = lax.dynamic_slice_in_dim(up_bias_whole, uly * units, units)
    output_bias_all, down_bias_all = named[2], named[3]
    gain1, gain2, shift2 = named[4], named[6], named[7]

    qkv_bias = jnp.concatenate(
        [jnp.zeros((width,), f32), value_bias_own[128:], value_bias_own[:128], query_bias_own]
    )

    inner = groups * width
    rest_cuts = [
        (0, depth, 0, inner),
        (0, depth, inner, units),
        (0, depth, inner + units, units),
    ]
    cotangent_later = after(cotangent, *token_slots[1:])
    cotangent_slots = [cotangent] + [passed_along(cotangent_later, by) for by in range(1, groups)]
    output_slots = [output_own] + [
        jnp.concatenate(
            [item[part : part + chunk, at * width : (at + 1) * width] for at in range(groups)], axis=0
        )
        for item in token_slots[1:]
    ]
    rest_own = jnp.concatenate(output_slots + [up_weight, down_weight.T], axis=1)
    if paired():
        rest_own = after(rest_own, qkv_second)
        rest_first = cube_swapped(rest_own, 4, 2)

    qkv_ready = after(qkv_whole, cotangent_slots[1])
    query, kv_own, xhat1_low = on_core(
        project_kernel,
        place,
        token_slots + [qkv_ready, named[4:6], qkv_bias[None]],
        [((rows, width), bf16), ((rows, 2 * width), bf16), ((rows, model), bf16)],
    )
    kv_y = blk_swapped(kv_own, 2)
    kv_core = blk_swapped(kv_own, 1)
    stats = ((8, rows), f32)
    turned = ((width, rows), f32)
    top, total, mixed_t = on_core(
        forward_near_kernel, place, (query, kv_own, kv_core), (stats, stats, turned)
    )
    kv_both = blk_swapped(after(kv_y, top, *cotangent_slots[2:]), 1)
    if paired():
        rest_second = cube_swapped(after(jnp.stack([rest_own, rest_first]), kv_own), 2, 4)
        rest_second = after(rest_second, kv_both)
        rest_held = jnp.concatenate([rest_own[None], rest_first[None], rest_second])
        rest_other = cube_swapped(rest_held, 1, 1)
        kv_both = after(kv_both, rest_held)
    mixed_low, mixed_t, lse = on_core(
        forward_far_kernel,
        place,
        (query, kv_y, kv_both, top, total, mixed_t),
        (((width, rows), bf16), turned, stats),
        (stats, stats),
    )
    mixed_slots = slots_of(mixed_low)
    if paired():
        rest_other = after(rest_other, mixed_low)
        output_t, up_whole, down_t = cube_placed(
            rest_cuts, (rest_own, rest_first, rest_second, rest_other)
        )
    else:
        whole = lax.all_gather(rest_own, CUBE, axis=0, tiled=False)
        output_t, up_whole, down_t = [whole[:, :, c : c + n] for _, _, c, n in rest_cuts]
    output_t = output_t.reshape(model, inner)
    up_whole = up_whole.reshape(model, units)
    down_t = down_t.reshape(model, units)

    slab = ((part, model), f32)
    slabs = [((part, model), bf16)] * (groups - 1)
    wide_low = ((rows, model), bf16)
    units_low = ((rows, units), bf16)
    middle, xhat2_low, mixed_own, active, hidden_back, second_own, *second_parts = on_core(
        middle_kernel,
        place,
        mixed_slots
        + token_slots
        + cotangent_slots
        + [output_t, up_whole, down_t, jnp.stack([output_bias_all, gain2, shift2]), up_bias_own[None]],
        [slab, wide_low, ((inner, part), bf16), units_low, units_low, slab] + slabs,
    )
    second_returned = slots_returned(second_parts)
    hidden_sum, seed_sum, outside_own, *outside_parts = on_core(
        outside_kernel,
        place,
        [active, down_t, hidden_back] + cotangent_slots,
        [((1, units), f32), ((1, model), f32), slab] + slabs,
    )
    second_own = after(second_own, outside_own)

    middle_back, branch_back, *mixed_back_t = on_core(
        branch_kernel,
        place,
        [second_own] + second_returned + [middle, cotangent, gain2[None], output_t],
        [slab, ((part, model), bf16)] + [((width, part), bf16)] * groups,
    )
    grad_slots = [mixed_back_t[0]] + [
        passed_along(mixed_back_t[by], -by) for by in range(groups - 1, 0, -1)
    ]
    wide_pairs = [
        ([xhat2_low], False, hidden_back, 0),
        (cotangent_slots, False, active, units),
        ([branch_back], True, mixed_own, 2 * units),
    ]
    wide_columns = 2 * units + inner
    if paired():
        wide_sent, wide_kept = grads_sent(wide_pairs, wide_columns, depth)
        wide_got = cube_swapped(wide_sent, 1, 1)
        grad_slots[1] = after(grad_slots[1], wide_sent)
    sides = [query] + grad_slots + [mixed_t, lse]
    pair = ((rows, 2 * width), bf16)
    dkv_both, query_grad_t = on_core(
        backward_both_kernel, place, sides + [kv_both], (pair, turned)
    )
    if paired():
        wide_held = wide_kept + after(wide_got, dkv_both).astype(f32)
        wide_next = wide_held[2:].astype(bf16)
        wide_got = cube_swapped(wide_next, 4, 2)
    dkv_y, query_grad_t = on_core(
        backward_y_kernel,
        place,
        sides + [kv_y, blk_swapped(dkv_both, 1), query_grad_t],
        (pair, turned),
        [((rows, 2 * width), f32)],
    )
    dkv_from_y = blk_swapped(dkv_y, 2)
    kv_last = after(kv_core, wide_next) if paired() else kv_core
    dkv_own, dkv_core, query_grad = on_core(
        backward_near_kernel,
        place,
        sides + [kv_own, kv_last, query_grad_t],
        (pair, pair, ((rows, width), bf16)),
        (turned,),
    )
    dkv_core = blk_swapped(dkv_core, 1)
    columns = -(-wide // 128) * 128
    back_operands = [dkv_own, dkv_core, dkv_from_y, query_grad, qkv_whole] + outside_parts
    back_outs = [slab] + [((2 * part, model), bf16)] * 3
    sums = (hidden_sum, seed_sum, branch_back)
    dqkv_kind = ((rows, columns), bf16)
    if paired():
        kinds = [((4, depth + VEC_ROWS, columns), kind) for kind in (bf16, f32)]
        normed_own, *normed_parts, near_sent, near_kept = on_core(
            last_kernel,
            cube_index().astype(jnp.int32).reshape(1),
            back_operands + [xhat1_low] + list(sums),
            back_outs + kinds,
            [dqkv_kind, ((model, columns), f32), ((8, VEC_ROWS, columns), f32)],
        )
    else:
        dqkv, normed_own, *normed_parts = on_core(
            gather_back_kernel, place, back_operands, [dqkv_kind] + back_outs
        )
    normed_returned = slots_returned(normed_parts)

    if paired():
        near_got = cube_swapped(near_sent, 1, 1).astype(f32)
        wide_held = wide_held[:2] + after(wide_got, near_sent).astype(f32)
        wide_last = wide_held[1].astype(bf16)
        near_held = near_kept + near_got
        near_next = near_held[2:].astype(bf16)
        near_got = cube_swapped(near_next, 4, 2).astype(f32)
        near_held = near_held[:2] + near_got
        near_got = cube_swapped(near_held[1].astype(bf16), 2, 4).astype(f32)
        near_total = near_held[0] + near_got
        wide_got = cube_swapped(wide_last, 2, 4).astype(f32)
        wide_total = wide_held[0] + wide_got
    else:
        near_total = grads_scattered([([xhat1_low], False, dqkv, 0)], columns, owners, sums)
        wide_total = grads_scattered(wide_pairs, wide_columns, owners, ())

    half = units // 2
    qkv_total, qkv_sums = near_total[:depth, :wide], near_total[depth, :wide]
    hidden_sums = near_total[depth + 1 : depth + 3, :half].reshape(-1)
    branch_sums, seed_sums = near_total[depth + 8, :depth], near_total[depth + 9, :depth]
    up_total, down_total = wide_total[:, :units], wide_total[:, units : 2 * units].T
    own_gain1, own_shift1 = first_gain.astype(f32), first_shift.astype(f32)
    own_gain2, own_shift2 = second_gain.astype(f32), second_shift.astype(f32)
    qkv_weight_grad = own_gain1[:, None] * qkv_total + own_shift1[:, None] * qkv_sums[None]
    up_weight_grad = own_gain2[:, None] * up_total + own_shift2[:, None] * hidden_sums[None]
    qkv_wide, up_wide = qkv_own.astype(f32), up_weight.astype(f32)
    terms = jnp.concatenate(
        [
            jnp.sum(qkv_wide * qkv_total, axis=1),
            jnp.sum(qkv_wide * qkv_sums[None], axis=1),
            jnp.sum(up_wide * up_total, axis=1),
            jnp.sum(up_wide * hidden_sums[None], axis=1),
            branch_sums,
            qkv_sums[2 * width :],
            qkv_sums[width + 64 : 2 * width],
            qkv_sums[width : width + 64],
            hidden_sums,
        ]
    )
    term_rows = -(-terms.shape[0] // (8 * width)) * 8
    terms = jnp.pad(terms, (0, term_rows * width - terms.shape[0])).reshape(term_rows, width)
    blocks = [wide_total[:, 2 * units + by * width :][:, :width] for by in range(groups)]
    final_sent = [jnp.concatenate([block, terms], axis=0).astype(bf16) for block in blocks[1:]]
    returned = [item.astype(f32) for item in slots_returned(final_sent)]
    output_total = blocks[0]
    for item in returned:
        output_total = output_total + item[:depth]
    all_terms = jnp.stack([terms.reshape(-1)] + [item[depth:].reshape(-1) for item in returned[::-1]])
    share = depth // groups
    added = jnp.sum(all_terms[:, : 5 * depth], axis=0).reshape(5, depth)
    added = lax.dynamic_slice_in_dim(added, uly * share, share, axis=1)
    rank = cube_index() * groups + uly

    def owned(start, length, count):
        at = rank * count
        source = (uly - at // length) % groups
        return lax.dynamic_slice(all_terms, (source, start + at % length), (1, count))[0]

    query_bias_grad = owned(5 * depth, width, share)
    value_bias_grad = owned(5 * depth + width, width, share)
    up_bias_grad = owned(5 * depth + 2 * width, units, up_bias.shape[0] // groups)
    down_bias_grad = lax.dynamic_slice_in_dim(seed_sums, uly * share, share)
    value_weight_grad = jnp.concatenate(
        [qkv_weight_grad[:, width + 64 : 2 * width], qkv_weight_grad[:, width : width + 64]], axis=1
    )

    normed_back = normed_own
    for item in normed_returned:
        normed_back = normed_back + after(item, *final_sent)[:part].astype(f32)
    outside = outside_own
    for item in normed_returned:
        outside = outside + after(item, *final_sent)[part:].astype(f32)
    xhat1, rstd1 = normalized(tokens.astype(f32))
    input_grad = (middle_back + norm_back(normed_back * gain1, xhat1, rstd1)).astype(bf16)
    result = (middle + (outside + down_bias_all)).astype(bf16)
    return (
        result,
        input_grad,
        qkv_weight_grad[:, 2 * width :],
        qkv_weight_grad[:, :width],
        value_weight_grad,
        output_total.T,
        up_weight_grad,
        down_total,
        query_bias_grad,
        value_bias_grad,
        added[4],
        up_bias_grad,
        down_bias_grad,
        added[0],
        added[1],
        added[2],
        added[3],
    )


def solution(mesh):
    rows = P(("fsdp", "blk", "uly"), None)
    tall, flat = P(("fsdp", "blk"), "uly"), P("uly", ("fsdp", "blk"))
    vector, vector_out = P(("fsdp", "blk")), P(("fsdp", "blk", "uly"))
    return jax.shard_map(
        shards,
        mesh=mesh,
        in_specs=(rows, tall, tall, tall, flat, tall, flat) + (vector,) * 9 + (rows,),
        out_specs=(rows, rows, tall, tall, tall, flat, tall, flat) + (vector_out,) * 9,
        check_vma=False,
    )
```

```python
import jax
import jax.numpy as jnp
from jax import lax
from jax.experimental import pallas as pl
from jax.experimental.pallas import tpu as pltpu
from jax.sharding import PartitionSpec as P

HEAD_DIM = 64
CUBE = ("fsdp", "blk")
VEC_ROWS = 16
VMEM_LIMIT = 56 * 1024 * 1024
KERNEL_COST = 30_000_000_000

KEY_GROUP, KEY_HALF = (0, 0, 1), (0, 1, 0)
VALUE_GROUP, VALUE_HALF = (2, 2, 1), (0, 1, 1)


def dot_plain(left, right):
    return jnp.dot(left, right, preferred_element_type=jnp.float32)


def dot_rows(left, right):
    return lax.dot_general(
        left, right, (((0,), (0,)), ((), ())), preferred_element_type=jnp.float32
    )


def dot_cols(left, right):
    return lax.dot_general(
        left, right, (((1,), (1,)), ((), ())), preferred_element_type=jnp.float32
    )


def passed_along(array, by):
    peers = lax.axis_size("uly")
    return lax.ppermute(array, "uly", [(i, (i + by) % peers) for i in range(peers)])


def slots_of(array):
    return [array] + [passed_along(array, by) for by in range(1, lax.axis_size("uly"))]


def blk_swapped(array, flip):
    peers = lax.axis_size("blk")
    return lax.ppermute(array, "blk", [(i, i ^ flip) for i in range(peers)])


def cube_swapped(array, even, odd):
    peers = lax.axis_size(CUBE)
    pairs = [(i, i ^ (odd if i & 1 else even)) for i in range(peers)]
    return lax.ppermute(array, CUBE, pairs)


def cube_index():
    return lax.axis_index("fsdp") * lax.axis_size("blk") + lax.axis_index("blk")


def place_kernel(cuts, index_ref, own, first, second, other, *outs):
    me = index_ref[0]
    odd = me & 1
    near, far = jnp.where(odd == 1, 2, 4), jnp.where(odd == 1, 4, 2)
    pieces = [
        (own, 0),
        (first, near),
        (second.at[0], far),
        (second.at[1], 6),
        (other.at[0], 1),
        (other.at[1], far ^ 1),
        (other.at[2], near ^ 1),
        (other.at[3], 7),
    ]
    for piece, flip in pieces:
        for out, (row, rows, column, columns) in zip(outs, cuts):
            out[me ^ flip] = piece[row : row + rows, column : column + columns]


def paired():
    return lax.axis_size("fsdp") == 2 and lax.axis_size("blk") == 4


def after(array, *others):
    return lax.optimization_barrier((array,) + others)[0]


def cube_placed(cuts, pieces):
    index = cube_index().astype(jnp.int32).reshape(1)
    outs = [((8, rows, columns), pieces[0].dtype) for _, rows, _, columns in cuts]
    return on_core(lambda *refs: place_kernel(cuts, *refs), index, pieces, outs)


def cube_flips(me):
    odd = me & 1
    return jnp.where(odd == 1, 2, 4), jnp.where(odd == 1, 4, 2)


def grads_kernel(pairs, spread, index, *refs):
    ins, (sent, kept_low, kept_high), (whole, extra) = refs[:-5], refs[-5:-2], refs[-2:]
    at = 0
    for count, flipped, column, columns in pairs:
        left, right = stacked_slots(ins[at : at + count]), ins[at + count][...]
        at += count + 1
        whole[:, column : column + columns] = dot_plain(left.T, right.T if flipped else right)
    rows = sent.shape[1]
    model, wide = whole.shape
    depth = model // 8
    if spread:
        hidden_sum, seed_sum, branch = ins[at], ins[at + 1], ins[at + 2]
        half = hidden_sum.shape[1] // 2
        right_sum = jnp.sum(right.astype(jnp.float32), axis=0, keepdims=True)
        branch_sum = jnp.sum(branch[...].astype(jnp.float32), axis=0, keepdims=True)
        whole_rows = jnp.concatenate([right_sum, jnp.zeros((7, wide), jnp.float32)], axis=0)
        part_rows = jnp.concatenate(
            [branch_sum, seed_sum[...], jnp.zeros((6, model), jnp.float32)], axis=0
        )
        for block in range(8):
            turned = part_rows if block == 0 else pltpu.roll(part_rows, model - depth * block, 1)
            extra[block, 0:8] = whole_rows
            extra[block, 1:2, 0:half] = hidden_sum[:, :half]
            extra[block, 2:3, 0:half] = hidden_sum[:, half:]
            extra[block, 8:16] = turned[:, :wide]
    me = index[0]
    near, far = cube_flips(me)
    for slot, flip in enumerate((0, near, far, 6)):
        block = me ^ flip ^ 1
        sent[slot, 0:depth] = whole[pl.ds(pl.multiple_of(block * depth, 8), depth)].astype(sent.dtype)
        if spread:
            sent[slot, depth:rows] = extra[block].astype(sent.dtype)
    for slot, flip in enumerate((0, far, near, 6)):
        block = me ^ flip
        kept = (kept_low if slot < 2 else kept_high).at[slot % 2]
        kept[0:depth] = whole[pl.ds(pl.multiple_of(block * depth, 8), depth)]
        if spread:
            kept[depth:rows] = extra[block]


def grads_sent(pairs, columns, depth):
    plan = [
        (len(left), flipped, column, right.shape[0 if flipped else 1])
        for left, flipped, right, column in pairs
    ]
    operands = [item for left, _, right, _ in pairs for item in [*left, right]]
    index = cube_index().astype(jnp.int32).reshape(1)
    return on_core(
        lambda *refs: grads_kernel(plan, False, *refs),
        index,
        operands,
        [((4, depth, columns), jnp.bfloat16)] + [((2, depth, columns), jnp.float32)] * 2,
        [((8 * depth, columns), jnp.float32), ((8, VEC_ROWS, columns), jnp.float32)],
    )


def grads_scattered(pairs, columns, owners, sums):
    blocks = []
    for left, flipped, right, _ in pairs:
        right = right.T if flipped else right
        blocks.append(dot_rows(stacked_slots(left), right))
    model = blocks[0].shape[0]
    depth = model // owners
    blocks = jnp.concatenate(blocks, axis=1).reshape(owners, depth, columns)
    if sums:
        hidden_sum, seed_sum, branch = sums
        half = hidden_sum.shape[1] // 2
        branch_sum = jnp.sum(branch.astype(jnp.float32), axis=0)
        extra = jnp.zeros((owners, VEC_ROWS, columns), jnp.float32)
        extra = extra.at[:, 0].set(jnp.sum(pairs[0][2].astype(jnp.float32), axis=0)[None])
        extra = extra.at[:, 1, :half].set(hidden_sum[:, :half])
        extra = extra.at[:, 2, :half].set(hidden_sum[:, half:])
        extra = extra.at[:, 8, :depth].set(branch_sum.reshape(owners, depth))
        extra = extra.at[:, 9, :depth].set(seed_sum.reshape(owners, depth))
        blocks = jnp.concatenate([blocks, extra], axis=1)
    return lax.psum_scatter(blocks, CUBE, scatter_dimension=0, tiled=False)


def half_padded(part, half):
    zero = jnp.zeros_like(part)
    return jnp.concatenate([part, zero] if half == 0 else [zero, part], axis=0)


def heads_across(array, halves):
    turned = array.T
    return [
        half_padded(turned[h * HEAD_DIM : (h + 1) * HEAD_DIM], halves[h])
        for h in range(len(halves))
    ]


def group_of(ref, group):
    return ref[:, group * 128 : (group + 1) * 128]


def slot_places(index, uly, slot_rows):
    return ((uly - index // slot_rows) & 3) * slot_rows + index % slot_rows


def causal(rows, uly):
    keys = lax.broadcasted_iota(jnp.int32, (rows, rows), 0)
    queries = lax.broadcasted_iota(jnp.int32, (rows, rows), 1)
    slot_rows = rows // 4
    return slot_places(keys, uly, slot_rows) <= slot_places(queries, uly, slot_rows)


def forward_block(query_t, kv_ref, top, total, mixed, allowed):
    turned = kv_ref[...].T
    for h in range(3):
        scores = dot_plain(group_of(kv_ref, KEY_GROUP[h]), query_t[h])
        if allowed is not None:
            scores = jnp.where(allowed, scores, -1e30)
        block_top = jnp.max(scores, axis=0, keepdims=True)
        low = VALUE_GROUP[h] * 128 + VALUE_HALF[h] * HEAD_DIM
        value_t = turned[low : low + HEAD_DIM]
        own = pl.ds(h * HEAD_DIM, HEAD_DIM)
        if allowed is not None:
            weights = jnp.exp(scores - block_top)
            top[h : h + 1] = block_top
            total[h : h + 1] = jnp.sum(weights, axis=0, keepdims=True)
            mixed[own] = dot_plain(value_t, weights.astype(jnp.bfloat16))
        else:
            old_top = top[h : h + 1]
            new_top = jnp.maximum(old_top, block_top)
            fade = jnp.exp(old_top - new_top)
            weights = jnp.exp(scores - new_top)
            top[h : h + 1] = new_top
            total[h : h + 1] = total[h : h + 1] * fade + jnp.sum(weights, axis=0, keepdims=True)
            mixed[own] = mixed[own] * fade + dot_plain(value_t, weights.astype(jnp.bfloat16))


def forward_near_kernel(place, query, kv_own, kv_core, top, total, mixed):
    blk, uly = place[0], place[1]
    query_t = heads_across(query[...], KEY_HALF)
    top[...] = jnp.zeros_like(top)
    total[...] = jnp.ones_like(total)
    forward_block(query_t, kv_own, top, total, mixed, causal(query.shape[0], uly))

    @pl.when((blk & 1) == 1)
    def _():
        forward_block(query_t, kv_core, top, total, mixed, None)


def forward_far_kernel(
    place, query, kv_y, kv_both, top_in, total_in, mixed_in, out, mixed, lse, top, total
):
    blk = place[0]
    top[...] = top_in[...]
    total[...] = total_in[...]
    mixed[...] = mixed_in[...]

    @pl.when((blk & 2) == 2)
    def _():
        query_t = heads_across(query[...], KEY_HALF)
        forward_block(query_t, kv_y, top, total, mixed, None)
        forward_block(query_t, kv_both, top, total, mixed, None)

    for h in range(3):
        own = pl.ds(h * HEAD_DIM, HEAD_DIM)
        mixed[own] = mixed[own] / total[h : h + 1]
    lse[...] = top[...] + jnp.log(total[...])
    out[...] = mixed[...].astype(jnp.bfloat16)


def backward_block(sides, kv_ref, dkv_ref, query_grad_t, allowed):
    query_t, grad_t, query_m, grad_m, delta, lse = sides
    turned = kv_ref[...].T
    columns = [None, None, None]

    def add(group, term):
        columns[group] = term if columns[group] is None else columns[group] + term

    for h in range(3):
        scores = dot_plain(group_of(kv_ref, KEY_GROUP[h]), query_t[h])
        probs = jnp.exp(scores - lse[h : h + 1])
        if allowed is not None:
            probs = jnp.where(allowed, probs, 0.0)
        prob_grad = dot_plain(group_of(kv_ref, VALUE_GROUP[h]), grad_t[h])
        score_grad = (probs * (prob_grad - delta[h])).astype(jnp.bfloat16)
        add(VALUE_GROUP[h], dot_plain(probs.astype(jnp.bfloat16), grad_m[h]))
        add(KEY_GROUP[h], dot_plain(score_grad, query_m[h]))
        low = KEY_GROUP[h] * 128 + KEY_HALF[h] * HEAD_DIM
        own = pl.ds(h * HEAD_DIM, HEAD_DIM)
        query_grad_t[own] += dot_plain(turned[low : low + HEAD_DIM], score_grad)
    for group in range(3):
        dkv_ref[:, group * 128 : (group + 1) * 128] = columns[group].astype(dkv_ref.dtype)


def backward_sides(query, grads, mixed, lse):
    query_t = heads_across(query[...], KEY_HALF)
    grad_all = jnp.concatenate([ref[...] for ref in grads], axis=1)
    grad_t = [
        half_padded(grad_all[h * HEAD_DIM : (h + 1) * HEAD_DIM], VALUE_HALF[h]) for h in range(3)
    ]
    product = grad_all.astype(jnp.float32) * mixed[...]
    delta = [
        jnp.sum(product[h * HEAD_DIM : (h + 1) * HEAD_DIM], axis=0, keepdims=True)
        for h in range(3)
    ]
    query_m = [item.T for item in query_t]
    grad_m = [item.T for item in grad_t]
    return query_t, grad_t, query_m, grad_m, delta, lse[...]


def backward_both_kernel(place, query, g0, g1, g2, g3, mixed, lse, kv_both, dkv_both, query_grad_t):
    query_grad_t[...] = jnp.zeros_like(query_grad_t)

    @pl.when((place[0] & 2) == 2)
    def _():
        sides = backward_sides(query, (g0, g1, g2, g3), mixed, lse)
        backward_block(sides, kv_both, dkv_both, query_grad_t, None)

    @pl.when((place[0] & 2) == 0)
    def _():
        dkv_both[...] = jnp.zeros_like(dkv_both)


def backward_y_kernel(
    place, query, g0, g1, g2, g3, mixed, lse, kv_y, dkv_core, grad_t_in, dkv_y, total, part
):
    total[...] = grad_t_in[...]

    @pl.when((place[0] & 2) == 2)
    def _():
        sides = backward_sides(query, (g0, g1, g2, g3), mixed, lse)
        backward_block(sides, kv_y, part, total, None)
        dkv_y[...] = (part[...] + dkv_core[...].astype(jnp.float32)).astype(dkv_y.dtype)

    @pl.when((place[0] & 2) == 0)
    def _():
        dkv_y[...] = jnp.zeros_like(dkv_y)


def backward_near_kernel(
    place,
    query,
    g0,
    g1,
    g2,
    g3,
    mixed,
    lse,
    kv_own,
    kv_core,
    grad_t_in,
    dkv_own,
    dkv_core,
    query_grad,
    total,
):
    blk, uly = place[0], place[1]
    total[...] = grad_t_in[...]
    sides = backward_sides(query, (g0, g1, g2, g3), mixed, lse)

    @pl.when((blk & 1) == 1)
    def _():
        backward_block(sides, kv_core, dkv_core, total, None)

    @pl.when((blk & 1) == 0)
    def _():
        dkv_core[...] = jnp.zeros_like(dkv_core)

    backward_block(sides, kv_own, dkv_own, total, causal(query.shape[0], uly))
    query_grad[...] = (total[...] * HEAD_DIM**-0.5).T.astype(jnp.bfloat16)


def on_core(kernel, place, operands, outs, scratch=()):
    vmem = pl.BlockSpec(memory_space=pltpu.VMEM)
    return pl.pallas_call(
        kernel,
        out_shape=[jax.ShapeDtypeStruct(shape, dtype) for shape, dtype in outs],
        in_specs=[pl.BlockSpec(memory_space=pltpu.SMEM)] + [vmem] * len(operands),
        out_specs=[vmem] * len(outs),
        scratch_shapes=[pltpu.VMEM(shape, dtype) for shape, dtype in scratch],
        compiler_params=pltpu.CompilerParams(vmem_limit_bytes=VMEM_LIMIT),
        cost_estimate=pl.CostEstimate(flops=KERNEL_COST, transcendentals=0, bytes_accessed=0),
    )(place, *operands)


def normalized(rows):
    centre = rows - jnp.mean(rows, axis=-1, keepdims=True)
    rstd = lax.rsqrt(jnp.mean(centre * centre, axis=-1, keepdims=True) + 1e-05)
    return centre * rstd, rstd


def norm_back(grad, xhat, rstd):
    return rstd * (
        grad
        - jnp.mean(grad, axis=-1, keepdims=True)
        - xhat * jnp.mean(grad * xhat, axis=-1, keepdims=True)
    )


def stacked_slots(refs):
    rows = refs[0].shape[0]
    return jnp.concatenate([ref[:rows] for ref in refs], axis=0)


def project_kernel(place, t0, t1, t2, t3, weight, named, bias, query, kv, xhat_low):
    rows = stacked_slots((t0, t1, t2, t3)).astype(jnp.float32)
    xhat, _ = normalized(rows)
    xhat_low[...] = xhat.astype(jnp.bfloat16)
    normed = (xhat * named[0:1] + named[1:2]).astype(jnp.bfloat16)
    qkv = dot_plain(normed, weight[...]) + bias[...]
    wide = kv.shape[1]
    kv[...] = qkv[:, :wide].astype(jnp.bfloat16)
    query[...] = qkv[:, wide:].astype(jnp.bfloat16) * jnp.asarray(HEAD_DIM**-0.5, jnp.bfloat16)


GELU_A, GELU_B = 0.7978845608028654, 0.044715


def middle_kernel(
    place,
    m0,
    m1,
    m2,
    m3,
    t0,
    t1,
    t2,
    t3,
    c0,
    c1,
    c2,
    c3,
    output_t,
    up,
    down_t,
    named,
    up_bias,
    middle_own,
    xhat_low,
    mixed_own,
    active_low,
    hidden_back_low,
    part_own,
    *parts,
):
    slot = t0.shape[0]
    mixed_t = jnp.concatenate(
        [m0[...]]
        + [
            jnp.concatenate([ref[:, (4 - by) * slot :], ref[:, : (4 - by) * slot]], axis=1)
            for by, ref in ((1, m1), (2, m2), (3, m3))
        ],
        axis=0,
    )
    mixed_own[...] = mixed_t[:, :slot]
    branch = dot_plain(output_t[...], mixed_t).T
    middle = stacked_slots((t0, t1, t2, t3)).astype(jnp.float32) + (branch + named[0:1])
    middle_own[...] = middle[:slot]
    xhat, _ = normalized(middle)
    xhat_low[...] = xhat.astype(jnp.bfloat16)
    second = (xhat * named[1:2] + named[2:3]).astype(jnp.bfloat16)
    hidden = dot_plain(second, up[...]) + up_bias[...]
    active_grad = dot_plain(stacked_slots((c0, c1, c2, c3)), down_t[...])
    square = hidden * hidden
    bent = jnp.tanh(GELU_A * hidden * (1.0 + GELU_B * square))
    active_low[...] = (0.5 * hidden * (1.0 + bent)).astype(jnp.bfloat16)
    slope = 0.5 * (1.0 + bent) + (0.5 * GELU_A) * hidden * (1.0 - bent * bent) * (
        1.0 + (3.0 * GELU_B) * square
    )
    hidden_back = (active_grad * slope).astype(jnp.bfloat16)
    hidden_back_low[...] = hidden_back
    second_back = dot_cols(hidden_back, up[...])
    part_own[...] = second_back[:slot]
    for by in range(1, 4):
        parts[by - 1][...] = second_back[by * slot : (by + 1) * slot].astype(jnp.bfloat16)


def outside_kernel(
    place, active, down_t, hidden_back, c0, c1, c2, c3, hidden_sum, seed_sum, part_own, *parts
):
    slot = part_own.shape[0]
    outside = dot_cols(active[...], down_t[...])
    part_own[...] = outside[:slot]
    for by in range(1, 4):
        parts[by - 1][...] = outside[by * slot : (by + 1) * slot].astype(jnp.bfloat16)
    hidden_sum[...] = jnp.sum(hidden_back[...].astype(jnp.float32), axis=0, keepdims=True)
    seed = stacked_slots((c0, c1, c2, c3)).astype(jnp.float32)
    seed_sum[...] = jnp.sum(seed, axis=0, keepdims=True)


def branch_kernel(
    place,
    part_own,
    r1,
    r2,
    r3,
    middle,
    seed,
    gain,
    output_t,
    middle_back,
    branch_back,
    *mixed_back_t,
):
    second_back = part_own[...]
    for ref in (r1, r2, r3):
        second_back = second_back + ref[...].astype(jnp.float32)
    xhat, rstd = normalized(middle[...])
    grad = seed[...].astype(jnp.float32) + norm_back(second_back * gain[...], xhat, rstd)
    middle_back[...] = grad
    low = grad.astype(jnp.bfloat16)
    branch_back[...] = low
    turned = dot_plain(low, output_t[...]).T.astype(jnp.bfloat16)
    width = mixed_back_t[0].shape[0]
    for by in range(4):
        mixed_back_t[by][...] = turned[by * width : (by + 1) * width]


def gather_back_kernel(
    place, own, core, far, query, weight, outside, dqkv, part_own, *parts
):
    wide = own.shape[1]
    width = query.shape[1]
    total = own[...].astype(jnp.float32) + core[...].astype(jnp.float32)
    kv_grad = (total + far[...].astype(jnp.float32)).astype(jnp.bfloat16)
    dqkv[:, :wide] = kv_grad
    dqkv[:, wide : wide + width] = query[...]
    spare = dqkv.shape[1] - wide - width
    dqkv[:, wide + width :] = jnp.zeros((query.shape[0], spare), jnp.bfloat16)
    normed_back = dot_cols(dqkv[:, : wide + width], weight[...])
    slot = part_own.shape[0]
    part_own[...] = normed_back[:slot]
    for by in range(1, 4):
        parts[by - 1][:slot] = normed_back[by * slot : (by + 1) * slot].astype(jnp.bfloat16)
    parts[1][slot:] = outside[...]


def last_kernel(index, *refs):
    ins, (xhat, hidden_sum, seed_sum, branch) = refs[:6], refs[6:10]
    part_own, p1, p2, p3, sent, kept_low, kept_high, dqkv, whole, extra = refs[10:]
    gather_back_kernel(index, *ins, dqkv, part_own, p1, p2, p3)
    plan = [(1, False, 0, dqkv.shape[1])]
    grads_kernel(
        plan,
        True,
        index,
        xhat,
        dqkv,
        hidden_sum,
        seed_sum,
        branch,
        sent,
        kept_low,
        kept_high,
        whole,
        extra,
    )


def own_rows_kernel(
    place,
    normed_own,
    n1,
    n2,
    n3,
    outside_own,
    o1,
    o3,
    tokens,
    middle_back,
    middle,
    gain,
    bias,
    result,
    input_grad,
):
    normed_back, outside = normed_own[...], outside_own[...]
    slot = normed_back.shape[0]
    for ref in (n1, n2, n3):
        normed_back = normed_back + ref[:slot].astype(jnp.float32)
    for ref in (o1, n2.at[slot:], o3):
        outside = outside + ref[...].astype(jnp.float32)
    xhat, rstd = normalized(tokens[...].astype(jnp.float32))
    grad = middle_back[...] + norm_back(normed_back * gain[...], xhat, rstd)
    input_grad[...] = grad.astype(jnp.bfloat16)
    result[...] = (middle[...] + (outside + bias[...])).astype(jnp.bfloat16)


def slots_returned(parts):
    return [passed_along(parts[by - 1], -by) for by in range(1, 4)]


def shards(
    tokens,
    query_weight,
    key_weight,
    value_weight,
    output_weight,
    up_weight,
    down_weight,
    query_bias,
    value_bias,
    output_bias,
    up_bias,
    down_bias,
    first_gain,
    first_shift,
    second_gain,
    second_shift,
    cotangent,
):
    bf16, f32 = jnp.bfloat16, jnp.float32
    uly, blk = lax.axis_index("uly"), lax.axis_index("blk")
    groups = lax.axis_size("uly")
    owners = lax.axis_size(CUBE)
    part = tokens.shape[0]
    rows = groups * part
    depth, width = query_weight.shape
    units = up_weight.shape[1]
    model = depth * owners
    place = jnp.stack([blk, uly]).astype(jnp.int32)

    qkv_own = jnp.concatenate(
        [key_weight, value_weight[:, 128:], value_weight[:, :128], query_weight], axis=1
    )
    vectors = [
        query_bias,
        value_bias,
        output_bias,
        down_bias,
        first_gain,
        first_shift,
        second_gain,
        second_shift,
    ]
    up_rows = up_bias.shape[0] // depth
    named = len(vectors) + up_rows
    wide = 3 * width
    vector_rows = jnp.concatenate(
        [vector.reshape(1, depth) for vector in vectors] + [up_bias.reshape(up_rows, depth)]
    )
    vector_rows = jnp.pad(vector_rows, ((0, VEC_ROWS - named), (0, wide - depth)))
    chunk = depth // groups
    output_own = output_weight.T
    output_rows = jnp.concatenate(
        [output_own[at * chunk : (at + 1) * chunk] for at in range(groups)], axis=1
    )
    spare = -(part + chunk) % 16
    token_sent = jnp.concatenate([tokens, jnp.pad(output_rows, ((0, spare), (0, 0)))], axis=0)
    token_slots = [tokens, passed_along(token_sent, 1), None, None]
    qkv_sent = jnp.concatenate([qkv_own, vector_rows], axis=0)
    qkv_cuts = [(0, depth, 0, wide), (depth, VEC_ROWS, 0, wide)]
    if paired():
        qkv_sent = after(qkv_sent, token_slots[1])
        token_later = after(token_sent, token_slots[1])
        token_slots[3] = passed_along(token_later, 3)
        token_slots[2] = passed_along(token_later, 2)
        qkv_first = after(cube_swapped(qkv_sent, 4, 2), token_slots[3])
        qkv_second = cube_swapped(jnp.stack([qkv_sent, qkv_first]), 2, 4)
        qkv_second = after(qkv_second, token_slots[2])
        qkv_other = cube_swapped(
            jnp.concatenate([qkv_sent[None], qkv_first[None], qkv_second]), 1, 1
        )
        qkv_whole, vector_whole = cube_placed(
            qkv_cuts, (qkv_sent, qkv_first, qkv_second, qkv_other)
        )
    else:
        token_slots = [tokens] + slots_of(token_sent)[1:]
        whole = lax.all_gather(qkv_sent, CUBE, axis=0, tiled=False)
        qkv_whole, vector_whole = whole[:, :depth], whole[:, depth:]
    qkv_whole = qkv_whole.reshape(model, wide)
    vector_whole = vector_whole[:, :named, :depth].astype(f32)
    up_bias_whole = vector_whole[:, len(vectors) :].reshape(-1)
    named = vector_whole.transpose(1, 0, 2).reshape(named, model)
    query_bias_own = lax.dynamic_slice_in_dim(named[0], uly * width, width)
    value_bias_own = lax.dynamic_slice_in_dim(named[1], uly * width, width)
    up_bias_own = lax.dynamic_slice_in_dim(up_bias_whole, uly * units, units)
    output_bias_all, down_bias_all = named[2], named[3]
    gain1, gain2, shift2 = named[4], named[6], named[7]

    qkv_bias = jnp.concatenate(
        [jnp.zeros((width,), f32), value_bias_own[128:], value_bias_own[:128], query_bias_own]
    )

    inner = groups * width
    rest_cuts = [
        (0, depth, 0, inner),
        (0, depth, inner, units),
        (0, depth, inner + units, units),
    ]
    cotangent_later = after(cotangent, *token_slots[1:])
    cotangent_slots = [cotangent] + [passed_along(cotangent_later, by) for by in range(1, groups)]
    output_slots = [output_own] + [
        jnp.concatenate(
            [item[part : part + chunk, at * width : (at + 1) * width] for at in range(groups)], axis=0
        )
        for item in token_slots[1:]
    ]
    rest_own = jnp.concatenate(output_slots + [up_weight, down_weight.T], axis=1)
    if paired():
        rest_own = after(rest_own, qkv_second)
        rest_first = cube_swapped(rest_own, 4, 2)

    qkv_ready = after(qkv_whole, cotangent_slots[1])
    query, kv_own, xhat1_low = on_core(
        project_kernel,
        place,
        token_slots + [qkv_ready, named[4:6], qkv_bias[None]],
        [((rows, width), bf16), ((rows, 2 * width), bf16), ((rows, model), bf16)],
    )
    kv_y = blk_swapped(kv_own, 2)
    kv_core = blk_swapped(kv_own, 1)
    stats = ((8, rows), f32)
    turned = ((width, rows), f32)
    if paired():
        rest_second = cube_swapped(jnp.stack([rest_own, rest_first]), 2, 4)
        kv_core = after(kv_core, rest_second)
    top, total, mixed_t = on_core(
        forward_near_kernel, place, (query, kv_own, kv_core), (stats, stats, turned)
    )
    kv_both = blk_swapped(after(kv_y, top, *cotangent_slots[2:]), 1)
    if paired():
        rest_second = after(rest_second, kv_both)
        rest_held = jnp.concatenate([rest_own[None], rest_first[None], rest_second])
        rest_other = cube_swapped(rest_held, 1, 1)
        kv_both = after(kv_both, rest_held)
    mixed_low, mixed_t, lse = on_core(
        forward_far_kernel,
        place,
        (query, kv_y, kv_both, top, total, mixed_t),
        (((width, rows), bf16), turned, stats),
        (stats, stats),
    )
    mixed_slots = slots_of(mixed_low)
    if paired():
        rest_other = after(rest_other, mixed_low)
        output_t, up_whole, down_t = cube_placed(
            rest_cuts, (rest_own, rest_first, rest_second, rest_other)
        )
    else:
        whole = lax.all_gather(rest_own, CUBE, axis=0, tiled=False)
        output_t, up_whole, down_t = [whole[:, :, c : c + n] for _, _, c, n in rest_cuts]
    output_t = output_t.reshape(model, inner)
    up_whole = up_whole.reshape(model, units)
    down_t = down_t.reshape(model, units)

    slab = ((part, model), f32)
    slabs = [((part, model), bf16)] * (groups - 1)
    wide_low = ((rows, model), bf16)
    units_low = ((rows, units), bf16)
    middle, xhat2_low, mixed_own, active, hidden_back, second_own, *second_parts = on_core(
        middle_kernel,
        place,
        mixed_slots
        + token_slots
        + cotangent_slots
        + [output_t, up_whole, down_t, jnp.stack([output_bias_all, gain2, shift2]), up_bias_own[None]],
        [slab, wide_low, ((inner, part), bf16), units_low, units_low, slab] + slabs,
    )
    second_returned = slots_returned(second_parts)
    hidden_sum, seed_sum, outside_own, *outside_parts = on_core(
        outside_kernel,
        place,
        [active, down_t, hidden_back] + cotangent_slots,
        [((1, units), f32), ((1, model), f32), slab] + slabs,
    )
    second_own = after(second_own, outside_own)

    middle_back, branch_back, *mixed_back_t = on_core(
        branch_kernel,
        place,
        [second_own] + second_returned + [middle, cotangent, gain2[None], output_t],
        [slab, ((part, model), bf16)] + [((width, part), bf16)] * groups,
    )
    grad_slots = [mixed_back_t[0]] + [
        passed_along(mixed_back_t[by], -by) for by in range(groups - 1, 0, -1)
    ]
    wide_pairs = [
        ([xhat2_low], False, hidden_back, 0),
        (cotangent_slots, False, active, units),
        ([branch_back], True, mixed_own, 2 * units),
    ]
    wide_columns = 2 * units + inner
    if paired():
        wide_sent, wide_low_part, wide_high_part = grads_sent(wide_pairs, wide_columns, depth)
        wide_got = cube_swapped(wide_sent, 1, 1)
        grad_slots[1] = after(grad_slots[1], wide_sent)
    outside_returned = [
        passed_along(after(outside_parts[by - 1], *mixed_back_t), -by) for by in (1, 3)
    ]
    grad_slots[1] = after(grad_slots[1], *outside_returned)
    sides = [query] + grad_slots + [mixed_t, lse]
    pair = ((rows, 2 * width), bf16)
    dkv_both, query_grad_t = on_core(
        backward_both_kernel, place, sides + [kv_both], (pair, turned)
    )
    if paired():
        wide_got = after(wide_got, dkv_both)
        wide_next = (wide_high_part + wide_got[2:].astype(f32)).astype(bf16)
        wide_more = cube_swapped(wide_next, 4, 2)
    dkv_y, query_grad_t = on_core(
        backward_y_kernel,
        place,
        sides + [kv_y, blk_swapped(dkv_both, 1), query_grad_t],
        (pair, turned),
        [((rows, 2 * width), f32)],
    )
    dkv_from_y = blk_swapped(dkv_y, 2)
    kv_last = after(kv_core, wide_next) if paired() else kv_core
    dkv_own, dkv_core, query_grad = on_core(
        backward_near_kernel,
        place,
        sides + [kv_own, kv_last, query_grad_t],
        (pair, pair, ((rows, width), bf16)),
        (turned,),
    )
    dkv_core = blk_swapped(dkv_core, 1)
    columns = -(-wide // 128) * 128
    back_operands = [dkv_own, dkv_core, dkv_from_y, query_grad, qkv_whole, outside_parts[1]]
    back_outs = [slab, slabs[0], ((2 * part, model), bf16), slabs[0]]
    sums = (hidden_sum, seed_sum, branch_back)
    dqkv_kind = ((rows, columns), bf16)
    if paired():
        kinds = [((4, depth + VEC_ROWS, columns), bf16)]
        kinds += [((2, depth + VEC_ROWS, columns), f32)] * 2
        normed_own, *normed_parts, near_sent, near_low, near_high = on_core(
            last_kernel,
            cube_index().astype(jnp.int32).reshape(1),
            back_operands + [xhat1_low] + list(sums),
            back_outs + kinds,
            [dqkv_kind, ((model, columns), f32), ((8, VEC_ROWS, columns), f32)],
        )
    else:
        dqkv, normed_own, *normed_parts = on_core(
            gather_back_kernel, place, back_operands, [dqkv_kind] + back_outs
        )
    normed_returned = slots_returned(normed_parts)

    if paired():
        near_got = cube_swapped(near_sent, 1, 1)
        wide_more = after(wide_more, near_sent)
        wide_last = wide_low_part[1] + wide_got[1].astype(f32) + wide_more[1].astype(f32)
        wide_end = cube_swapped(wide_last.astype(bf16), 2, 4)
        near_next = (near_high + near_got[2:].astype(f32)).astype(bf16)
        near_more = cube_swapped(near_next, 4, 2)
        near_last = near_low[1] + near_got[1].astype(f32) + near_more[1].astype(f32)
        near_end = cube_swapped(near_last.astype(bf16), 2, 4)
        near_total = near_low[0] + near_got[0].astype(f32) + near_more[0].astype(f32)
        near_total = near_total + near_end.astype(f32)
        wide_total = wide_low_part[0] + wide_got[0].astype(f32) + wide_more[0].astype(f32)
        wide_total = wide_total + wide_end.astype(f32)
    else:
        near_total = grads_scattered([([xhat1_low], False, dqkv, 0)], columns, owners, sums)
        wide_total = grads_scattered(wide_pairs, wide_columns, owners, ())

    half = units // 2
    qkv_total, qkv_sums = near_total[:depth, :wide], near_total[depth, :wide]
    hidden_sums = near_total[depth + 1 : depth + 3, :half].reshape(-1)
    branch_sums, seed_sums = near_total[depth + 8, :depth], near_total[depth + 9, :depth]
    up_total, down_total = wide_total[:, :units], wide_total[:, units : 2 * units].T
    own_gain1, own_shift1 = first_gain.astype(f32), first_shift.astype(f32)
    own_gain2, own_shift2 = second_gain.astype(f32), second_shift.astype(f32)
    qkv_weight_grad = own_gain1[:, None] * qkv_total + own_shift1[:, None] * qkv_sums[None]
    up_weight_grad = own_gain2[:, None] * up_total + own_shift2[:, None] * hidden_sums[None]
    qkv_wide, up_wide = qkv_own.astype(f32), up_weight.astype(f32)
    terms = jnp.concatenate(
        [
            jnp.sum(qkv_wide * qkv_total, axis=1),
            jnp.sum(qkv_wide * qkv_sums[None], axis=1),
            jnp.sum(up_wide * up_total, axis=1),
            jnp.sum(up_wide * hidden_sums[None], axis=1),
            branch_sums,
            qkv_sums[2 * width :],
            qkv_sums[width + 64 : 2 * width],
            qkv_sums[width : width + 64],
            hidden_sums,
        ]
    )
    term_rows = -(-terms.shape[0] // (8 * width)) * 8
    terms = jnp.pad(terms, (0, term_rows * width - terms.shape[0])).reshape(term_rows, width)
    blocks = [wide_total[:, 2 * units + by * width :][:, :width] for by in range(groups)]
    final_sent = [jnp.concatenate([block, terms], axis=0).astype(bf16) for block in blocks[1:]]
    returned = [item.astype(f32) for item in slots_returned(final_sent)]
    output_total = blocks[0]
    for item in returned:
        output_total = output_total + item[:depth]
    all_terms = jnp.stack([terms.reshape(-1)] + [item[depth:].reshape(-1) for item in returned[::-1]])
    share = depth // groups
    added = jnp.sum(all_terms[:, : 5 * depth], axis=0).reshape(5, depth)
    added = lax.dynamic_slice_in_dim(added, uly * share, share, axis=1)
    rank = cube_index() * groups + uly

    def owned(start, length, count):
        at = rank * count
        source = (uly - at // length) % groups
        return lax.dynamic_slice(all_terms, (source, start + at % length), (1, count))[0]

    query_bias_grad = owned(5 * depth, width, share)
    value_bias_grad = owned(5 * depth + width, width, share)
    up_bias_grad = owned(5 * depth + 2 * width, units, up_bias.shape[0] // groups)
    down_bias_grad = lax.dynamic_slice_in_dim(seed_sums, uly * share, share)
    value_weight_grad = jnp.concatenate(
        [qkv_weight_grad[:, width + 64 : 2 * width], qkv_weight_grad[:, width : width + 64]], axis=1
    )

    result, input_grad = on_core(
        own_rows_kernel,
        place,
        [normed_own]
        + [after(item, *final_sent) for item in normed_returned]
        + [outside_own]
        + outside_returned
        + [tokens, middle_back, middle, gain1[None], down_bias_all[None]],
        [((part, model), bf16)] * 2,
    )
    return (
        result,
        input_grad,
        qkv_weight_grad[:, 2 * width :],
        qkv_weight_grad[:, :width],
        value_weight_grad,
        output_total.T,
        up_weight_grad,
        down_total,
        query_bias_grad,
        value_bias_grad,
        added[4],
        up_bias_grad,
        down_bias_grad,
        added[0],
        added[1],
        added[2],
        added[3],
    )


def solution(mesh):
    rows = P(("fsdp", "blk", "uly"), None)
    tall, flat = P(("fsdp", "blk"), "uly"), P("uly", ("fsdp", "blk"))
    vector, vector_out = P(("fsdp", "blk")), P(("fsdp", "blk", "uly"))
    return jax.shard_map(
        shards,
        mesh=mesh,
        in_specs=(rows, tall, tall, tall, flat, tall, flat) + (vector,) * 9 + (rows,),
        out_specs=(rows, rows, tall, tall, tall, flat, tall, flat) + (vector_out,) * 9,
        check_vma=False,
    )
```

```python
import jax
import jax.numpy as jnp
from jax import lax
from jax.experimental import pallas as pl
from jax.experimental.pallas import tpu as pltpu
from jax.sharding import PartitionSpec as P

HEAD_DIM = 64
CUBE = ("fsdp", "blk")
VEC_ROWS = 16
VMEM_LIMIT = 56 * 1024 * 1024
KERNEL_COST = 30_000_000_000

KEY_GROUP, KEY_HALF = (0, 0, 1), (0, 1, 0)
VALUE_GROUP, VALUE_HALF = (2, 2, 1), (0, 1, 1)


def dot_plain(left, right):
    return jnp.dot(left, right, preferred_element_type=jnp.float32)


def dot_rows(left, right):
    return lax.dot_general(
        left, right, (((0,), (0,)), ((), ())), preferred_element_type=jnp.float32
    )


def dot_cols(left, right):
    return lax.dot_general(
        left, right, (((1,), (1,)), ((), ())), preferred_element_type=jnp.float32
    )


def passed_along(array, by):
    peers = lax.axis_size("uly")
    return lax.ppermute(array, "uly", [(i, (i + by) % peers) for i in range(peers)])


def slots_of(array):
    return [array] + [passed_along(array, by) for by in range(1, lax.axis_size("uly"))]


def blk_swapped(array, flip):
    peers = lax.axis_size("blk")
    return lax.ppermute(array, "blk", [(i, i ^ flip) for i in range(peers)])


def cube_swapped(array, even, odd):
    peers = lax.axis_size(CUBE)
    pairs = [(i, i ^ (odd if i & 1 else even)) for i in range(peers)]
    return lax.ppermute(array, CUBE, pairs)


def cube_index():
    return lax.axis_index("fsdp") * lax.axis_size("blk") + lax.axis_index("blk")


def cube_pieces(me, own, first, second, other):
    odd = me & 1
    near, far = jnp.where(odd == 1, 2, 4), jnp.where(odd == 1, 4, 2)
    return [
        (own, 0),
        (first, near),
        (second.at[0], far),
        (second.at[1], 6),
        (other.at[0], 1),
        (other.at[1], far ^ 1),
        (other.at[2], near ^ 1),
        (other.at[3], 7),
    ]


def place_kernel(cuts, index_ref, own, first, second, other, *outs):
    me = index_ref[0]
    for piece, flip in cube_pieces(me, own, first, second, other):
        for out, (row, rows, column, columns) in zip(outs, cuts):
            out[me ^ flip] = piece[row : row + rows, column : column + columns]


def paired():
    return lax.axis_size("fsdp") == 2 and lax.axis_size("blk") == 4


def after(array, *others):
    return lax.optimization_barrier((array,) + others)[0]


def cube_placed(cuts, pieces):
    index = cube_index().astype(jnp.int32).reshape(1)
    outs = [((8, rows, columns), pieces[0].dtype) for _, rows, _, columns in cuts]
    return on_core(lambda *refs: place_kernel(cuts, *refs), index, pieces, outs)


def cube_flips(me):
    odd = me & 1
    return jnp.where(odd == 1, 2, 4), jnp.where(odd == 1, 4, 2)


def grads_kernel(pairs, spread, index, *refs):
    ins, (sent, kept_low, kept_high), (whole, extra) = refs[:-5], refs[-5:-2], refs[-2:]
    at = 0
    for count, flipped, column, columns in pairs:
        left, right = stacked_slots(ins[at : at + count]), ins[at + count][...]
        at += count + 1
        whole[:, column : column + columns] = dot_plain(left.T, right.T if flipped else right)
    rows = sent.shape[1]
    model, wide = whole.shape
    depth = model // 8
    if spread:
        hidden_sum, seed_sum, branch = ins[at], ins[at + 1], ins[at + 2]
        half = hidden_sum.shape[1] // 2
        right_sum = jnp.sum(right.astype(jnp.float32), axis=0, keepdims=True)
        branch_sum = jnp.sum(branch[...].astype(jnp.float32), axis=0, keepdims=True)
        whole_rows = jnp.concatenate([right_sum, jnp.zeros((7, wide), jnp.float32)], axis=0)
        part_rows = jnp.concatenate(
            [branch_sum, seed_sum[...], jnp.zeros((6, model), jnp.float32)], axis=0
        )
        for block in range(8):
            turned = part_rows if block == 0 else pltpu.roll(part_rows, model - depth * block, 1)
            extra[block, 0:8] = whole_rows
            extra[block, 1:2, 0:half] = hidden_sum[:, :half]
            extra[block, 2:3, 0:half] = hidden_sum[:, half:]
            extra[block, 8:16] = turned[:, :wide]
    me = index[0]
    near, far = cube_flips(me)
    for slot, flip in enumerate((0, near, far, 6)):
        block = me ^ flip ^ 1
        sent[slot, 0:depth] = whole[pl.ds(pl.multiple_of(block * depth, 8), depth)].astype(sent.dtype)
        if spread:
            sent[slot, depth:rows] = extra[block].astype(sent.dtype)
    for slot, flip in enumerate((0, far, near, 6)):
        block = me ^ flip
        kept = (kept_low if slot < 2 else kept_high).at[slot % 2]
        kept[0:depth] = whole[pl.ds(pl.multiple_of(block * depth, 8), depth)]
        if spread:
            kept[depth:rows] = extra[block]


def grads_sent(pairs, columns, depth):
    plan = [
        (len(left), flipped, column, right.shape[0 if flipped else 1])
        for left, flipped, right, column in pairs
    ]
    operands = [item for left, _, right, _ in pairs for item in [*left, right]]
    index = cube_index().astype(jnp.int32).reshape(1)
    return on_core(
        lambda *refs: grads_kernel(plan, False, *refs),
        index,
        operands,
        [((4, depth, columns), jnp.bfloat16)] + [((2, depth, columns), jnp.float32)] * 2,
        [((8 * depth, columns), jnp.float32), ((8, VEC_ROWS, columns), jnp.float32)],
    )


def grads_scattered(pairs, columns, owners, sums):
    blocks = []
    for left, flipped, right, _ in pairs:
        right = right.T if flipped else right
        blocks.append(dot_rows(stacked_slots(left), right))
    model = blocks[0].shape[0]
    depth = model // owners
    blocks = jnp.concatenate(blocks, axis=1).reshape(owners, depth, columns)
    if sums:
        hidden_sum, seed_sum, branch = sums
        half = hidden_sum.shape[1] // 2
        branch_sum = jnp.sum(branch.astype(jnp.float32), axis=0)
        extra = jnp.zeros((owners, VEC_ROWS, columns), jnp.float32)
        extra = extra.at[:, 0].set(jnp.sum(pairs[0][2].astype(jnp.float32), axis=0)[None])
        extra = extra.at[:, 1, :half].set(hidden_sum[:, :half])
        extra = extra.at[:, 2, :half].set(hidden_sum[:, half:])
        extra = extra.at[:, 8, :depth].set(branch_sum.reshape(owners, depth))
        extra = extra.at[:, 9, :depth].set(seed_sum.reshape(owners, depth))
        blocks = jnp.concatenate([blocks, extra], axis=1)
    return lax.psum_scatter(blocks, CUBE, scatter_dimension=0, tiled=False)


def half_padded(part, half):
    zero = jnp.zeros_like(part)
    return jnp.concatenate([part, zero] if half == 0 else [zero, part], axis=0)


def heads_across(array, halves):
    turned = array.T
    return [
        half_padded(turned[h * HEAD_DIM : (h + 1) * HEAD_DIM], halves[h])
        for h in range(len(halves))
    ]


def group_of(ref, group):
    return ref[:, group * 128 : (group + 1) * 128]


def slot_places(index, uly, slot_rows):
    return ((uly - index // slot_rows) & 3) * slot_rows + index % slot_rows


def causal(rows, uly):
    keys = lax.broadcasted_iota(jnp.int32, (rows, rows), 0)
    queries = lax.broadcasted_iota(jnp.int32, (rows, rows), 1)
    slot_rows = rows // 4
    return slot_places(keys, uly, slot_rows) <= slot_places(queries, uly, slot_rows)


def forward_block(query_t, kv_ref, top, total, mixed, allowed):
    turned = kv_ref[...].T
    for h in range(3):
        scores = dot_plain(group_of(kv_ref, KEY_GROUP[h]), query_t[h])
        if allowed is not None:
            scores = jnp.where(allowed, scores, -1e30)
        block_top = jnp.max(scores, axis=0, keepdims=True)
        low = VALUE_GROUP[h] * 128 + VALUE_HALF[h] * HEAD_DIM
        value_t = turned[low : low + HEAD_DIM]
        own = pl.ds(h * HEAD_DIM, HEAD_DIM)
        if allowed is not None:
            weights = jnp.exp(scores - block_top)
            top[h : h + 1] = block_top
            total[h : h + 1] = jnp.sum(weights, axis=0, keepdims=True)
            mixed[own] = dot_plain(value_t, weights.astype(jnp.bfloat16))
        else:
            old_top = top[h : h + 1]
            new_top = jnp.maximum(old_top, block_top)
            fade = jnp.exp(old_top - new_top)
            weights = jnp.exp(scores - new_top)
            top[h : h + 1] = new_top
            total[h : h + 1] = total[h : h + 1] * fade + jnp.sum(weights, axis=0, keepdims=True)
            mixed[own] = mixed[own] * fade + dot_plain(value_t, weights.astype(jnp.bfloat16))


def forward_near_kernel(place, query, kv_own, kv_core, top, total, mixed):
    blk, uly = place[0], place[1]
    query_t = heads_across(query[...], KEY_HALF)
    top[...] = jnp.zeros_like(top)
    total[...] = jnp.ones_like(total)
    forward_block(query_t, kv_own, top, total, mixed, causal(query.shape[0], uly))

    @pl.when((blk & 1) == 1)
    def _():
        forward_block(query_t, kv_core, top, total, mixed, None)


def forward_far_kernel(
    place, query, kv_y, kv_both, top_in, total_in, mixed_in, out, mixed, lse, top, total
):
    blk = place[0]
    top[...] = top_in[...]
    total[...] = total_in[...]
    mixed[...] = mixed_in[...]

    @pl.when((blk & 2) == 2)
    def _():
        query_t = heads_across(query[...], KEY_HALF)
        forward_block(query_t, kv_y, top, total, mixed, None)
        forward_block(query_t, kv_both, top, total, mixed, None)

    for h in range(3):
        own = pl.ds(h * HEAD_DIM, HEAD_DIM)
        mixed[own] = mixed[own] / total[h : h + 1]
    lse[...] = top[...] + jnp.log(total[...])
    out[...] = mixed[...].astype(jnp.bfloat16)


def backward_block(sides, kv_ref, dkv_ref, query_grad_t, allowed):
    query_t, grad_t, query_m, grad_m, delta, lse = sides
    turned = kv_ref[...].T
    columns = [None, None, None]

    def add(group, term):
        columns[group] = term if columns[group] is None else columns[group] + term

    for h in range(3):
        scores = dot_plain(group_of(kv_ref, KEY_GROUP[h]), query_t[h])
        probs = jnp.exp(scores - lse[h : h + 1])
        if allowed is not None:
            probs = jnp.where(allowed, probs, 0.0)
        prob_grad = dot_plain(group_of(kv_ref, VALUE_GROUP[h]), grad_t[h])
        score_grad = (probs * (prob_grad - delta[h])).astype(jnp.bfloat16)
        add(VALUE_GROUP[h], dot_plain(probs.astype(jnp.bfloat16), grad_m[h]))
        add(KEY_GROUP[h], dot_plain(score_grad, query_m[h]))
        low = KEY_GROUP[h] * 128 + KEY_HALF[h] * HEAD_DIM
        own = pl.ds(h * HEAD_DIM, HEAD_DIM)
        query_grad_t[own] += dot_plain(turned[low : low + HEAD_DIM], score_grad)
    for group in range(3):
        dkv_ref[:, group * 128 : (group + 1) * 128] = columns[group].astype(dkv_ref.dtype)


def backward_sides(query, grads, mixed, lse):
    query_t = heads_across(query[...], KEY_HALF)
    grad_all = jnp.concatenate([ref[...] for ref in grads], axis=1)
    grad_t = [
        half_padded(grad_all[h * HEAD_DIM : (h + 1) * HEAD_DIM], VALUE_HALF[h]) for h in range(3)
    ]
    product = grad_all.astype(jnp.float32) * mixed[...]
    delta = [
        jnp.sum(product[h * HEAD_DIM : (h + 1) * HEAD_DIM], axis=0, keepdims=True)
        for h in range(3)
    ]
    query_m = [item.T for item in query_t]
    grad_m = [item.T for item in grad_t]
    return query_t, grad_t, query_m, grad_m, delta, lse[...]


def backward_both_kernel(place, query, g0, g1, g2, g3, mixed, lse, kv_both, dkv_both, query_grad_t):
    query_grad_t[...] = jnp.zeros_like(query_grad_t)

    @pl.when((place[0] & 2) == 2)
    def _():
        sides = backward_sides(query, (g0, g1, g2, g3), mixed, lse)
        backward_block(sides, kv_both, dkv_both, query_grad_t, None)

    @pl.when((place[0] & 2) == 0)
    def _():
        dkv_both[...] = jnp.zeros_like(dkv_both)


def backward_y_kernel(
    place, query, g0, g1, g2, g3, mixed, lse, kv_y, dkv_core, grad_t_in, dkv_y, total, part
):
    total[...] = grad_t_in[...]

    @pl.when((place[0] & 2) == 2)
    def _():
        sides = backward_sides(query, (g0, g1, g2, g3), mixed, lse)
        backward_block(sides, kv_y, part, total, None)
        dkv_y[...] = (part[...] + dkv_core[...].astype(jnp.float32)).astype(dkv_y.dtype)

    @pl.when((place[0] & 2) == 0)
    def _():
        dkv_y[...] = jnp.zeros_like(dkv_y)


def backward_near_kernel(
    place,
    query,
    g0,
    g1,
    g2,
    g3,
    mixed,
    lse,
    kv_own,
    kv_core,
    grad_t_in,
    dkv_own,
    dkv_core,
    query_grad,
    total,
):
    blk, uly = place[0], place[1]
    total[...] = grad_t_in[...]
    sides = backward_sides(query, (g0, g1, g2, g3), mixed, lse)

    @pl.when((blk & 1) == 1)
    def _():
        backward_block(sides, kv_core, dkv_core, total, None)

    @pl.when((blk & 1) == 0)
    def _():
        dkv_core[...] = jnp.zeros_like(dkv_core)

    backward_block(sides, kv_own, dkv_own, total, causal(query.shape[0], uly))
    query_grad[...] = (total[...] * HEAD_DIM**-0.5).T.astype(jnp.bfloat16)


def on_core(kernel, place, operands, outs, scratch=()):
    vmem = pl.BlockSpec(memory_space=pltpu.VMEM)
    return pl.pallas_call(
        kernel,
        out_shape=[jax.ShapeDtypeStruct(shape, dtype) for shape, dtype in outs],
        in_specs=[pl.BlockSpec(memory_space=pltpu.SMEM)] + [vmem] * len(operands),
        out_specs=[vmem] * len(outs),
        scratch_shapes=[pltpu.VMEM(shape, dtype) for shape, dtype in scratch],
        compiler_params=pltpu.CompilerParams(vmem_limit_bytes=VMEM_LIMIT),
        cost_estimate=pl.CostEstimate(flops=KERNEL_COST, transcendentals=0, bytes_accessed=0),
    )(place, *operands)


def normalized(rows):
    centre = rows - jnp.mean(rows, axis=-1, keepdims=True)
    rstd = lax.rsqrt(jnp.mean(centre * centre, axis=-1, keepdims=True) + 1e-05)
    return centre * rstd, rstd


def norm_back(grad, xhat, rstd):
    return rstd * (
        grad
        - jnp.mean(grad, axis=-1, keepdims=True)
        - xhat * jnp.mean(grad * xhat, axis=-1, keepdims=True)
    )


def stacked_slots(refs):
    rows = refs[0].shape[0]
    return jnp.concatenate([ref[:rows] for ref in refs], axis=0)


def project(rows, weight, gain, shift, bias, query, kv, xhat_low):
    xhat, _ = normalized(rows.astype(jnp.float32))
    xhat_low[...] = xhat.astype(jnp.bfloat16)
    normed = (xhat * gain + shift).astype(jnp.bfloat16)
    qkv = dot_plain(normed, weight) + bias
    wide = kv.shape[1]
    kv[...] = qkv[:, :wide].astype(jnp.bfloat16)
    query[...] = qkv[:, wide:].astype(jnp.bfloat16) * jnp.asarray(HEAD_DIM**-0.5, jnp.bfloat16)


def project_kernel(place, t0, t1, t2, t3, weight, named, bias, query, kv, xhat_low):
    rows = stacked_slots((t0, t1, t2, t3))
    project(rows, weight[...], named[0:1], named[1:2], bias[...], query, kv, xhat_low)


def entry_kernel(
    index,
    own,
    first,
    second,
    other,
    t0,
    t1,
    t2,
    t3,
    weight,
    named_out,
    up_own,
    query,
    kv,
    xhat_low,
):
    me, uly = index[0], index[1]
    model, wide = weight.shape
    depth, width = model // 8, wide // 3
    rows = named_out.shape[0]
    lane = lax.broadcasted_iota(jnp.int32, (rows, model), 1)
    named = jnp.zeros((rows, model), jnp.float32)
    for piece, flip in cube_pieces(me, own, first, second, other):
        at = me ^ flip
        weight[pl.ds(pl.multiple_of(at * depth, 16), depth), :] = piece[:depth, :]
        vector = piece[depth : depth + rows, :128].astype(jnp.float32)
        vector = jnp.concatenate([vector, jnp.zeros((rows, model - 128), jnp.float32)], axis=1)
        named = named + pltpu.roll(jnp.where(lane < depth, vector, 0.0), at * depth, 1)
    named_out[...] = named
    turned = pltpu.roll(named, ((4 - uly) & 3) * width, 1)

    def moved(row, by, low, high):
        block = row // 8 * 8
        item = pltpu.roll(turned[block : block + 8], by, 1) if by else turned[block : block + 8]
        inside = (lane[:8] >= low) & (lane[:8] < high)
        return jnp.where(inside, item, 0.0)[row - block : row - block + 1]

    bias = moved(1, 64, width, width + 64) + moved(1, width + 64, width + 64, 2 * width)
    bias = bias + moved(0, 2 * width, 2 * width, 3 * width)
    up = jnp.zeros((1, model), jnp.float32)
    for row in range(4):
        up = up + moved(8 + row, depth * row, depth * row, depth * (row + 1))
        up = up + moved(8 + row, depth * (3 + row), depth * (4 + row), depth * (5 + row))
    up_own[...] = up
    rows = stacked_slots((t0, t1, t2, t3))
    project(rows, weight[...], named[4:5], named[5:6], bias[:, :wide], query, kv, xhat_low)


GELU_A, GELU_B = 0.7978845608028654, 0.044715


def middle_kernel(
    place,
    m0,
    m1,
    m2,
    m3,
    t0,
    t1,
    t2,
    t3,
    c0,
    c1,
    c2,
    c3,
    output_t,
    up,
    down_t,
    named,
    up_bias,
    middle_own,
    xhat_low,
    mixed_own,
    active_low,
    hidden_back_low,
    part_own,
    *parts,
):
    slot = t0.shape[0]
    mixed_t = jnp.concatenate(
        [m0[...]]
        + [
            jnp.concatenate([ref[:, (4 - by) * slot :], ref[:, : (4 - by) * slot]], axis=1)
            for by, ref in ((1, m1), (2, m2), (3, m3))
        ],
        axis=0,
    )
    mixed_own[...] = mixed_t[:, :slot]
    branch = dot_plain(output_t[...], mixed_t).T
    middle = stacked_slots((t0, t1, t2, t3)).astype(jnp.float32) + (branch + named[0:1])
    middle_own[...] = middle[:slot]
    xhat, _ = normalized(middle)
    xhat_low[...] = xhat.astype(jnp.bfloat16)
    second = (xhat * named[1:2] + named[2:3]).astype(jnp.bfloat16)
    hidden = dot_plain(second, up[...]) + up_bias[...]
    active_grad = dot_plain(stacked_slots((c0, c1, c2, c3)), down_t[...])
    square = hidden * hidden
    bent = jnp.tanh(GELU_A * hidden * (1.0 + GELU_B * square))
    active_low[...] = (0.5 * hidden * (1.0 + bent)).astype(jnp.bfloat16)
    slope = 0.5 * (1.0 + bent) + (0.5 * GELU_A) * hidden * (1.0 - bent * bent) * (
        1.0 + (3.0 * GELU_B) * square
    )
    hidden_back = (active_grad * slope).astype(jnp.bfloat16)
    hidden_back_low[...] = hidden_back
    second_back = dot_cols(hidden_back, up[...])
    part_own[...] = second_back[:slot]
    for by in range(1, 4):
        parts[by - 1][...] = second_back[by * slot : (by + 1) * slot].astype(jnp.bfloat16)


def outside_kernel(
    place, active, down_t, hidden_back, c0, c1, c2, c3, hidden_sum, seed_sum, part_own, *parts
):
    slot = part_own.shape[0]
    outside = dot_cols(active[...], down_t[...])
    part_own[...] = outside[:slot]
    for by in range(1, 4):
        parts[by - 1][...] = outside[by * slot : (by + 1) * slot].astype(jnp.bfloat16)
    hidden_sum[...] = jnp.sum(hidden_back[...].astype(jnp.float32), axis=0, keepdims=True)
    seed = stacked_slots((c0, c1, c2, c3)).astype(jnp.float32)
    seed_sum[...] = jnp.sum(seed, axis=0, keepdims=True)


def branch_kernel(
    place,
    part_own,
    r1,
    r2,
    r3,
    middle,
    seed,
    gain,
    output_t,
    middle_back,
    branch_back,
    *mixed_back_t,
):
    second_back = part_own[...]
    for ref in (r1, r2, r3):
        second_back = second_back + ref[...].astype(jnp.float32)
    xhat, rstd = normalized(middle[...])
    grad = seed[...].astype(jnp.float32) + norm_back(second_back * gain[...], xhat, rstd)
    middle_back[...] = grad
    low = grad.astype(jnp.bfloat16)
    branch_back[...] = low
    turned = dot_plain(low, output_t[...]).T.astype(jnp.bfloat16)
    width = mixed_back_t[0].shape[0]
    for by in range(4):
        mixed_back_t[by][...] = turned[by * width : (by + 1) * width]


def gather_back_kernel(
    place, own, core, far, query, weight, outside, dqkv, part_own, *parts
):
    wide = own.shape[1]
    width = query.shape[1]
    total = own[...].astype(jnp.float32) + core[...].astype(jnp.float32)
    kv_grad = (total + far[...].astype(jnp.float32)).astype(jnp.bfloat16)
    dqkv[:, :wide] = kv_grad
    dqkv[:, wide : wide + width] = query[...]
    spare = dqkv.shape[1] - wide - width
    dqkv[:, wide + width :] = jnp.zeros((query.shape[0], spare), jnp.bfloat16)
    normed_back = dot_cols(dqkv[:, : wide + width], weight[...])
    slot = part_own.shape[0]
    part_own[...] = normed_back[:slot]
    for by in range(1, 4):
        parts[by - 1][:slot] = normed_back[by * slot : (by + 1) * slot].astype(jnp.bfloat16)
    parts[1][slot:] = outside[...]


def last_kernel(index, *refs):
    ins, (xhat, hidden_sum, seed_sum, branch) = refs[:6], refs[6:10]
    part_own, p1, p2, p3, sent, kept_low, kept_high, dqkv, whole, extra = refs[10:]
    gather_back_kernel(index, *ins, dqkv, part_own, p1, p2, p3)
    plan = [(1, False, 0, dqkv.shape[1])]
    grads_kernel(
        plan,
        True,
        index,
        xhat,
        dqkv,
        hidden_sum,
        seed_sum,
        branch,
        sent,
        kept_low,
        kept_high,
        whole,
        extra,
    )


def own_rows_kernel(
    place,
    normed_own,
    n1,
    n2,
    n3,
    outside_own,
    o1,
    o3,
    tokens,
    middle_back,
    middle,
    gain,
    bias,
    result,
    input_grad,
):
    normed_back, outside = normed_own[...], outside_own[...]
    slot = normed_back.shape[0]
    for ref in (n1, n2, n3):
        normed_back = normed_back + ref[:slot].astype(jnp.float32)
    for ref in (o1, n2.at[slot:], o3):
        outside = outside + ref[...].astype(jnp.float32)
    xhat, rstd = normalized(tokens[...].astype(jnp.float32))
    grad = middle_back[...] + norm_back(normed_back * gain[...], xhat, rstd)
    input_grad[...] = grad.astype(jnp.bfloat16)
    result[...] = (middle[...] + (outside + bias[...])).astype(jnp.bfloat16)


def slots_returned(parts):
    return [passed_along(parts[by - 1], -by) for by in range(1, 4)]


def shards(
    tokens,
    query_weight,
    key_weight,
    value_weight,
    output_weight,
    up_weight,
    down_weight,
    query_bias,
    value_bias,
    output_bias,
    up_bias,
    down_bias,
    first_gain,
    first_shift,
    second_gain,
    second_shift,
    cotangent,
):
    bf16, f32 = jnp.bfloat16, jnp.float32
    uly, blk = lax.axis_index("uly"), lax.axis_index("blk")
    groups = lax.axis_size("uly")
    owners = lax.axis_size(CUBE)
    part = tokens.shape[0]
    rows = groups * part
    depth, width = query_weight.shape
    units = up_weight.shape[1]
    model = depth * owners
    place = jnp.stack([blk, uly]).astype(jnp.int32)

    qkv_own = jnp.concatenate(
        [key_weight, value_weight[:, 128:], value_weight[:, :128], query_weight], axis=1
    )
    vectors = [
        query_bias,
        value_bias,
        output_bias,
        down_bias,
        first_gain,
        first_shift,
        second_gain,
        second_shift,
    ]
    up_rows = up_bias.shape[0] // depth
    named = len(vectors) + up_rows
    wide = 3 * width
    vector_rows = jnp.concatenate(
        [vector.reshape(1, depth) for vector in vectors] + [up_bias.reshape(up_rows, depth)]
    )
    vector_rows = jnp.pad(vector_rows, ((0, VEC_ROWS - named), (0, wide - depth)))
    chunk = depth // groups
    output_own = output_weight.T
    output_rows = jnp.concatenate(
        [output_own[at * chunk : (at + 1) * chunk] for at in range(groups)], axis=1
    )
    spare = -(part + chunk) % 16
    token_sent = jnp.concatenate([tokens, jnp.pad(output_rows, ((0, spare), (0, 0)))], axis=0)
    token_slots = [tokens, passed_along(token_sent, 1), None, None]
    qkv_sent = jnp.concatenate([qkv_own, vector_rows], axis=0)
    if paired():
        qkv_sent = after(qkv_sent, token_slots[1])
        token_later = after(token_sent, token_slots[1])
        token_slots[3] = passed_along(token_later, 3)
        token_slots[2] = passed_along(token_later, 2)
        qkv_first = after(cube_swapped(qkv_sent, 4, 2), token_slots[3])
        qkv_second = cube_swapped(jnp.stack([qkv_sent, qkv_first]), 2, 4)
        qkv_second = after(qkv_second, token_slots[2])
        qkv_other = cube_swapped(
            jnp.concatenate([qkv_sent[None], qkv_first[None], qkv_second]), 1, 1
        )
    else:
        token_slots = [tokens] + slots_of(token_sent)[1:]
        whole = lax.all_gather(qkv_sent, CUBE, axis=0, tiled=False)
        qkv_whole, vector_whole = whole[:, :depth], whole[:, depth:]

    inner = groups * width
    rest_cuts = [
        (0, depth, 0, inner),
        (0, depth, inner, units),
        (0, depth, inner + units, units),
    ]
    cotangent_later = after(cotangent, *token_slots[1:])
    cotangent_slots = [cotangent] + [passed_along(cotangent_later, by) for by in range(1, groups)]
    output_slots = [output_own] + [
        jnp.concatenate(
            [item[part : part + chunk, at * width : (at + 1) * width] for at in range(groups)], axis=0
        )
        for item in token_slots[1:]
    ]
    rest_own = jnp.concatenate(output_slots + [up_weight, down_weight.T], axis=1)
    if paired():
        rest_own = after(rest_own, qkv_second)
        rest_first = cube_swapped(rest_own, 4, 2)

    project_outs = [((rows, width), bf16), ((rows, 2 * width), bf16), ((rows, model), bf16)]
    if paired():
        qkv_whole, named, up_bias_own, query, kv_own, xhat1_low = on_core(
            entry_kernel,
            jnp.stack([cube_index(), uly]).astype(jnp.int32),
            [qkv_sent, qkv_first, qkv_second, qkv_other] + token_slots,
            [((model, wide), bf16), ((VEC_ROWS, model), f32), ((1, units), f32)] + project_outs,
        )
    else:
        qkv_whole = qkv_whole.reshape(model, wide)
        vector_whole = vector_whole[:, :named, :depth].astype(f32)
        up_bias_whole = vector_whole[:, len(vectors) :].reshape(-1)
        named = vector_whole.transpose(1, 0, 2).reshape(named, model)
        query_bias_own = lax.dynamic_slice_in_dim(named[0], uly * width, width)
        value_bias_own = lax.dynamic_slice_in_dim(named[1], uly * width, width)
        up_bias_own = lax.dynamic_slice_in_dim(up_bias_whole, uly * units, units)
        qkv_bias = jnp.concatenate(
            [jnp.zeros((width,), f32), value_bias_own[128:], value_bias_own[:128], query_bias_own]
        )
        up_bias_own = up_bias_own[None]
        query, kv_own, xhat1_low = on_core(
            project_kernel,
            place,
            token_slots + [qkv_whole, named[4:6], qkv_bias[None]],
            project_outs,
        )
    output_bias_all, down_bias_all = named[2], named[3]
    gain1, gain2, shift2 = named[4], named[6], named[7]
    kv_y = blk_swapped(kv_own, 2)
    kv_core = blk_swapped(kv_own, 1)
    stats = ((8, rows), f32)
    turned = ((width, rows), f32)
    if paired():
        rest_second = cube_swapped(after(jnp.stack([rest_own, rest_first]), kv_own), 2, 4)
    top, total, mixed_t = on_core(
        forward_near_kernel, place, (query, kv_own, kv_core), (stats, stats, turned)
    )
    kv_both = blk_swapped(after(kv_y, top, *cotangent_slots[1:]), 1)
    if paired():
        rest_second = after(rest_second, kv_both)
        rest_held = jnp.concatenate([rest_own[None], rest_first[None], rest_second])
        rest_other = cube_swapped(rest_held, 1, 1)
        kv_both = after(kv_both, rest_held)
    mixed_low, mixed_t, lse = on_core(
        forward_far_kernel,
        place,
        (query, kv_y, kv_both, top, total, mixed_t),
        (((width, rows), bf16), turned, stats),
        (stats, stats),
    )
    mixed_slots = slots_of(mixed_low)
    if paired():
        rest_other = after(rest_other, mixed_low)
        output_t, up_whole, down_t = cube_placed(
            rest_cuts, (rest_own, rest_first, rest_second, rest_other)
        )
    else:
        whole = lax.all_gather(rest_own, CUBE, axis=0, tiled=False)
        output_t, up_whole, down_t = [whole[:, :, c : c + n] for _, _, c, n in rest_cuts]
    output_t = output_t.reshape(model, inner)
    up_whole = up_whole.reshape(model, units)
    down_t = down_t.reshape(model, units)

    slab = ((part, model), f32)
    slabs = [((part, model), bf16)] * (groups - 1)
    wide_low = ((rows, model), bf16)
    units_low = ((rows, units), bf16)
    middle, xhat2_low, mixed_own, active, hidden_back, second_own, *second_parts = on_core(
        middle_kernel,
        place,
        mixed_slots
        + token_slots
        + cotangent_slots
        + [output_t, up_whole, down_t, jnp.stack([output_bias_all, gain2, shift2]), up_bias_own],
        [slab, wide_low, ((inner, part), bf16), units_low, units_low, slab] + slabs,
    )
    second_returned = slots_returned(second_parts)
    hidden_sum, seed_sum, outside_own, *outside_parts = on_core(
        outside_kernel,
        place,
        [active, down_t, hidden_back] + cotangent_slots,
        [((1, units), f32), ((1, model), f32), slab] + slabs,
    )
    second_own = after(second_own, outside_own)

    middle_back, branch_back, *mixed_back_t = on_core(
        branch_kernel,
        place,
        [second_own] + second_returned + [middle, cotangent, gain2[None], output_t],
        [slab, ((part, model), bf16)] + [((width, part), bf16)] * groups,
    )
    grad_slots = [mixed_back_t[0]] + [
        passed_along(mixed_back_t[by], -by) for by in range(groups - 1, 0, -1)
    ]
    wide_pairs = [
        ([xhat2_low], False, hidden_back, 0),
        (cotangent_slots, False, active, units),
        ([branch_back], True, mixed_own, 2 * units),
    ]
    wide_columns = 2 * units + inner
    if paired():
        wide_sent, wide_low_part, wide_high_part = grads_sent(wide_pairs, wide_columns, depth)
        wide_got = cube_swapped(wide_sent, 1, 1)
        grad_slots[1] = after(grad_slots[1], wide_sent)
    outside_returned = [
        passed_along(after(outside_parts[by - 1], *mixed_back_t), -by) for by in (1, 3)
    ]
    grad_slots[1] = after(grad_slots[1], *outside_returned)
    sides = [query] + grad_slots + [mixed_t, lse]
    pair = ((rows, 2 * width), bf16)
    dkv_both, query_grad_t = on_core(
        backward_both_kernel, place, sides + [kv_both], (pair, turned)
    )
    if paired():
        wide_got = after(wide_got, dkv_both)
        wide_next = (wide_high_part + wide_got[2:].astype(f32)).astype(bf16)
        wide_more = cube_swapped(wide_next, 4, 2)
    dkv_y, query_grad_t = on_core(
        backward_y_kernel,
        place,
        sides + [kv_y, blk_swapped(dkv_both, 1), query_grad_t],
        (pair, turned),
        [((rows, 2 * width), f32)],
    )
    dkv_from_y = blk_swapped(dkv_y, 2)
    kv_last = after(kv_core, wide_next) if paired() else kv_core
    dkv_own, dkv_core, query_grad = on_core(
        backward_near_kernel,
        place,
        sides + [kv_own, kv_last, query_grad_t],
        (pair, pair, ((rows, width), bf16)),
        (turned,),
    )
    dkv_core = blk_swapped(dkv_core, 1)
    columns = -(-wide // 128) * 128
    back_operands = [dkv_own, dkv_core, dkv_from_y, query_grad, qkv_whole, outside_parts[1]]
    back_outs = [slab, slabs[0], ((2 * part, model), bf16), slabs[0]]
    sums = (hidden_sum, seed_sum, branch_back)
    dqkv_kind = ((rows, columns), bf16)
    if paired():
        kinds = [((4, depth + VEC_ROWS, columns), bf16)]
        kinds += [((2, depth + VEC_ROWS, columns), f32)] * 2
        normed_own, *normed_parts, near_sent, near_low, near_high = on_core(
            last_kernel,
            cube_index().astype(jnp.int32).reshape(1),
            back_operands + [xhat1_low] + list(sums),
            back_outs + kinds,
            [dqkv_kind, ((model, columns), f32), ((8, VEC_ROWS, columns), f32)],
        )
    else:
        dqkv, normed_own, *normed_parts = on_core(
            gather_back_kernel, place, back_operands, [dqkv_kind] + back_outs
        )
    normed_returned = slots_returned(normed_parts)

    if paired():
        near_got = cube_swapped(near_sent, 1, 1)
        wide_more = after(wide_more, near_sent)
        wide_last = wide_low_part[1] + wide_got[1].astype(f32) + wide_more[1].astype(f32)
        wide_end = cube_swapped(wide_last.astype(bf16), 2, 4)
        near_next = (near_high + near_got[2:].astype(f32)).astype(bf16)
        near_more = cube_swapped(near_next, 4, 2)
        near_last = near_low[1] + near_got[1].astype(f32) + near_more[1].astype(f32)
        near_end = cube_swapped(near_last.astype(bf16), 2, 4)
        near_total = near_low[0] + near_got[0].astype(f32) + near_more[0].astype(f32)
        near_total = near_total + near_end.astype(f32)
        wide_total = wide_low_part[0] + wide_got[0].astype(f32) + wide_more[0].astype(f32)
        wide_total = wide_total + wide_end.astype(f32)
    else:
        near_total = grads_scattered([([xhat1_low], False, dqkv, 0)], columns, owners, sums)
        wide_total = grads_scattered(wide_pairs, wide_columns, owners, ())

    half = units // 2
    qkv_total, qkv_sums = near_total[:depth, :wide], near_total[depth, :wide]
    hidden_sums = near_total[depth + 1 : depth + 3, :half].reshape(-1)
    branch_sums, seed_sums = near_total[depth + 8, :depth], near_total[depth + 9, :depth]
    up_total, down_total = wide_total[:, :units], wide_total[:, units : 2 * units].T
    own_gain1, own_shift1 = first_gain.astype(f32), first_shift.astype(f32)
    own_gain2, own_shift2 = second_gain.astype(f32), second_shift.astype(f32)
    qkv_weight_grad = own_gain1[:, None] * qkv_total + own_shift1[:, None] * qkv_sums[None]
    up_weight_grad = own_gain2[:, None] * up_total + own_shift2[:, None] * hidden_sums[None]
    qkv_wide, up_wide = qkv_own.astype(f32), up_weight.astype(f32)
    terms = jnp.concatenate(
        [
            jnp.sum(qkv_wide * qkv_total, axis=1),
            jnp.sum(qkv_wide * qkv_sums[None], axis=1),
            jnp.sum(up_wide * up_total, axis=1),
            jnp.sum(up_wide * hidden_sums[None], axis=1),
            branch_sums,
            qkv_sums[2 * width :],
            qkv_sums[width + 64 : 2 * width],
            qkv_sums[width : width + 64],
            hidden_sums,
        ]
    )
    term_rows = -(-terms.shape[0] // (8 * width)) * 8
    terms = jnp.pad(terms, (0, term_rows * width - terms.shape[0])).reshape(term_rows, width)
    blocks = [wide_total[:, 2 * units + by * width :][:, :width] for by in range(groups)]
    final_sent = [jnp.concatenate([block, terms], axis=0).astype(bf16) for block in blocks[1:]]
    returned = [item.astype(f32) for item in slots_returned(final_sent)]
    output_total = blocks[0]
    for item in returned:
        output_total = output_total + item[:depth]
    all_terms = jnp.stack([terms.reshape(-1)] + [item[depth:].reshape(-1) for item in returned[::-1]])
    share = depth // groups
    added = jnp.sum(all_terms[:, : 5 * depth], axis=0).reshape(5, depth)
    added = lax.dynamic_slice_in_dim(added, uly * share, share, axis=1)
    rank = cube_index() * groups + uly

    def owned(start, length, count):
        at = rank * count
        source = (uly - at // length) % groups
        return lax.dynamic_slice(all_terms, (source, start + at % length), (1, count))[0]

    query_bias_grad = owned(5 * depth, width, share)
    value_bias_grad = owned(5 * depth + width, width, share)
    up_bias_grad = owned(5 * depth + 2 * width, units, up_bias.shape[0] // groups)
    down_bias_grad = lax.dynamic_slice_in_dim(seed_sums, uly * share, share)
    value_weight_grad = jnp.concatenate(
        [qkv_weight_grad[:, width + 64 : 2 * width], qkv_weight_grad[:, width : width + 64]], axis=1
    )

    result, input_grad = on_core(
        own_rows_kernel,
        place,
        [normed_own]
        + [after(item, *final_sent) for item in normed_returned]
        + [outside_own]
        + outside_returned
        + [tokens, middle_back, middle, gain1[None], down_bias_all[None]],
        [((part, model), bf16)] * 2,
    )
    return (
        result,
        input_grad,
        qkv_weight_grad[:, 2 * width :],
        qkv_weight_grad[:, :width],
        value_weight_grad,
        output_total.T,
        up_weight_grad,
        down_total,
        query_bias_grad,
        value_bias_grad,
        added[4],
        up_bias_grad,
        down_bias_grad,
        added[0],
        added[1],
        added[2],
        added[3],
    )


def solution(mesh):
    rows = P(("fsdp", "blk", "uly"), None)
    tall, flat = P(("fsdp", "blk"), "uly"), P("uly", ("fsdp", "blk"))
    vector, vector_out = P(("fsdp", "blk")), P(("fsdp", "blk", "uly"))
    return jax.shard_map(
        shards,
        mesh=mesh,
        in_specs=(rows, tall, tall, tall, flat, tall, flat) + (vector,) * 9 + (rows,),
        out_specs=(rows, rows, tall, tall, tall, flat, tall, flat) + (vector_out,) * 9,
        check_vma=False,
    )
```

```python
import jax
import jax.numpy as jnp
from jax import lax
from jax.experimental import pallas as pl
from jax.experimental.pallas import tpu as pltpu
from jax.sharding import PartitionSpec as P

HEAD_DIM = 64
CUBE = ("fsdp", "blk")
VEC_ROWS = 16
VMEM_LIMIT = 56 * 1024 * 1024
KERNEL_COST = 30_000_000_000

KEY_GROUP, KEY_HALF = (0, 0, 1), (0, 1, 0)
VALUE_GROUP, VALUE_HALF = (2, 2, 1), (0, 1, 1)


def dot_plain(left, right):
    return jnp.dot(left, right, preferred_element_type=jnp.float32)


def dot_rows(left, right):
    return lax.dot_general(
        left, right, (((0,), (0,)), ((), ())), preferred_element_type=jnp.float32
    )


def dot_cols(left, right):
    return lax.dot_general(
        left, right, (((1,), (1,)), ((), ())), preferred_element_type=jnp.float32
    )


def passed_along(array, by):
    peers = lax.axis_size("uly")
    return lax.ppermute(array, "uly", [(i, (i + by) % peers) for i in range(peers)])


def slots_of(array):
    return [array] + [passed_along(array, by) for by in range(1, lax.axis_size("uly"))]


def blk_swapped(array, flip):
    peers = lax.axis_size("blk")
    return lax.ppermute(array, "blk", [(i, i ^ flip) for i in range(peers)])


def cube_swapped(array, even, odd):
    peers = lax.axis_size(CUBE)
    pairs = [(i, i ^ (odd if i & 1 else even)) for i in range(peers)]
    return lax.ppermute(array, CUBE, pairs)


def cube_index():
    return lax.axis_index("fsdp") * lax.axis_size("blk") + lax.axis_index("blk")


def cube_pieces(me, own, first, second, other):
    odd = me & 1
    near, far = jnp.where(odd == 1, 2, 4), jnp.where(odd == 1, 4, 2)
    return [
        (own, 0),
        (first, near),
        (second.at[0], far),
        (second.at[1], 6),
        (other.at[0], 1),
        (other.at[1], far ^ 1),
        (other.at[2], near ^ 1),
        (other.at[3], 7),
    ]


def place_kernel(cuts, index_ref, own, first, second, other, *outs):
    me = index_ref[0]
    for piece, flip in cube_pieces(me, own, first, second, other):
        for out, (row, rows, column, columns) in zip(outs, cuts):
            out[me ^ flip] = piece[row : row + rows, column : column + columns]


def paired():
    return lax.axis_size("fsdp") == 2 and lax.axis_size("blk") == 4


def after(array, *others):
    return lax.optimization_barrier((array,) + others)[0]


def cube_placed(cuts, pieces):
    index = cube_index().astype(jnp.int32).reshape(1)
    outs = [((8, rows, columns), pieces[0].dtype) for _, rows, _, columns in cuts]
    return on_core(lambda *refs: place_kernel(cuts, *refs), index, pieces, outs)


def cube_flips(me):
    odd = me & 1
    return jnp.where(odd == 1, 2, 4), jnp.where(odd == 1, 4, 2)


def grads_kernel(pairs, spread, index, *refs):
    ins, (sent, kept_low, kept_high), (whole, extra) = refs[:-5], refs[-5:-2], refs[-2:]
    at = 0
    for count, flipped, column, columns in pairs:
        left, right = stacked_slots(ins[at : at + count]), ins[at + count][...]
        at += count + 1
        whole[:, column : column + columns] = dot_plain(left.T, right.T if flipped else right)
    rows = sent.shape[1]
    model, wide = whole.shape
    depth = model // 8
    if spread:
        hidden_sum, seed_sum, branch = ins[at], ins[at + 1], ins[at + 2]
        half = hidden_sum.shape[1] // 2
        right_sum = jnp.sum(right.astype(jnp.float32), axis=0, keepdims=True)
        branch_sum = jnp.sum(branch[...].astype(jnp.float32), axis=0, keepdims=True)
        whole_rows = jnp.concatenate([right_sum, jnp.zeros((7, wide), jnp.float32)], axis=0)
        part_rows = jnp.concatenate(
            [branch_sum, seed_sum[...], jnp.zeros((6, model), jnp.float32)], axis=0
        )
        for block in range(8):
            turned = part_rows if block == 0 else pltpu.roll(part_rows, model - depth * block, 1)
            extra[block, 0:8] = whole_rows
            extra[block, 1:2, 0:half] = hidden_sum[:, :half]
            extra[block, 2:3, 0:half] = hidden_sum[:, half:]
            extra[block, 8:16] = turned[:, :wide]
    me = index[0]
    near, far = cube_flips(me)
    for slot, flip in enumerate((0, near, far, 6)):
        block = me ^ flip ^ 1
        sent[slot, 0:depth] = whole[pl.ds(pl.multiple_of(block * depth, 8), depth)].astype(sent.dtype)
        if spread:
            sent[slot, depth:rows] = extra[block].astype(sent.dtype)
    for slot, flip in enumerate((0, far, near, 6)):
        block = me ^ flip
        kept = (kept_low if slot < 2 else kept_high).at[slot % 2]
        kept[0:depth] = whole[pl.ds(pl.multiple_of(block * depth, 8), depth)]
        if spread:
            kept[depth:rows] = extra[block]


def grads_sent(pairs, columns, depth):
    plan = [
        (len(left), flipped, column, right.shape[0 if flipped else 1])
        for left, flipped, right, column in pairs
    ]
    operands = [item for left, _, right, _ in pairs for item in [*left, right]]
    index = cube_index().astype(jnp.int32).reshape(1)
    return on_core(
        lambda *refs: grads_kernel(plan, False, *refs),
        index,
        operands,
        [((4, depth, columns), jnp.bfloat16)] + [((2, depth, columns), jnp.float32)] * 2,
        [((8 * depth, columns), jnp.float32), ((8, VEC_ROWS, columns), jnp.float32)],
    )


def grads_scattered(pairs, columns, owners, sums):
    blocks = []
    for left, flipped, right, _ in pairs:
        right = right.T if flipped else right
        blocks.append(dot_rows(stacked_slots(left), right))
    model = blocks[0].shape[0]
    depth = model // owners
    blocks = jnp.concatenate(blocks, axis=1).reshape(owners, depth, columns)
    if sums:
        hidden_sum, seed_sum, branch = sums
        half = hidden_sum.shape[1] // 2
        branch_sum = jnp.sum(branch.astype(jnp.float32), axis=0)
        extra = jnp.zeros((owners, VEC_ROWS, columns), jnp.float32)
        extra = extra.at[:, 0].set(jnp.sum(pairs[0][2].astype(jnp.float32), axis=0)[None])
        extra = extra.at[:, 1, :half].set(hidden_sum[:, :half])
        extra = extra.at[:, 2, :half].set(hidden_sum[:, half:])
        extra = extra.at[:, 8, :depth].set(branch_sum.reshape(owners, depth))
        extra = extra.at[:, 9, :depth].set(seed_sum.reshape(owners, depth))
        blocks = jnp.concatenate([blocks, extra], axis=1)
    return lax.psum_scatter(blocks, CUBE, scatter_dimension=0, tiled=False)


def half_padded(part, half):
    zero = jnp.zeros_like(part)
    return jnp.concatenate([part, zero] if half == 0 else [zero, part], axis=0)


def heads_across(array, halves):
    turned = array.T
    return [
        half_padded(turned[h * HEAD_DIM : (h + 1) * HEAD_DIM], halves[h])
        for h in range(len(halves))
    ]


def group_of(ref, group):
    return ref[:, group * 128 : (group + 1) * 128]


def slot_places(index, uly, slot_rows):
    return ((uly - index // slot_rows) & 3) * slot_rows + index % slot_rows


def causal(rows, uly):
    keys = lax.broadcasted_iota(jnp.int32, (rows, rows), 0)
    queries = lax.broadcasted_iota(jnp.int32, (rows, rows), 1)
    slot_rows = rows // 4
    return slot_places(keys, uly, slot_rows) <= slot_places(queries, uly, slot_rows)


def forward_block(query_t, kv_ref, top, total, mixed, allowed):
    turned = kv_ref[...].T
    for h in range(3):
        scores = dot_plain(group_of(kv_ref, KEY_GROUP[h]), query_t[h])
        if allowed is not None:
            scores = jnp.where(allowed, scores, -1e30)
        block_top = jnp.max(scores, axis=0, keepdims=True)
        low = VALUE_GROUP[h] * 128 + VALUE_HALF[h] * HEAD_DIM
        value_t = turned[low : low + HEAD_DIM]
        own = pl.ds(h * HEAD_DIM, HEAD_DIM)
        if allowed is not None:
            weights = jnp.exp(scores - block_top)
            top[h : h + 1] = block_top
            total[h : h + 1] = jnp.sum(weights, axis=0, keepdims=True)
            mixed[own] = dot_plain(value_t, weights.astype(jnp.bfloat16))
        else:
            old_top = top[h : h + 1]
            new_top = jnp.maximum(old_top, block_top)
            fade = jnp.exp(old_top - new_top)
            weights = jnp.exp(scores - new_top)
            top[h : h + 1] = new_top
            total[h : h + 1] = total[h : h + 1] * fade + jnp.sum(weights, axis=0, keepdims=True)
            mixed[own] = mixed[own] * fade + dot_plain(value_t, weights.astype(jnp.bfloat16))


def forward_near_kernel(place, query, kv_own, kv_core, top, total, mixed):
    blk, uly = place[0], place[1]
    query_t = heads_across(query[...], KEY_HALF)
    top[...] = jnp.zeros_like(top)
    total[...] = jnp.ones_like(total)
    forward_block(query_t, kv_own, top, total, mixed, causal(query.shape[0], uly))

    @pl.when((blk & 1) == 1)
    def _():
        forward_block(query_t, kv_core, top, total, mixed, None)


def forward_far_kernel(
    place, query, kv_y, kv_both, top_in, total_in, mixed_in, out, mixed, lse, top, total
):
    blk = place[0]
    top[...] = top_in[...]
    total[...] = total_in[...]
    mixed[...] = mixed_in[...]

    @pl.when((blk & 2) == 2)
    def _():
        query_t = heads_across(query[...], KEY_HALF)
        forward_block(query_t, kv_y, top, total, mixed, None)
        forward_block(query_t, kv_both, top, total, mixed, None)

    for h in range(3):
        own = pl.ds(h * HEAD_DIM, HEAD_DIM)
        mixed[own] = mixed[own] / total[h : h + 1]
    lse[...] = top[...] + jnp.log(total[...])
    out[...] = mixed[...].astype(jnp.bfloat16)


def backward_block(sides, kv_ref, dkv_ref, query_grad_t, allowed):
    query_t, grad_t, query_m, grad_m, delta, lse = sides
    turned = kv_ref[...].T
    columns = [None, None, None]

    def add(group, term):
        columns[group] = term if columns[group] is None else columns[group] + term

    for h in range(3):
        scores = dot_plain(group_of(kv_ref, KEY_GROUP[h]), query_t[h])
        probs = jnp.exp(scores - lse[h : h + 1])
        if allowed is not None:
            probs = jnp.where(allowed, probs, 0.0)
        prob_grad = dot_plain(group_of(kv_ref, VALUE_GROUP[h]), grad_t[h])
        score_grad = (probs * (prob_grad - delta[h])).astype(jnp.bfloat16)
        add(VALUE_GROUP[h], dot_plain(probs.astype(jnp.bfloat16), grad_m[h]))
        add(KEY_GROUP[h], dot_plain(score_grad, query_m[h]))
        low = KEY_GROUP[h] * 128 + KEY_HALF[h] * HEAD_DIM
        own = pl.ds(h * HEAD_DIM, HEAD_DIM)
        query_grad_t[own] += dot_plain(turned[low : low + HEAD_DIM], score_grad)
    for group in range(3):
        dkv_ref[:, group * 128 : (group + 1) * 128] = columns[group].astype(dkv_ref.dtype)


def backward_sides(query, grads, mixed, lse):
    query_t = heads_across(query[...], KEY_HALF)
    grad_all = jnp.concatenate([ref[...] for ref in grads], axis=1)
    grad_t = [
        half_padded(grad_all[h * HEAD_DIM : (h + 1) * HEAD_DIM], VALUE_HALF[h]) for h in range(3)
    ]
    product = grad_all.astype(jnp.float32) * mixed[...]
    delta = [
        jnp.sum(product[h * HEAD_DIM : (h + 1) * HEAD_DIM], axis=0, keepdims=True)
        for h in range(3)
    ]
    query_m = [item.T for item in query_t]
    grad_m = [item.T for item in grad_t]
    return query_t, grad_t, query_m, grad_m, delta, lse[...]


def backward_both_kernel(place, query, g0, g1, g2, g3, mixed, lse, kv_both, dkv_both, query_grad_t):
    query_grad_t[...] = jnp.zeros_like(query_grad_t)

    @pl.when((place[0] & 2) == 2)
    def _():
        sides = backward_sides(query, (g0, g1, g2, g3), mixed, lse)
        backward_block(sides, kv_both, dkv_both, query_grad_t, None)

    @pl.when((place[0] & 2) == 0)
    def _():
        dkv_both[...] = jnp.zeros_like(dkv_both)


def backward_y_kernel(
    place, query, g0, g1, g2, g3, mixed, lse, kv_y, dkv_core, grad_t_in, dkv_y, total, part
):
    total[...] = grad_t_in[...]

    @pl.when((place[0] & 2) == 2)
    def _():
        sides = backward_sides(query, (g0, g1, g2, g3), mixed, lse)
        backward_block(sides, kv_y, part, total, None)
        dkv_y[...] = (part[...] + dkv_core[...].astype(jnp.float32)).astype(dkv_y.dtype)

    @pl.when((place[0] & 2) == 0)
    def _():
        dkv_y[...] = jnp.zeros_like(dkv_y)


def backward_near_kernel(
    place,
    query,
    g0,
    g1,
    g2,
    g3,
    mixed,
    lse,
    kv_own,
    kv_core,
    grad_t_in,
    dkv_own,
    dkv_core,
    query_grad,
    total,
):
    blk, uly = place[0], place[1]
    total[...] = grad_t_in[...]
    sides = backward_sides(query, (g0, g1, g2, g3), mixed, lse)

    @pl.when((blk & 1) == 1)
    def _():
        backward_block(sides, kv_core, dkv_core, total, None)

    @pl.when((blk & 1) == 0)
    def _():
        dkv_core[...] = jnp.zeros_like(dkv_core)

    backward_block(sides, kv_own, dkv_own, total, causal(query.shape[0], uly))
    query_grad[...] = (total[...] * HEAD_DIM**-0.5).T.astype(jnp.bfloat16)


def on_core(kernel, place, operands, outs, scratch=()):
    vmem = pl.BlockSpec(memory_space=pltpu.VMEM)
    return pl.pallas_call(
        kernel,
        out_shape=[jax.ShapeDtypeStruct(shape, dtype) for shape, dtype in outs],
        in_specs=[pl.BlockSpec(memory_space=pltpu.SMEM)] + [vmem] * len(operands),
        out_specs=[vmem] * len(outs),
        scratch_shapes=[pltpu.VMEM(shape, dtype) for shape, dtype in scratch],
        compiler_params=pltpu.CompilerParams(vmem_limit_bytes=VMEM_LIMIT),
        cost_estimate=pl.CostEstimate(flops=KERNEL_COST, transcendentals=0, bytes_accessed=0),
    )(place, *operands)


def normalized(rows):
    centre = rows - jnp.mean(rows, axis=-1, keepdims=True)
    rstd = lax.rsqrt(jnp.mean(centre * centre, axis=-1, keepdims=True) + 1e-05)
    return centre * rstd, rstd


def norm_back(grad, xhat, rstd):
    return rstd * (
        grad
        - jnp.mean(grad, axis=-1, keepdims=True)
        - xhat * jnp.mean(grad * xhat, axis=-1, keepdims=True)
    )


def stacked_slots(refs):
    rows = refs[0].shape[0]
    return jnp.concatenate([ref[:rows] for ref in refs], axis=0)


def project(rows, weight, gain, shift, bias, query, kv, xhat_low):
    xhat, _ = normalized(rows.astype(jnp.float32))
    xhat_low[...] = xhat.astype(jnp.bfloat16)
    normed = (xhat * gain + shift).astype(jnp.bfloat16)
    qkv = dot_plain(normed, weight) + bias
    wide = kv.shape[1]
    kv[...] = qkv[:, :wide].astype(jnp.bfloat16)
    query[...] = qkv[:, wide:].astype(jnp.bfloat16) * jnp.asarray(HEAD_DIM**-0.5, jnp.bfloat16)


def project_kernel(place, t0, t1, t2, t3, weight, named, bias, query, kv, xhat_low):
    rows = stacked_slots((t0, t1, t2, t3))
    project(rows, weight[...], named[0:1], named[1:2], bias[...], query, kv, xhat_low)


def entry_kernel(
    index,
    own,
    first,
    second,
    other,
    t0,
    t1,
    t2,
    t3,
    weight,
    named_out,
    up_own,
    query,
    kv,
    xhat_low,
):
    me, uly = index[0], index[1]
    model, wide = weight.shape
    depth, width = model // 8, wide // 3
    rows = named_out.shape[0]
    lane = lax.broadcasted_iota(jnp.int32, (rows, model), 1)
    named = jnp.zeros((rows, model), jnp.float32)
    for piece, flip in cube_pieces(me, own, first, second, other):
        at = me ^ flip
        weight[pl.ds(pl.multiple_of(at * depth, 16), depth), :] = piece[:depth, :]
        vector = piece[depth : depth + rows, :128].astype(jnp.float32)
        vector = jnp.concatenate([vector, jnp.zeros((rows, model - 128), jnp.float32)], axis=1)
        named = named + pltpu.roll(jnp.where(lane < depth, vector, 0.0), at * depth, 1)
    named_out[...] = named
    turned = pltpu.roll(named, ((4 - uly) & 3) * width, 1)

    def moved(row, by, low, high):
        block = row // 8 * 8
        item = pltpu.roll(turned[block : block + 8], by, 1) if by else turned[block : block + 8]
        inside = (lane[:8] >= low) & (lane[:8] < high)
        return jnp.where(inside, item, 0.0)[row - block : row - block + 1]

    bias = moved(1, 64, width, width + 64) + moved(1, width + 64, width + 64, 2 * width)
    bias = bias + moved(0, 2 * width, 2 * width, 3 * width)
    up = jnp.zeros((1, model), jnp.float32)
    for row in range(4):
        up = up + moved(8 + row, depth * row, depth * row, depth * (row + 1))
        up = up + moved(8 + row, depth * (3 + row), depth * (4 + row), depth * (5 + row))
    up_own[...] = up
    rows = stacked_slots((t0, t1, t2, t3))
    project(rows, weight[...], named[4:5], named[5:6], bias[:, :wide], query, kv, xhat_low)


GELU_A, GELU_B = 0.7978845608028654, 0.044715


def middle_kernel(
    place,
    m0,
    m1,
    m2,
    m3,
    t0,
    t1,
    t2,
    t3,
    c0,
    c1,
    c2,
    c3,
    output_t,
    up,
    down_t,
    named,
    up_bias,
    middle_own,
    xhat_low,
    mixed_own,
    active_low,
    hidden_back_low,
    part_own,
    *parts,
):
    slot = t0.shape[0]
    mixed_t = jnp.concatenate(
        [m0[...]]
        + [
            jnp.concatenate([ref[:, (4 - by) * slot :], ref[:, : (4 - by) * slot]], axis=1)
            for by, ref in ((1, m1), (2, m2), (3, m3))
        ],
        axis=0,
    )
    mixed_own[...] = mixed_t[:, :slot]
    branch = dot_plain(output_t[...], mixed_t).T
    middle = stacked_slots((t0, t1, t2, t3)).astype(jnp.float32) + (branch + named[0:1])
    middle_own[...] = middle[:slot]
    xhat, _ = normalized(middle)
    xhat_low[...] = xhat.astype(jnp.bfloat16)
    second = (xhat * named[1:2] + named[2:3]).astype(jnp.bfloat16)
    hidden = dot_plain(second, up[...]) + up_bias[...]
    active_grad = dot_plain(stacked_slots((c0, c1, c2, c3)), down_t[...])
    square = hidden * hidden
    bent = jnp.tanh(GELU_A * hidden * (1.0 + GELU_B * square))
    active_low[...] = (0.5 * hidden * (1.0 + bent)).astype(jnp.bfloat16)
    slope = 0.5 * (1.0 + bent) + (0.5 * GELU_A) * hidden * (1.0 - bent * bent) * (
        1.0 + (3.0 * GELU_B) * square
    )
    hidden_back = (active_grad * slope).astype(jnp.bfloat16)
    hidden_back_low[...] = hidden_back
    second_back = dot_cols(hidden_back, up[...])
    part_own[...] = second_back[:slot]
    for by in range(1, 4):
        parts[by - 1][...] = second_back[by * slot : (by + 1) * slot].astype(jnp.bfloat16)


def outside_kernel(
    place, active, down_t, hidden_back, c0, c1, c2, c3, hidden_sum, seed_sum, part_own, *parts
):
    slot = part_own.shape[0]
    outside = dot_cols(active[...], down_t[...])
    part_own[...] = outside[:slot]
    for by in range(1, 4):
        parts[by - 1][...] = outside[by * slot : (by + 1) * slot].astype(jnp.bfloat16)
    hidden_sum[...] = jnp.sum(hidden_back[...].astype(jnp.float32), axis=0, keepdims=True)
    seed = stacked_slots((c0, c1, c2, c3)).astype(jnp.float32)
    seed_sum[...] = jnp.sum(seed, axis=0, keepdims=True)


def branch_kernel(
    place,
    part_own,
    r1,
    r2,
    r3,
    middle,
    seed,
    gain,
    output_t,
    middle_back,
    branch_back,
    *mixed_back_t,
):
    second_back = part_own[...]
    for ref in (r1, r2, r3):
        second_back = second_back + ref[...].astype(jnp.float32)
    xhat, rstd = normalized(middle[...])
    grad = seed[...].astype(jnp.float32) + norm_back(second_back * gain[...], xhat, rstd)
    middle_back[...] = grad
    low = grad.astype(jnp.bfloat16)
    branch_back[...] = low
    turned = dot_plain(low, output_t[...]).T.astype(jnp.bfloat16)
    width = mixed_back_t[0].shape[0]
    for by in range(4):
        mixed_back_t[by][...] = turned[by * width : (by + 1) * width]


def gather_back_kernel(
    place, own, core, far, query, weight, outside, dqkv, part_own, *parts
):
    wide = own.shape[1]
    width = query.shape[1]
    total = own[...].astype(jnp.float32) + core[...].astype(jnp.float32)
    kv_grad = (total + far[...].astype(jnp.float32)).astype(jnp.bfloat16)
    dqkv[:, :wide] = kv_grad
    dqkv[:, wide : wide + width] = query[...]
    spare = dqkv.shape[1] - wide - width
    dqkv[:, wide + width :] = jnp.zeros((query.shape[0], spare), jnp.bfloat16)
    normed_back = dot_cols(dqkv[:, : wide + width], weight[...])
    slot = part_own.shape[0]
    part_own[...] = normed_back[:slot]
    for by in range(1, 4):
        parts[by - 1][:slot] = normed_back[by * slot : (by + 1) * slot].astype(jnp.bfloat16)
    parts[1][slot:] = outside[...]


def last_kernel(index, *refs):
    ins, (xhat, hidden_sum, seed_sum, branch) = refs[:6], refs[6:10]
    part_own, p1, p2, p3, sent, kept_low, kept_high, dqkv, whole, extra = refs[10:]
    gather_back_kernel(index, *ins, dqkv, part_own, p1, p2, p3)
    plan = [(1, False, 0, dqkv.shape[1])]
    grads_kernel(
        plan,
        True,
        index,
        xhat,
        dqkv,
        hidden_sum,
        seed_sum,
        branch,
        sent,
        kept_low,
        kept_high,
        whole,
        extra,
    )


def own_rows_kernel(
    place,
    normed_own,
    n1,
    n2,
    n3,
    outside_own,
    o1,
    o3,
    tokens,
    middle_back,
    middle,
    gain,
    bias,
    result,
    input_grad,
):
    normed_back, outside = normed_own[...], outside_own[...]
    slot = normed_back.shape[0]
    for ref in (n1, n2, n3):
        normed_back = normed_back + ref[:slot].astype(jnp.float32)
    for ref in (o1, n2.at[slot:], o3):
        outside = outside + ref[...].astype(jnp.float32)
    xhat, rstd = normalized(tokens[...].astype(jnp.float32))
    grad = middle_back[...] + norm_back(normed_back * gain[...], xhat, rstd)
    input_grad[...] = grad.astype(jnp.bfloat16)
    result[...] = (middle[...] + (outside + bias[...])).astype(jnp.bfloat16)


def slots_returned(parts):
    return [passed_along(parts[by - 1], -by) for by in range(1, 4)]


def shards(
    tokens,
    query_weight,
    key_weight,
    value_weight,
    output_weight,
    up_weight,
    down_weight,
    query_bias,
    value_bias,
    output_bias,
    up_bias,
    down_bias,
    first_gain,
    first_shift,
    second_gain,
    second_shift,
    cotangent,
):
    bf16, f32 = jnp.bfloat16, jnp.float32
    uly, blk = lax.axis_index("uly"), lax.axis_index("blk")
    groups = lax.axis_size("uly")
    owners = lax.axis_size(CUBE)
    part = tokens.shape[0]
    rows = groups * part
    depth, width = query_weight.shape
    units = up_weight.shape[1]
    model = depth * owners
    place = jnp.stack([blk, uly]).astype(jnp.int32)

    qkv_own = jnp.concatenate(
        [key_weight, value_weight[:, 128:], value_weight[:, :128], query_weight], axis=1
    )
    vectors = [
        query_bias,
        value_bias,
        output_bias,
        down_bias,
        first_gain,
        first_shift,
        second_gain,
        second_shift,
    ]
    up_rows = up_bias.shape[0] // depth
    named = len(vectors) + up_rows
    wide = 3 * width
    vector_rows = jnp.concatenate(
        [vector.reshape(1, depth) for vector in vectors] + [up_bias.reshape(up_rows, depth)]
    )
    vector_rows = jnp.pad(vector_rows, ((0, VEC_ROWS - named), (0, wide - depth)))
    chunk = depth // groups
    output_own = output_weight.T
    output_rows = jnp.concatenate(
        [output_own[at * chunk : (at + 1) * chunk] for at in range(groups)], axis=1
    )
    spare = -(part + chunk) % 16
    token_sent = jnp.concatenate([tokens, jnp.pad(output_rows, ((0, spare), (0, 0)))], axis=0)
    token_slots = [tokens, passed_along(token_sent, 1), None, None]
    qkv_sent = jnp.concatenate([qkv_own, vector_rows], axis=0)
    if paired():
        qkv_sent = after(qkv_sent, token_slots[1])
        token_later = after(token_sent, token_slots[1])
        token_slots[3] = passed_along(token_later, 3)
        token_slots[2] = passed_along(token_later, 2)
        qkv_first = after(cube_swapped(qkv_sent, 4, 2), token_slots[3])
        qkv_second = cube_swapped(jnp.stack([qkv_sent, qkv_first]), 2, 4)
        qkv_second = after(qkv_second, token_slots[2])
        qkv_other = cube_swapped(
            jnp.concatenate([qkv_sent[None], qkv_first[None], qkv_second]), 1, 1
        )
    else:
        token_slots = [tokens] + slots_of(token_sent)[1:]
        whole = lax.all_gather(qkv_sent, CUBE, axis=0, tiled=False)
        qkv_whole, vector_whole = whole[:, :depth], whole[:, depth:]

    inner = groups * width
    rest_cuts = [
        (0, depth, 0, inner),
        (0, depth, inner, units),
        (0, depth, inner + units, units),
    ]
    cotangent_later = after(cotangent, *token_slots[1:])
    cotangent_slots = [cotangent] + [passed_along(cotangent_later, by) for by in range(1, groups)]
    output_slots = [output_own] + [
        jnp.concatenate(
            [item[part : part + chunk, at * width : (at + 1) * width] for at in range(groups)], axis=0
        )
        for item in token_slots[1:]
    ]
    rest_own = jnp.concatenate(output_slots + [up_weight, down_weight.T], axis=1)
    if paired():
        rest_own = after(rest_own, qkv_second)
        rest_first = cube_swapped(rest_own, 4, 2)

    project_outs = [((rows, width), bf16), ((rows, 2 * width), bf16), ((rows, model), bf16)]
    if paired():
        qkv_whole, named, up_bias_own, query, kv_own, xhat1_low = on_core(
            entry_kernel,
            jnp.stack([cube_index(), uly]).astype(jnp.int32),
            [qkv_sent, qkv_first, qkv_second, qkv_other] + token_slots,
            [((model, wide), bf16), ((VEC_ROWS, model), f32), ((1, units), f32)] + project_outs,
        )
    else:
        qkv_whole = qkv_whole.reshape(model, wide)
        vector_whole = vector_whole[:, :named, :depth].astype(f32)
        up_bias_whole = vector_whole[:, len(vectors) :].reshape(-1)
        named = vector_whole.transpose(1, 0, 2).reshape(named, model)
        query_bias_own = lax.dynamic_slice_in_dim(named[0], uly * width, width)
        value_bias_own = lax.dynamic_slice_in_dim(named[1], uly * width, width)
        up_bias_own = lax.dynamic_slice_in_dim(up_bias_whole, uly * units, units)
        qkv_bias = jnp.concatenate(
            [jnp.zeros((width,), f32), value_bias_own[128:], value_bias_own[:128], query_bias_own]
        )
        up_bias_own = up_bias_own[None]
        query, kv_own, xhat1_low = on_core(
            project_kernel,
            place,
            token_slots + [qkv_whole, named[4:6], qkv_bias[None]],
            project_outs,
        )
    output_bias_all, down_bias_all = named[2], named[3]
    gain1, gain2, shift2 = named[4], named[6], named[7]
    kv_y = blk_swapped(kv_own, 2)
    kv_core = blk_swapped(kv_own, 1)
    stats = ((8, rows), f32)
    turned = ((width, rows), f32)
    if paired():
        rest_second = cube_swapped(after(jnp.stack([rest_own, rest_first]), kv_own), 2, 4)
    top, total, mixed_t = on_core(
        forward_near_kernel, place, (query, kv_own, kv_core), (stats, stats, turned)
    )
    kv_both = blk_swapped(after(kv_y, top, *cotangent_slots[1:]), 1)
    if paired():
        rest_second = after(rest_second, kv_both)
        rest_held = jnp.concatenate([rest_own[None], rest_first[None], rest_second])
        rest_other = cube_swapped(rest_held, 1, 1)
        kv_both = after(kv_both, rest_held)
    mixed_low, mixed_t, lse = on_core(
        forward_far_kernel,
        place,
        (query, kv_y, kv_both, top, total, mixed_t),
        (((width, rows), bf16), turned, stats),
        (stats, stats),
    )
    mixed_slots = slots_of(mixed_low)
    if paired():
        rest_other = after(rest_other, mixed_low)
        output_t, up_whole, down_t = cube_placed(
            rest_cuts, (rest_own, rest_first, rest_second, rest_other)
        )
    else:
        whole = lax.all_gather(rest_own, CUBE, axis=0, tiled=False)
        output_t, up_whole, down_t = [whole[:, :, c : c + n] for _, _, c, n in rest_cuts]
    output_t = output_t.reshape(model, inner)
    up_whole = up_whole.reshape(model, units)
    down_t = down_t.reshape(model, units)

    slab = ((part, model), f32)
    slabs = [((part, model), bf16)] * (groups - 1)
    wide_low = ((rows, model), bf16)
    units_low = ((rows, units), bf16)
    middle, xhat2_low, mixed_own, active, hidden_back, second_own, *second_parts = on_core(
        middle_kernel,
        place,
        mixed_slots
        + token_slots
        + cotangent_slots
        + [output_t, up_whole, down_t, jnp.stack([output_bias_all, gain2, shift2]), up_bias_own],
        [slab, wide_low, ((inner, part), bf16), units_low, units_low, slab] + slabs,
    )
    second_returned = slots_returned(second_parts)
    hidden_sum, seed_sum, outside_own, *outside_parts = on_core(
        outside_kernel,
        place,
        [active, down_t, hidden_back] + cotangent_slots,
        [((1, units), f32), ((1, model), f32), slab] + slabs,
    )

    middle_back, branch_back, *mixed_back_t = on_core(
        branch_kernel,
        place,
        [second_own] + second_returned + [middle, cotangent, gain2[None], output_t],
        [slab, ((part, model), bf16)] + [((width, part), bf16)] * groups,
    )
    grad_slots = [mixed_back_t[0]] + [
        passed_along(mixed_back_t[by], -by) for by in range(groups - 1, 0, -1)
    ]
    wide_pairs = [
        ([xhat2_low], False, hidden_back, 0),
        (cotangent_slots, False, active, units),
        ([branch_back], True, mixed_own, 2 * units),
    ]
    wide_columns = 2 * units + inner
    if paired():
        wide_sent, wide_low_part, wide_high_part = grads_sent(wide_pairs, wide_columns, depth)
        wide_got = cube_swapped(wide_sent, 1, 1)
        grad_slots[1] = after(grad_slots[1], wide_sent)
    outside_returned = [
        passed_along(after(outside_parts[by - 1], *mixed_back_t), -by) for by in (1, 3)
    ]
    grad_slots[1] = after(grad_slots[1], *outside_returned)
    sides = [query] + grad_slots + [mixed_t, lse]
    pair = ((rows, 2 * width), bf16)
    dkv_both, query_grad_t = on_core(
        backward_both_kernel, place, sides + [kv_both], (pair, turned)
    )
    if paired():
        wide_got = after(wide_got, dkv_both)
        wide_next = (wide_high_part + wide_got[2:].astype(f32)).astype(bf16)
        wide_more = cube_swapped(wide_next, 4, 2)
    dkv_y, query_grad_t = on_core(
        backward_y_kernel,
        place,
        sides + [kv_y, blk_swapped(dkv_both, 1), query_grad_t],
        (pair, turned),
        [((rows, 2 * width), f32)],
    )
    dkv_from_y = blk_swapped(dkv_y, 2)
    kv_last = after(kv_core, wide_next) if paired() else kv_core
    dkv_own, dkv_core, query_grad = on_core(
        backward_near_kernel,
        place,
        sides + [kv_own, kv_last, query_grad_t],
        (pair, pair, ((rows, width), bf16)),
        (turned,),
    )
    dkv_core = blk_swapped(dkv_core, 1)
    columns = -(-wide // 128) * 128
    back_operands = [dkv_own, dkv_core, dkv_from_y, query_grad, qkv_whole, outside_parts[1]]
    back_outs = [slab, slabs[0], ((2 * part, model), bf16), slabs[0]]
    sums = (hidden_sum, seed_sum, branch_back)
    dqkv_kind = ((rows, columns), bf16)
    if paired():
        kinds = [((4, depth + VEC_ROWS, columns), bf16)]
        kinds += [((2, depth + VEC_ROWS, columns), f32)] * 2
        normed_own, *normed_parts, near_sent, near_low, near_high = on_core(
            last_kernel,
            cube_index().astype(jnp.int32).reshape(1),
            back_operands + [xhat1_low] + list(sums),
            back_outs + kinds,
            [dqkv_kind, ((model, columns), f32), ((8, VEC_ROWS, columns), f32)],
        )
    else:
        dqkv, normed_own, *normed_parts = on_core(
            gather_back_kernel, place, back_operands, [dqkv_kind] + back_outs
        )
    normed_returned = slots_returned(normed_parts)

    if paired():
        near_got = cube_swapped(near_sent, 1, 1)
        near_next = (near_high + near_got[2:].astype(f32)).astype(bf16)
        wide_more = after(wide_more, near_next)
        wide_last = wide_low_part[1] + wide_got[1].astype(f32) + wide_more[1].astype(f32)
        wide_end = cube_swapped(wide_last.astype(bf16), 2, 4)
        near_more = cube_swapped(near_next, 4, 2)
        near_last = near_low[1] + near_got[1].astype(f32) + near_more[1].astype(f32)
        near_end = cube_swapped(near_last.astype(bf16), 2, 4)
        near_total = near_low[0] + near_got[0].astype(f32) + near_more[0].astype(f32)
        near_total = near_total + near_end.astype(f32)
        wide_total = wide_low_part[0] + wide_got[0].astype(f32) + wide_more[0].astype(f32)
        wide_total = wide_total + wide_end.astype(f32)
    else:
        near_total = grads_scattered([([xhat1_low], False, dqkv, 0)], columns, owners, sums)
        wide_total = grads_scattered(wide_pairs, wide_columns, owners, ())

    half = units // 2
    qkv_total, qkv_sums = near_total[:depth, :wide], near_total[depth, :wide]
    hidden_sums = near_total[depth + 1 : depth + 3, :half].reshape(-1)
    branch_sums, seed_sums = near_total[depth + 8, :depth], near_total[depth + 9, :depth]
    up_total, down_total = wide_total[:, :units], wide_total[:, units : 2 * units].T
    own_gain1, own_shift1 = first_gain.astype(f32), first_shift.astype(f32)
    own_gain2, own_shift2 = second_gain.astype(f32), second_shift.astype(f32)
    qkv_weight_grad = own_gain1[:, None] * qkv_total + own_shift1[:, None] * qkv_sums[None]
    up_weight_grad = own_gain2[:, None] * up_total + own_shift2[:, None] * hidden_sums[None]
    qkv_wide, up_wide = qkv_own.astype(f32), up_weight.astype(f32)
    terms = jnp.concatenate(
        [
            jnp.sum(qkv_wide * qkv_total, axis=1),
            jnp.sum(qkv_wide * qkv_sums[None], axis=1),
            jnp.sum(up_wide * up_total, axis=1),
            jnp.sum(up_wide * hidden_sums[None], axis=1),
            branch_sums,
            qkv_sums[2 * width :],
            qkv_sums[width + 64 : 2 * width],
            qkv_sums[width : width + 64],
            hidden_sums,
        ]
    )
    term_rows = -(-terms.shape[0] // (8 * width)) * 8
    terms = jnp.pad(terms, (0, term_rows * width - terms.shape[0])).reshape(term_rows, width)
    blocks = [wide_total[:, 2 * units + by * width :][:, :width] for by in range(groups)]
    final_sent = [jnp.concatenate([block, terms], axis=0).astype(bf16) for block in blocks[1:]]
    returned = [item.astype(f32) for item in slots_returned(final_sent)]
    output_total = blocks[0]
    for item in returned:
        output_total = output_total + item[:depth]
    all_terms = jnp.stack([terms.reshape(-1)] + [item[depth:].reshape(-1) for item in returned[::-1]])
    share = depth // groups
    added = jnp.sum(all_terms[:, : 5 * depth], axis=0).reshape(5, depth)
    added = lax.dynamic_slice_in_dim(added, uly * share, share, axis=1)
    rank = cube_index() * groups + uly

    def owned(start, length, count):
        at = rank * count
        source = (uly - at // length) % groups
        return lax.dynamic_slice(all_terms, (source, start + at % length), (1, count))[0]

    query_bias_grad = owned(5 * depth, width, share)
    value_bias_grad = owned(5 * depth + width, width, share)
    up_bias_grad = owned(5 * depth + 2 * width, units, up_bias.shape[0] // groups)
    down_bias_grad = lax.dynamic_slice_in_dim(seed_sums, uly * share, share)
    value_weight_grad = jnp.concatenate(
        [qkv_weight_grad[:, width + 64 : 2 * width], qkv_weight_grad[:, width : width + 64]], axis=1
    )

    result, input_grad = on_core(
        own_rows_kernel,
        place,
        [normed_own]
        + [after(item, *final_sent) for item in normed_returned]
        + [outside_own]
        + outside_returned
        + [tokens, middle_back, middle, gain1[None], down_bias_all[None]],
        [((part, model), bf16)] * 2,
    )
    return (
        result,
        input_grad,
        qkv_weight_grad[:, 2 * width :],
        qkv_weight_grad[:, :width],
        value_weight_grad,
        output_total.T,
        up_weight_grad,
        down_total,
        query_bias_grad,
        value_bias_grad,
        added[4],
        up_bias_grad,
        down_bias_grad,
        added[0],
        added[1],
        added[2],
        added[3],
    )


def solution(mesh):
    rows = P(("fsdp", "blk", "uly"), None)
    tall, flat = P(("fsdp", "blk"), "uly"), P("uly", ("fsdp", "blk"))
    vector, vector_out = P(("fsdp", "blk")), P(("fsdp", "blk", "uly"))
    return jax.shard_map(
        shards,
        mesh=mesh,
        in_specs=(rows, tall, tall, tall, flat, tall, flat) + (vector,) * 9 + (rows,),
        out_specs=(rows, rows, tall, tall, tall, flat, tall, flat) + (vector_out,) * 9,
        check_vma=False,
    )
```

```python
import jax
import jax.numpy as jnp
from jax import lax
from jax.experimental import pallas as pl
from jax.experimental.pallas import tpu as pltpu
from jax.sharding import PartitionSpec as P

HEAD_DIM = 64
CUBE = ("fsdp", "blk")
VEC_ROWS = 16
VMEM_LIMIT = 56 * 1024 * 1024
KERNEL_COST = 60_000_000_000

KEY_GROUP, KEY_HALF = (0, 0, 1), (0, 1, 0)
VALUE_GROUP, VALUE_HALF = (2, 2, 1), (0, 1, 1)


def dot_plain(left, right):
    return jnp.dot(left, right, preferred_element_type=jnp.float32)


def dot_rows(left, right):
    return lax.dot_general(
        left, right, (((0,), (0,)), ((), ())), preferred_element_type=jnp.float32
    )


def dot_cols(left, right):
    return lax.dot_general(
        left, right, (((1,), (1,)), ((), ())), preferred_element_type=jnp.float32
    )


def passed_along(array, by):
    peers = lax.axis_size("uly")
    return lax.ppermute(array, "uly", [(i, (i + by) % peers) for i in range(peers)])


def slots_of(array):
    return [array] + [passed_along(array, by) for by in range(1, lax.axis_size("uly"))]


def blk_swapped(array, flip):
    peers = lax.axis_size("blk")
    return lax.ppermute(array, "blk", [(i, i ^ flip) for i in range(peers)])


def cube_swapped(array, even, odd):
    peers = lax.axis_size(CUBE)
    pairs = [(i, i ^ (odd if i & 1 else even)) for i in range(peers)]
    return lax.ppermute(array, CUBE, pairs)


def cube_index():
    return lax.axis_index("fsdp") * lax.axis_size("blk") + lax.axis_index("blk")


def cube_pieces(me, own, first, second, other):
    odd = me & 1
    near, far = jnp.where(odd == 1, 2, 4), jnp.where(odd == 1, 4, 2)
    return [
        (own, 0),
        (first, near),
        (second.at[0], far),
        (second.at[1], 6),
        (other.at[0], 1),
        (other.at[1], far ^ 1),
        (other.at[2], near ^ 1),
        (other.at[3], 7),
    ]


def place_kernel(cuts, index_ref, own, first, second, other, *outs):
    me = index_ref[0]
    for piece, flip in cube_pieces(me, own, first, second, other):
        for out, (row, rows, column, columns) in zip(outs, cuts):
            out[me ^ flip] = piece[row : row + rows, column : column + columns]


def paired():
    return lax.axis_size("fsdp") == 2 and lax.axis_size("blk") == 4


def after(array, *others):
    return lax.optimization_barrier((array,) + others)[0]


def cube_placed(cuts, pieces):
    index = cube_index().astype(jnp.int32).reshape(1)
    outs = [((8, rows, columns), pieces[0].dtype) for _, rows, _, columns in cuts]
    return on_core(lambda *refs: place_kernel(cuts, *refs), index, pieces, outs)


def cube_flips(me):
    odd = me & 1
    return jnp.where(odd == 1, 2, 4), jnp.where(odd == 1, 4, 2)


def grads_kernel(pairs, spread, index, *refs):
    ins, (sent, kept_low, kept_high), (whole, extra) = refs[:-5], refs[-5:-2], refs[-2:]
    at = 0
    for count, flipped, column, columns in pairs:
        left, right = stacked_slots(ins[at : at + count]), ins[at + count][...]
        at += count + 1
        whole[:, column : column + columns] = dot_plain(left.T, right.T if flipped else right)
    rows = sent.shape[1]
    model, wide = whole.shape
    depth = model // 8
    if spread:
        hidden_sum, seed_sum, branch = ins[at], ins[at + 1], ins[at + 2]
        half = hidden_sum.shape[1] // 2
        right_sum = jnp.sum(right.astype(jnp.float32), axis=0, keepdims=True)
        branch_sum = jnp.sum(branch[...].astype(jnp.float32), axis=0, keepdims=True)
        whole_rows = jnp.concatenate([right_sum, jnp.zeros((7, wide), jnp.float32)], axis=0)
        part_rows = jnp.concatenate(
            [branch_sum, seed_sum[...], jnp.zeros((6, model), jnp.float32)], axis=0
        )
        for block in range(8):
            turned = part_rows if block == 0 else pltpu.roll(part_rows, model - depth * block, 1)
            extra[block, 0:8] = whole_rows
            extra[block, 1:2, 0:half] = hidden_sum[:, :half]
            extra[block, 2:3, 0:half] = hidden_sum[:, half:]
            extra[block, 8:16] = turned[:, :wide]
    me = index[0]
    near, far = cube_flips(me)
    for slot, flip in enumerate((0, near, far, 6)):
        block = me ^ flip ^ 1
        sent[slot, 0:depth] = whole[pl.ds(pl.multiple_of(block * depth, 8), depth)].astype(sent.dtype)
        if spread:
            sent[slot, depth:rows] = extra[block].astype(sent.dtype)
    for slot, flip in enumerate((0, far, near, 6)):
        block = me ^ flip
        kept = (kept_low if slot < 2 else kept_high).at[slot % 2]
        kept[0:depth] = whole[pl.ds(pl.multiple_of(block * depth, 8), depth)]
        if spread:
            kept[depth:rows] = extra[block]


def grads_sent(pairs, columns, depth):
    plan = [
        (len(left), flipped, column, right.shape[0 if flipped else 1])
        for left, flipped, right, column in pairs
    ]
    operands = [item for left, _, right, _ in pairs for item in [*left, right]]
    index = cube_index().astype(jnp.int32).reshape(1)
    return on_core(
        lambda *refs: grads_kernel(plan, False, *refs),
        index,
        operands,
        [((4, depth, columns), jnp.bfloat16)] + [((2, depth, columns), jnp.float32)] * 2,
        [((8 * depth, columns), jnp.float32), ((8, VEC_ROWS, columns), jnp.float32)],
    )


def grads_scattered(pairs, columns, owners, sums):
    blocks = []
    for left, flipped, right, _ in pairs:
        right = right.T if flipped else right
        blocks.append(dot_rows(stacked_slots(left), right))
    model = blocks[0].shape[0]
    depth = model // owners
    blocks = jnp.concatenate(blocks, axis=1).reshape(owners, depth, columns)
    if sums:
        hidden_sum, seed_sum, branch = sums
        half = hidden_sum.shape[1] // 2
        branch_sum = jnp.sum(branch.astype(jnp.float32), axis=0)
        extra = jnp.zeros((owners, VEC_ROWS, columns), jnp.float32)
        extra = extra.at[:, 0].set(jnp.sum(pairs[0][2].astype(jnp.float32), axis=0)[None])
        extra = extra.at[:, 1, :half].set(hidden_sum[:, :half])
        extra = extra.at[:, 2, :half].set(hidden_sum[:, half:])
        extra = extra.at[:, 8, :depth].set(branch_sum.reshape(owners, depth))
        extra = extra.at[:, 9, :depth].set(seed_sum.reshape(owners, depth))
        blocks = jnp.concatenate([blocks, extra], axis=1)
    return lax.psum_scatter(blocks, CUBE, scatter_dimension=0, tiled=False)


def half_padded(part, half):
    zero = jnp.zeros_like(part)
    return jnp.concatenate([part, zero] if half == 0 else [zero, part], axis=0)


def heads_across(array, halves):
    turned = array.T
    return [
        half_padded(turned[h * HEAD_DIM : (h + 1) * HEAD_DIM], halves[h])
        for h in range(len(halves))
    ]


def group_of(ref, group):
    return ref[:, group * 128 : (group + 1) * 128]


def slot_places(index, uly, slot_rows):
    return ((uly - index // slot_rows) & 3) * slot_rows + index % slot_rows


def causal(rows, uly):
    keys = lax.broadcasted_iota(jnp.int32, (rows, rows), 0)
    queries = lax.broadcasted_iota(jnp.int32, (rows, rows), 1)
    slot_rows = rows // 4
    return slot_places(keys, uly, slot_rows) <= slot_places(queries, uly, slot_rows)


def forward_block(query_t, kv_ref, top, total, mixed, allowed):
    turned = kv_ref[...].T
    for h in range(3):
        scores = dot_plain(group_of(kv_ref, KEY_GROUP[h]), query_t[h])
        if allowed is not None:
            scores = jnp.where(allowed, scores, -1e30)
        block_top = jnp.max(scores, axis=0, keepdims=True)
        low = VALUE_GROUP[h] * 128 + VALUE_HALF[h] * HEAD_DIM
        value_t = turned[low : low + HEAD_DIM]
        own = pl.ds(h * HEAD_DIM, HEAD_DIM)
        if allowed is not None:
            weights = jnp.exp(scores - block_top)
            top[h : h + 1] = block_top
            total[h : h + 1] = jnp.sum(weights, axis=0, keepdims=True)
            mixed[own] = dot_plain(value_t, weights.astype(jnp.bfloat16))
        else:
            old_top = top[h : h + 1]
            new_top = jnp.maximum(old_top, block_top)
            fade = jnp.exp(old_top - new_top)
            weights = jnp.exp(scores - new_top)
            top[h : h + 1] = new_top
            total[h : h + 1] = total[h : h + 1] * fade + jnp.sum(weights, axis=0, keepdims=True)
            mixed[own] = mixed[own] * fade + dot_plain(value_t, weights.astype(jnp.bfloat16))


def forward_near_kernel(place, query, kv_own, kv_core, top, total, mixed):
    blk, uly = place[0], place[1]
    query_t = heads_across(query[...], KEY_HALF)
    top[...] = jnp.zeros_like(top)
    total[...] = jnp.ones_like(total)
    forward_block(query_t, kv_own, top, total, mixed, causal(query.shape[0], uly))

    @pl.when((blk & 1) == 1)
    def _():
        forward_block(query_t, kv_core, top, total, mixed, None)


def forward_far_kernel(
    place, query, kv_y, kv_both, top_in, total_in, mixed_in, out, mixed, lse, top, total
):
    blk = place[0]
    top[...] = top_in[...]
    total[...] = total_in[...]
    mixed[...] = mixed_in[...]

    @pl.when((blk & 2) == 2)
    def _():
        query_t = heads_across(query[...], KEY_HALF)
        forward_block(query_t, kv_y, top, total, mixed, None)
        forward_block(query_t, kv_both, top, total, mixed, None)

    for h in range(3):
        own = pl.ds(h * HEAD_DIM, HEAD_DIM)
        mixed[own] = mixed[own] / total[h : h + 1]
    lse[...] = top[...] + jnp.log(total[...])
    out[...] = mixed[...].astype(jnp.bfloat16)


def backward_block(sides, kv_ref, dkv_ref, query_grad_t, allowed):
    query_t, grad_t, query_m, grad_m, delta, lse = sides
    turned = kv_ref[...].T
    columns = [None, None, None]

    def add(group, term):
        columns[group] = term if columns[group] is None else columns[group] + term

    for h in range(3):
        scores = dot_plain(group_of(kv_ref, KEY_GROUP[h]), query_t[h])
        probs = jnp.exp(scores - lse[h : h + 1])
        if allowed is not None:
            probs = jnp.where(allowed, probs, 0.0)
        prob_grad = dot_plain(group_of(kv_ref, VALUE_GROUP[h]), grad_t[h])
        score_grad = (probs * (prob_grad - delta[h])).astype(jnp.bfloat16)
        add(VALUE_GROUP[h], dot_plain(probs.astype(jnp.bfloat16), grad_m[h]))
        add(KEY_GROUP[h], dot_plain(score_grad, query_m[h]))
        low = KEY_GROUP[h] * 128 + KEY_HALF[h] * HEAD_DIM
        own = pl.ds(h * HEAD_DIM, HEAD_DIM)
        query_grad_t[own] += dot_plain(turned[low : low + HEAD_DIM], score_grad)
    for group in range(3):
        dkv_ref[:, group * 128 : (group + 1) * 128] = columns[group].astype(dkv_ref.dtype)


def backward_sides(query, grads, mixed, lse):
    query_t = heads_across(query[...], KEY_HALF)
    grad_all = jnp.concatenate([ref[...] for ref in grads], axis=1)
    grad_t = [
        half_padded(grad_all[h * HEAD_DIM : (h + 1) * HEAD_DIM], VALUE_HALF[h]) for h in range(3)
    ]
    product = grad_all.astype(jnp.float32) * mixed[...]
    delta = [
        jnp.sum(product[h * HEAD_DIM : (h + 1) * HEAD_DIM], axis=0, keepdims=True)
        for h in range(3)
    ]
    query_m = [item.T for item in query_t]
    grad_m = [item.T for item in grad_t]
    return query_t, grad_t, query_m, grad_m, delta, lse[...]


def backward_both_kernel(place, query, g0, g1, g2, g3, mixed, lse, kv_both, dkv_both, query_grad_t):
    query_grad_t[...] = jnp.zeros_like(query_grad_t)

    @pl.when((place[0] & 2) == 2)
    def _():
        sides = backward_sides(query, (g0, g1, g2, g3), mixed, lse)
        backward_block(sides, kv_both, dkv_both, query_grad_t, None)

    @pl.when((place[0] & 2) == 0)
    def _():
        dkv_both[...] = jnp.zeros_like(dkv_both)


def backward_y_kernel(
    place, query, g0, g1, g2, g3, mixed, lse, kv_y, dkv_core, grad_t_in, dkv_y, total, part
):
    total[...] = grad_t_in[...]

    @pl.when((place[0] & 2) == 2)
    def _():
        sides = backward_sides(query, (g0, g1, g2, g3), mixed, lse)
        backward_block(sides, kv_y, part, total, None)
        dkv_y[...] = (part[...] + dkv_core[...].astype(jnp.float32)).astype(dkv_y.dtype)

    @pl.when((place[0] & 2) == 0)
    def _():
        dkv_y[...] = jnp.zeros_like(dkv_y)


def backward_near_kernel(
    place,
    query,
    g0,
    g1,
    g2,
    g3,
    mixed,
    lse,
    kv_own,
    kv_core,
    grad_t_in,
    dkv_own,
    dkv_core,
    query_grad,
    total,
):
    blk, uly = place[0], place[1]
    total[...] = grad_t_in[...]
    sides = backward_sides(query, (g0, g1, g2, g3), mixed, lse)

    @pl.when((blk & 1) == 1)
    def _():
        backward_block(sides, kv_core, dkv_core, total, None)

    @pl.when((blk & 1) == 0)
    def _():
        dkv_core[...] = jnp.zeros_like(dkv_core)

    backward_block(sides, kv_own, dkv_own, total, causal(query.shape[0], uly))
    query_grad[...] = (total[...] * HEAD_DIM**-0.5).T.astype(jnp.bfloat16)


def on_core(kernel, place, operands, outs, scratch=()):
    vmem = pl.BlockSpec(memory_space=pltpu.VMEM)
    return pl.pallas_call(
        kernel,
        out_shape=[jax.ShapeDtypeStruct(shape, dtype) for shape, dtype in outs],
        in_specs=[pl.BlockSpec(memory_space=pltpu.SMEM)] + [vmem] * len(operands),
        out_specs=[vmem] * len(outs),
        scratch_shapes=[pltpu.VMEM(shape, dtype) for shape, dtype in scratch],
        compiler_params=pltpu.CompilerParams(vmem_limit_bytes=VMEM_LIMIT),
        cost_estimate=pl.CostEstimate(flops=KERNEL_COST, transcendentals=0, bytes_accessed=0),
    )(place, *operands)


def normalized(rows):
    centre = rows - jnp.mean(rows, axis=-1, keepdims=True)
    rstd = lax.rsqrt(jnp.mean(centre * centre, axis=-1, keepdims=True) + 1e-05)
    return centre * rstd, rstd


def norm_back(grad, xhat, rstd):
    return rstd * (
        grad
        - jnp.mean(grad, axis=-1, keepdims=True)
        - xhat * jnp.mean(grad * xhat, axis=-1, keepdims=True)
    )


def stacked_slots(refs):
    rows = refs[0].shape[0]
    return jnp.concatenate([ref[:rows] for ref in refs], axis=0)


def project(rows, weight, gain, shift, bias, query, kv, xhat_low):
    xhat, _ = normalized(rows.astype(jnp.float32))
    xhat_low[...] = xhat.astype(jnp.bfloat16)
    normed = (xhat * gain + shift).astype(jnp.bfloat16)
    qkv = dot_plain(normed, weight) + bias
    wide = kv.shape[1]
    kv[...] = qkv[:, :wide].astype(jnp.bfloat16)
    query[...] = qkv[:, wide:].astype(jnp.bfloat16) * jnp.asarray(HEAD_DIM**-0.5, jnp.bfloat16)


def project_kernel(place, t0, t1, t2, t3, weight, named, bias, query, kv, xhat_low):
    rows = stacked_slots((t0, t1, t2, t3))
    project(rows, weight[...], named[0:1], named[1:2], bias[...], query, kv, xhat_low)


def entry_kernel(
    index,
    own,
    first,
    second,
    other,
    t0,
    t1,
    t2,
    t3,
    weight,
    named_out,
    up_own,
    query,
    kv,
    xhat_low,
):
    me, uly = index[0], index[1]
    model, wide = weight.shape
    depth, width = model // 8, wide // 3
    rows = named_out.shape[0]
    lane = lax.broadcasted_iota(jnp.int32, (rows, model), 1)
    named = jnp.zeros((rows, model), jnp.float32)
    for piece, flip in cube_pieces(me, own, first, second, other):
        at = me ^ flip
        weight[pl.ds(pl.multiple_of(at * depth, 16), depth), :] = piece[:depth, :]
        vector = piece[depth : depth + rows, :128].astype(jnp.float32)
        vector = jnp.concatenate([vector, jnp.zeros((rows, model - 128), jnp.float32)], axis=1)
        named = named + pltpu.roll(jnp.where(lane < depth, vector, 0.0), at * depth, 1)
    named_out[...] = named
    turned = pltpu.roll(named, ((4 - uly) & 3) * width, 1)

    def moved(row, by, low, high):
        block = row // 8 * 8
        item = pltpu.roll(turned[block : block + 8], by, 1) if by else turned[block : block + 8]
        inside = (lane[:8] >= low) & (lane[:8] < high)
        return jnp.where(inside, item, 0.0)[row - block : row - block + 1]

    bias = moved(1, 64, width, width + 64) + moved(1, width + 64, width + 64, 2 * width)
    bias = bias + moved(0, 2 * width, 2 * width, 3 * width)
    up = jnp.zeros((1, model), jnp.float32)
    for row in range(4):
        up = up + moved(8 + row, depth * row, depth * row, depth * (row + 1))
        up = up + moved(8 + row, depth * (3 + row), depth * (4 + row), depth * (5 + row))
    up_own[...] = up
    rows = stacked_slots((t0, t1, t2, t3))
    project(rows, weight[...], named[4:5], named[5:6], bias[:, :wide], query, kv, xhat_low)


GELU_A, GELU_B = 0.7978845608028654, 0.044715


def middle_kernel(
    place,
    m0,
    m1,
    m2,
    m3,
    t0,
    t1,
    t2,
    t3,
    c0,
    c1,
    c2,
    c3,
    output_t,
    up,
    down_t,
    named,
    up_bias,
    middle_own,
    xhat_low,
    mixed_own,
    active_low,
    hidden_back_low,
    part_own,
    *parts,
):
    slot = t0.shape[0]
    mixed_t = jnp.concatenate(
        [m0[...]]
        + [
            jnp.concatenate([ref[:, (4 - by) * slot :], ref[:, : (4 - by) * slot]], axis=1)
            for by, ref in ((1, m1), (2, m2), (3, m3))
        ],
        axis=0,
    )
    mixed_own[...] = mixed_t[:, :slot]
    branch = dot_plain(output_t[...], mixed_t).T
    middle = stacked_slots((t0, t1, t2, t3)).astype(jnp.float32) + (branch + named[0:1])
    middle_own[...] = middle[:slot]
    xhat, _ = normalized(middle)
    xhat_low[...] = xhat.astype(jnp.bfloat16)
    second = (xhat * named[1:2] + named[2:3]).astype(jnp.bfloat16)
    hidden = dot_plain(second, up[...]) + up_bias[...]
    active_grad = dot_plain(stacked_slots((c0, c1, c2, c3)), down_t[...])
    square = hidden * hidden
    bent = jnp.tanh(GELU_A * hidden * (1.0 + GELU_B * square))
    active_low[...] = (0.5 * hidden * (1.0 + bent)).astype(jnp.bfloat16)
    slope = 0.5 * (1.0 + bent) + (0.5 * GELU_A) * hidden * (1.0 - bent * bent) * (
        1.0 + (3.0 * GELU_B) * square
    )
    hidden_back = (active_grad * slope).astype(jnp.bfloat16)
    hidden_back_low[...] = hidden_back
    second_back = dot_cols(hidden_back, up[...])
    part_own[...] = second_back[:slot]
    for by in range(1, 4):
        parts[by - 1][...] = second_back[by * slot : (by + 1) * slot].astype(jnp.bfloat16)


def outside_kernel(
    place, active, down_t, hidden_back, c0, c1, c2, c3, hidden_sum, seed_sum, part_own, *parts
):
    slot = part_own.shape[0]
    outside = dot_cols(active[...], down_t[...])
    part_own[...] = outside[:slot]
    for by in range(1, 4):
        parts[by - 1][...] = outside[by * slot : (by + 1) * slot].astype(jnp.bfloat16)
    hidden_sum[...] = jnp.sum(hidden_back[...].astype(jnp.float32), axis=0, keepdims=True)
    seed = stacked_slots((c0, c1, c2, c3)).astype(jnp.float32)
    seed_sum[...] = jnp.sum(seed, axis=0, keepdims=True)


def branch_kernel(
    place,
    part_own,
    r1,
    r2,
    r3,
    middle,
    seed,
    gain,
    output_t,
    middle_back,
    branch_back,
    *mixed_back_t,
):
    second_back = part_own[...]
    for ref in (r1, r2, r3):
        second_back = second_back + ref[...].astype(jnp.float32)
    xhat, rstd = normalized(middle[...])
    grad = seed[...].astype(jnp.float32) + norm_back(second_back * gain[...], xhat, rstd)
    middle_back[...] = grad
    low = grad.astype(jnp.bfloat16)
    branch_back[...] = low
    turned = dot_plain(low, output_t[...]).T.astype(jnp.bfloat16)
    width = mixed_back_t[0].shape[0]
    for by in range(4):
        mixed_back_t[by][...] = turned[by * width : (by + 1) * width]


def gather_back_kernel(
    place, own, core, far, query, weight, outside, dqkv, part_own, *parts
):
    wide = own.shape[1]
    width = query.shape[1]
    total = own[...].astype(jnp.float32) + core[...].astype(jnp.float32)
    kv_grad = (total + far[...].astype(jnp.float32)).astype(jnp.bfloat16)
    dqkv[:, :wide] = kv_grad
    dqkv[:, wide : wide + width] = query[...]
    spare = dqkv.shape[1] - wide - width
    dqkv[:, wide + width :] = jnp.zeros((query.shape[0], spare), jnp.bfloat16)
    normed_back = dot_cols(dqkv[:, : wide + width], weight[...])
    slot = part_own.shape[0]
    part_own[...] = normed_back[:slot]
    for by in range(1, 4):
        parts[by - 1][:slot] = normed_back[by * slot : (by + 1) * slot].astype(jnp.bfloat16)
    parts[1][slot:] = outside[...]


def last_kernel(index, *refs):
    ins, (xhat, hidden_sum, seed_sum, branch) = refs[:6], refs[6:10]
    part_own, p1, p2, p3, sent, kept_low, kept_high, dqkv, whole, extra = refs[10:]
    gather_back_kernel(index, *ins, dqkv, part_own, p1, p2, p3)
    plan = [(1, False, 0, dqkv.shape[1])]
    grads_kernel(
        plan,
        True,
        index,
        xhat,
        dqkv,
        hidden_sum,
        seed_sum,
        branch,
        sent,
        kept_low,
        kept_high,
        whole,
        extra,
    )


def own_rows_kernel(
    place,
    normed_own,
    n1,
    n2,
    n3,
    outside_own,
    o1,
    o3,
    tokens,
    middle_back,
    middle,
    gain,
    bias,
    result,
    input_grad,
):
    normed_back, outside = normed_own[...], outside_own[...]
    slot = normed_back.shape[0]
    for ref in (n1, n2, n3):
        normed_back = normed_back + ref[:slot].astype(jnp.float32)
    for ref in (o1, n2.at[slot:], o3):
        outside = outside + ref[...].astype(jnp.float32)
    xhat, rstd = normalized(tokens[...].astype(jnp.float32))
    grad = middle_back[...] + norm_back(normed_back * gain[...], xhat, rstd)
    input_grad[...] = grad.astype(jnp.bfloat16)
    result[...] = (middle[...] + (outside + bias[...])).astype(jnp.bfloat16)


def slots_returned(parts):
    return [passed_along(parts[by - 1], -by) for by in range(1, 4)]


def shards(
    tokens,
    query_weight,
    key_weight,
    value_weight,
    output_weight,
    up_weight,
    down_weight,
    query_bias,
    value_bias,
    output_bias,
    up_bias,
    down_bias,
    first_gain,
    first_shift,
    second_gain,
    second_shift,
    cotangent,
):
    bf16, f32 = jnp.bfloat16, jnp.float32
    uly, blk = lax.axis_index("uly"), lax.axis_index("blk")
    groups = lax.axis_size("uly")
    owners = lax.axis_size(CUBE)
    part = tokens.shape[0]
    rows = groups * part
    depth, width = query_weight.shape
    units = up_weight.shape[1]
    model = depth * owners
    place = jnp.stack([blk, uly]).astype(jnp.int32)

    qkv_own = jnp.concatenate(
        [key_weight, value_weight[:, 128:], value_weight[:, :128], query_weight], axis=1
    )
    vectors = [
        query_bias,
        value_bias,
        output_bias,
        down_bias,
        first_gain,
        first_shift,
        second_gain,
        second_shift,
    ]
    up_rows = up_bias.shape[0] // depth
    named = len(vectors) + up_rows
    wide = 3 * width
    vector_rows = jnp.concatenate(
        [vector.reshape(1, depth) for vector in vectors] + [up_bias.reshape(up_rows, depth)]
    )
    vector_rows = jnp.pad(vector_rows, ((0, VEC_ROWS - named), (0, wide - depth)))
    chunk = depth // groups
    output_own = output_weight.T
    output_rows = jnp.concatenate(
        [output_own[at * chunk : (at + 1) * chunk] for at in range(groups)], axis=1
    )
    spare = -(part + chunk) % 16
    token_sent = jnp.concatenate([tokens, jnp.pad(output_rows, ((0, spare), (0, 0)))], axis=0)
    token_slots = [tokens, passed_along(token_sent, 1), None, None]
    qkv_sent = jnp.concatenate([qkv_own, vector_rows], axis=0)
    if paired():
        qkv_sent = after(qkv_sent, token_slots[1])
        token_later = after(token_sent, token_slots[1])
        token_slots[3] = passed_along(token_later, 3)
        token_slots[2] = passed_along(token_later, 2)
        qkv_first = after(cube_swapped(qkv_sent, 4, 2), token_slots[3])
        qkv_second = cube_swapped(jnp.stack([qkv_sent, qkv_first]), 2, 4)
        qkv_second = after(qkv_second, token_slots[2])
        qkv_other = cube_swapped(
            jnp.concatenate([qkv_sent[None], qkv_first[None], qkv_second]), 1, 1
        )
    else:
        token_slots = [tokens] + slots_of(token_sent)[1:]
        whole = lax.all_gather(qkv_sent, CUBE, axis=0, tiled=False)
        qkv_whole, vector_whole = whole[:, :depth], whole[:, depth:]

    inner = groups * width
    rest_cuts = [
        (0, depth, 0, inner),
        (0, depth, inner, units),
        (0, depth, inner + units, units),
    ]
    cotangent_later = after(cotangent, *token_slots[1:])
    cotangent_slots = [cotangent] + [passed_along(cotangent_later, by) for by in range(1, groups)]
    output_slots = [output_own] + [
        jnp.concatenate(
            [item[part : part + chunk, at * width : (at + 1) * width] for at in range(groups)], axis=0
        )
        for item in token_slots[1:]
    ]
    rest_own = jnp.concatenate(output_slots + [up_weight, down_weight.T], axis=1)
    if paired():
        rest_own = after(rest_own, qkv_second)
        rest_first = cube_swapped(rest_own, 4, 2)

    project_outs = [((rows, width), bf16), ((rows, 2 * width), bf16), ((rows, model), bf16)]
    if paired():
        qkv_whole, named, up_bias_own, query, kv_own, xhat1_low = on_core(
            entry_kernel,
            jnp.stack([cube_index(), uly]).astype(jnp.int32),
            [qkv_sent, qkv_first, qkv_second, qkv_other] + token_slots,
            [((model, wide), bf16), ((VEC_ROWS, model), f32), ((1, units), f32)] + project_outs,
        )
    else:
        qkv_whole = qkv_whole.reshape(model, wide)
        vector_whole = vector_whole[:, :named, :depth].astype(f32)
        up_bias_whole = vector_whole[:, len(vectors) :].reshape(-1)
        named = vector_whole.transpose(1, 0, 2).reshape(named, model)
        query_bias_own = lax.dynamic_slice_in_dim(named[0], uly * width, width)
        value_bias_own = lax.dynamic_slice_in_dim(named[1], uly * width, width)
        up_bias_own = lax.dynamic_slice_in_dim(up_bias_whole, uly * units, units)
        qkv_bias = jnp.concatenate(
            [jnp.zeros((width,), f32), value_bias_own[128:], value_bias_own[:128], query_bias_own]
        )
        up_bias_own = up_bias_own[None]
        query, kv_own, xhat1_low = on_core(
            project_kernel,
            place,
            token_slots + [qkv_whole, named[4:6], qkv_bias[None]],
            project_outs,
        )
    output_bias_all, down_bias_all = named[2], named[3]
    gain1, gain2, shift2 = named[4], named[6], named[7]
    kv_y = blk_swapped(kv_own, 2)
    kv_core = blk_swapped(kv_own, 1)
    stats = ((8, rows), f32)
    turned = ((width, rows), f32)
    if paired():
        rest_second = cube_swapped(after(jnp.stack([rest_own, rest_first]), kv_own), 2, 4)
    top, total, mixed_t = on_core(
        forward_near_kernel, place, (query, kv_own, kv_core), (stats, stats, turned)
    )
    kv_both = blk_swapped(after(kv_y, top, *cotangent_slots[1:]), 1)
    if paired():
        rest_second = after(rest_second, kv_both)
        rest_held = jnp.concatenate([rest_own[None], rest_first[None], rest_second])
        rest_other = cube_swapped(rest_held, 1, 1)
        kv_both = after(kv_both, rest_held)
    mixed_low, mixed_t, lse = on_core(
        forward_far_kernel,
        place,
        (query, kv_y, kv_both, top, total, mixed_t),
        (((width, rows), bf16), turned, stats),
        (stats, stats),
    )
    mixed_slots = slots_of(mixed_low)
    if paired():
        rest_other = after(rest_other, mixed_low)
        output_t, up_whole, down_t = cube_placed(
            rest_cuts, (rest_own, rest_first, rest_second, rest_other)
        )
    else:
        whole = lax.all_gather(rest_own, CUBE, axis=0, tiled=False)
        output_t, up_whole, down_t = [whole[:, :, c : c + n] for _, _, c, n in rest_cuts]
    output_t = output_t.reshape(model, inner)
    up_whole = up_whole.reshape(model, units)
    down_t = down_t.reshape(model, units)

    slab = ((part, model), f32)
    slabs = [((part, model), bf16)] * (groups - 1)
    wide_low = ((rows, model), bf16)
    units_low = ((rows, units), bf16)
    middle, xhat2_low, mixed_own, active, hidden_back, second_own, *second_parts = on_core(
        middle_kernel,
        place,
        mixed_slots
        + token_slots
        + cotangent_slots
        + [output_t, up_whole, down_t, jnp.stack([output_bias_all, gain2, shift2]), up_bias_own],
        [slab, wide_low, ((inner, part), bf16), units_low, units_low, slab] + slabs,
    )
    second_returned = slots_returned(second_parts)
    hidden_sum, seed_sum, outside_own, *outside_parts = on_core(
        outside_kernel,
        place,
        [active, down_t, hidden_back] + cotangent_slots,
        [((1, units), f32), ((1, model), f32), slab] + slabs,
    )

    middle_back, branch_back, *mixed_back_t = on_core(
        branch_kernel,
        place,
        [second_own] + second_returned + [middle, cotangent, gain2[None], output_t],
        [slab, ((part, model), bf16)] + [((width, part), bf16)] * groups,
    )
    grad_slots = [mixed_back_t[0]] + [
        passed_along(mixed_back_t[by], -by) for by in range(groups - 1, 0, -1)
    ]
    wide_pairs = [
        ([xhat2_low], False, hidden_back, 0),
        (cotangent_slots, False, active, units),
        ([branch_back], True, mixed_own, 2 * units),
    ]
    wide_columns = 2 * units + inner
    if paired():
        wide_sent, wide_low_part, wide_high_part = grads_sent(wide_pairs, wide_columns, depth)
        wide_got = cube_swapped(wide_sent, 1, 1)
        grad_slots[1] = after(grad_slots[1], wide_sent)
    outside_returned = [
        passed_along(after(outside_parts[by - 1], *mixed_back_t), -by) for by in (1, 3)
    ]
    grad_slots[1] = after(grad_slots[1], *outside_returned)
    sides = [query] + grad_slots + [mixed_t, lse]
    pair = ((rows, 2 * width), bf16)
    dkv_both, query_grad_t = on_core(
        backward_both_kernel, place, sides + [kv_both], (pair, turned)
    )
    if paired():
        wide_got = after(wide_got, dkv_both)
        wide_next = (wide_high_part + wide_got[2:].astype(f32)).astype(bf16)
        wide_more = cube_swapped(wide_next, 4, 2)
    dkv_y, query_grad_t = on_core(
        backward_y_kernel,
        place,
        sides + [kv_y, blk_swapped(dkv_both, 1), query_grad_t],
        (pair, turned),
        [((rows, 2 * width), f32)],
    )
    dkv_from_y = blk_swapped(dkv_y, 2)
    kv_last = after(kv_core, wide_next) if paired() else kv_core
    dkv_own, dkv_core, query_grad = on_core(
        backward_near_kernel,
        place,
        sides + [kv_own, kv_last, query_grad_t],
        (pair, pair, ((rows, width), bf16)),
        (turned,),
    )
    dkv_core = blk_swapped(dkv_core, 1)
    columns = -(-wide // 128) * 128
    back_operands = [dkv_own, dkv_core, dkv_from_y, query_grad, qkv_whole, outside_parts[1]]
    back_outs = [slab, slabs[0], ((2 * part, model), bf16), slabs[0]]
    sums = (hidden_sum, seed_sum, branch_back)
    dqkv_kind = ((rows, columns), bf16)
    if paired():
        kinds = [((4, depth + VEC_ROWS, columns), bf16)]
        kinds += [((2, depth + VEC_ROWS, columns), f32)] * 2
        normed_own, *normed_parts, near_sent, near_low, near_high = on_core(
            last_kernel,
            cube_index().astype(jnp.int32).reshape(1),
            back_operands + [xhat1_low] + list(sums),
            back_outs + kinds,
            [dqkv_kind, ((model, columns), f32), ((8, VEC_ROWS, columns), f32)],
        )
    else:
        dqkv, normed_own, *normed_parts = on_core(
            gather_back_kernel, place, back_operands, [dqkv_kind] + back_outs
        )
    normed_returned = slots_returned(normed_parts)

    if paired():
        near_got = cube_swapped(near_sent, 1, 1)
        near_next = (near_high + near_got[2:].astype(f32)).astype(bf16)
        wide_more = after(wide_more, near_next)
        wide_last = wide_low_part[1] + wide_got[1].astype(f32) + wide_more[1].astype(f32)
        wide_end = cube_swapped(wide_last.astype(bf16), 2, 4)
        near_more = cube_swapped(near_next, 4, 2)
        near_last = near_low[1] + near_got[1].astype(f32) + near_more[1].astype(f32)
        near_end = cube_swapped(near_last.astype(bf16), 2, 4)
        near_total = near_low[0] + near_got[0].astype(f32) + near_more[0].astype(f32)
        near_total = near_total + near_end.astype(f32)
        wide_total = wide_low_part[0] + wide_got[0].astype(f32) + wide_more[0].astype(f32)
        wide_total = wide_total + wide_end.astype(f32)
    else:
        near_total = grads_scattered([([xhat1_low], False, dqkv, 0)], columns, owners, sums)
        wide_total = grads_scattered(wide_pairs, wide_columns, owners, ())

    half = units // 2
    qkv_total, qkv_sums = near_total[:depth, :wide], near_total[depth, :wide]
    hidden_sums = near_total[depth + 1 : depth + 3, :half].reshape(-1)
    branch_sums, seed_sums = near_total[depth + 8, :depth], near_total[depth + 9, :depth]
    up_total, down_total = wide_total[:, :units], wide_total[:, units : 2 * units].T
    own_gain1, own_shift1 = first_gain.astype(f32), first_shift.astype(f32)
    own_gain2, own_shift2 = second_gain.astype(f32), second_shift.astype(f32)
    qkv_weight_grad = own_gain1[:, None] * qkv_total + own_shift1[:, None] * qkv_sums[None]
    up_weight_grad = own_gain2[:, None] * up_total + own_shift2[:, None] * hidden_sums[None]
    qkv_wide, up_wide = qkv_own.astype(f32), up_weight.astype(f32)
    terms = jnp.concatenate(
        [
            jnp.sum(qkv_wide * qkv_total, axis=1),
            jnp.sum(qkv_wide * qkv_sums[None], axis=1),
            jnp.sum(up_wide * up_total, axis=1),
            jnp.sum(up_wide * hidden_sums[None], axis=1),
            branch_sums,
            qkv_sums[2 * width :],
            qkv_sums[width + 64 : 2 * width],
            qkv_sums[width : width + 64],
            hidden_sums,
        ]
    )
    term_rows = -(-terms.shape[0] // (8 * width)) * 8
    terms = jnp.pad(terms, (0, term_rows * width - terms.shape[0])).reshape(term_rows, width)
    blocks = [wide_total[:, 2 * units + by * width :][:, :width] for by in range(groups)]
    final_sent = [jnp.concatenate([block, terms], axis=0).astype(bf16) for block in blocks[1:]]
    returned = [item.astype(f32) for item in slots_returned(final_sent)]
    output_total = blocks[0]
    for item in returned:
        output_total = output_total + item[:depth]
    all_terms = jnp.stack([terms.reshape(-1)] + [item[depth:].reshape(-1) for item in returned[::-1]])
    share = depth // groups
    added = jnp.sum(all_terms[:, : 5 * depth], axis=0).reshape(5, depth)
    added = lax.dynamic_slice_in_dim(added, uly * share, share, axis=1)
    rank = cube_index() * groups + uly

    def owned(start, length, count):
        at = rank * count
        source = (uly - at // length) % groups
        return lax.dynamic_slice(all_terms, (source, start + at % length), (1, count))[0]

    query_bias_grad = owned(5 * depth, width, share)
    value_bias_grad = owned(5 * depth + width, width, share)
    up_bias_grad = owned(5 * depth + 2 * width, units, up_bias.shape[0] // groups)
    down_bias_grad = lax.dynamic_slice_in_dim(seed_sums, uly * share, share)
    value_weight_grad = jnp.concatenate(
        [qkv_weight_grad[:, width + 64 : 2 * width], qkv_weight_grad[:, width : width + 64]], axis=1
    )

    result, input_grad = on_core(
        own_rows_kernel,
        place,
        [normed_own]
        + [after(item, *final_sent) for item in normed_returned]
        + [outside_own]
        + outside_returned
        + [tokens, middle_back, middle, gain1[None], down_bias_all[None]],
        [((part, model), bf16)] * 2,
    )
    return (
        result,
        input_grad,
        qkv_weight_grad[:, 2 * width :],
        qkv_weight_grad[:, :width],
        value_weight_grad,
        output_total.T,
        up_weight_grad,
        down_total,
        query_bias_grad,
        value_bias_grad,
        added[4],
        up_bias_grad,
        down_bias_grad,
        added[0],
        added[1],
        added[2],
        added[3],
    )


def solution(mesh):
    rows = P(("fsdp", "blk", "uly"), None)
    tall, flat = P(("fsdp", "blk"), "uly"), P("uly", ("fsdp", "blk"))
    vector, vector_out = P(("fsdp", "blk")), P(("fsdp", "blk", "uly"))
    return jax.shard_map(
        shards,
        mesh=mesh,
        in_specs=(rows, tall, tall, tall, flat, tall, flat) + (vector,) * 9 + (rows,),
        out_specs=(rows, rows, tall, tall, tall, flat, tall, flat) + (vector_out,) * 9,
        check_vma=False,
    )
```
